32 devices in a mesh: gx: 4 (over z), gy: 8 (over y, x, core).
Axes of the slice: x: 2, y: 2, z: 4, core: 2. Of those that a mesh axis runs over, the one named last changes fastest.
Arguments:
- positions: bfloat16 [32, 64, 3, 128], P('gx', 'gy'), may hold values from 0 to 1
- features: bfloat16 [32, 64, 256, 128], P('gx', 'gy'), may hold values from -6 to 6
- lever: float32 [32, 64, 3, 128], P('gx', 'gy'), may hold values from -4 to 4
- partner: int32 [32, 64, 6], P('gx', 'gy'), may hold values from 0 to 8, as said below
- body_slot: int32 [32, 64, 128], P('gx', 'gy'), may hold values from 0 to 127
- owner_dir: int32 [32, 64, 128], P('gx', 'gy'), may hold values from 0 to 8, as said below
- body_pose: float32 [4, 8, 7, 128], P('gx', 'gy'), as said below
- body_motion: float32 [4, 8, 6, 128], P('gx', 'gy'), may hold values from -5 to 5
- body_inverse: float32 [4, 8, 4, 128], P('gx', 'gy'), may hold values from 0.1 to 1
- weight_u: bfloat16 [512, 256], replicated, may hold values from -0.375 to 0.375
- weight_v: bfloat16 [128, 256], replicated, may hold values from -0.375 to 0.375
- radial_rate: float32 [4], replicated, may hold values from 0.5 to 4
Outputs:
- moved: float32 [32, 64, 3, 128], P('gx', 'gy')
- body_next: float32 [4, 8, 13, 128], P('gx', 'gy')
The draws below stay inside these ranges and needn't reach their ends.
Inputs may be any that keep to these rules, and one draw needn't show every extreme that they name: `partner`: each tile's 6 codes are distinct; code 3 (a + 1) + (b + 1) names the tile a tiles along the first and b along the second dimension, a, b in -1, 0, 1. `owner_dir`: code 3 (a + 1) + (b + 1) names the domain a, b domains away; a is -1 only in a domain's first row of 8 tiles and 1 only in its last, b likewise for its 8 columns. `body_pose`: rows 3 to 6 are unit quaternions with a positive first entry.
All inputs are finite; a program needn't handle non-finite values.
Results may differ from the reference program's by a relative error of at most 0.0023.
Values may be sent and summed in bfloat16 or wider, within the bound.
No kernel may reach another device: no remote copies, remote signals or barrier semaphores. Data moves between devices by JAX's collectives and lax.ppermute only.
A program may use at most 128 MiB of HBM per device.

```python
import math
import jax
import jax.numpy as jnp
from jax import lax

F = 256
H = 128
K = 4
NB = 6
TILE = 128
BOD = 128
TX = 8
TY = 8
NXT = 32
NYT = 64
N_GX = 4
N_GY = 8


def draw_partner(key, part):
    scores = jax.random.randint(key, (NXT, NYT, 9), 0, 1048576) * 16 + jnp.arange(9, dtype=jnp.int32)
    order = jnp.argsort(scores, axis=-1)
    return order[:, :, :NB].astype(jnp.int32)


def draw_owner_dir(key, part):
    key_a, key_b = jax.random.split(key)
    coin_x = jax.random.randint(key_a, (NXT, NYT, TILE), 0, 4)
    coin_y = jax.random.randint(key_b, (NXT, NYT, TILE), 0, 4)
    local_x = (jnp.arange(NXT, dtype=jnp.int32) % TX)[:, None, None]
    local_y = (jnp.arange(NYT, dtype=jnp.int32) % TY)[None, :, None]
    step_x = jnp.where((local_x == 0) & (coin_x == 1), -1, jnp.where((local_x == TX - 1) & (coin_x == 2), 1, 0))
    step_y = jnp.where((local_y == 0) & (coin_y == 1), -1, jnp.where((local_y == TY - 1) & (coin_y == 2), 1, 0))
    return ((step_x + 1) * 3 + step_y + 1).astype(jnp.int32)


def draw_body_pose(key, part):
    key_c, key_w, key_v = jax.random.split(key, 3)
    centre = 1.5 * jax.random.normal(key_c, (N_GX, N_GY, 3, BOD))
    leading = jax.random.uniform(key_w, (N_GX, N_GY, 1, BOD), minval=0.5, maxval=1.0)
    others = 0.5 * jax.random.normal(key_v, (N_GX, N_GY, 3, BOD))
    quat = jnp.concatenate([leading, others], axis=2)
    quat = quat / jnp.sqrt(jnp.sum(quat * quat, axis=2, keepdims=True))
    return jnp.concatenate([centre, quat], axis=2).astype(jnp.float32)


def place_ends(values, key, smallest, high):
    dims = values.shape
    spot = [jax.random.randint(jax.random.fold_in(key, axis), (), 0, dims[axis]) for axis in range(len(dims))]
    values = values.at[tuple(spot)].set(smallest)
    longest = dims.index(max(dims))
    spot[longest] = (spot[longest] + 1) % dims[longest]
    return values.at[tuple(spot)].set(high)


def levels(own_key, extent, shards, low, top_value):
    def one(position, shards_of):
        steps = jax.random.uniform(jax.random.fold_in(jax.random.fold_in(own_key, 6), position), (shards_of,), jnp.float32, low / len(shards), top_value / len(shards))
        return jnp.repeat(jnp.exp(steps), extent[position] // shards_of).reshape((-1,) + (1,) * (len(extent) - position - 1))

    level = one(*shards[0])
    for cut in shards[1:]:
        level = level * one(*cut)
    return level


def normal_values(stream_key, dims, deviation, most, cuts=(), kind=jnp.bfloat16):
    level = levels(stream_key, dims, cuts, -0.22, 0.18) if cuts else 1.0
    values = jax.random.normal(stream_key, dims, jnp.float32) * deviation * level
    return jnp.minimum(jnp.maximum(values, -most), most).astype(kind)


def setup_inputs(seed: int = 0) -> dict:
    arg_keys = jax.random.split(jax.random.key(seed), 13)
    positions = jnp.clip(1.0 * jax.random.uniform(arg_keys[0], (NXT, NYT, 3, TILE), jnp.float32) ** levels(arg_keys[0], (NXT, NYT, 3, TILE), ((0, 4), (1, 8)), -0.2, 0.2), 0.0, 1.0).astype(jnp.bfloat16)
    features = normal_values(arg_keys[1], (NXT, NYT, F, TILE), 1.0, 6.0, ((0, 4), (1, 8)))
    lever = normal_values(arg_keys[2], (NXT, NYT, 3, TILE), 1.0, 4.0, ((0, 4), (1, 8)), jnp.float32)
    partner = draw_partner(jax.random.fold_in(arg_keys[12], 71), 0)
    body_slot = place_ends(jax.random.randint(arg_keys[4], (NXT, NYT, TILE), 0, BOD), jax.random.fold_in(arg_keys[4], 1), 0, BOD - 1).astype(jnp.int32)
    owner_dir = draw_owner_dir(jax.random.fold_in(arg_keys[12], 71), 0)
    body_pose = draw_body_pose(jax.random.fold_in(arg_keys[12], 71), 0)
    body_motion = normal_values(arg_keys[7], (N_GX, N_GY, 6, BOD), 1.0, 5.0, ((0, 4), (1, 8)), jnp.float32)
    body_inverse = jnp.clip(jnp.exp(math.log(1.0) - 2.3025851 * jax.random.uniform(arg_keys[8], (N_GX, N_GY, 4, BOD), jnp.float32) ** levels(arg_keys[8], (N_GX, N_GY, 4, BOD), ((0, 4), (1, 8)), -0.2, 0.2)), 0.1, 1.0)
    weight_u = normal_values(arg_keys[9], (K * H, F), F ** -0.5, 0.375)
    weight_v = normal_values(arg_keys[10], (H, F), F ** -0.5, 0.375)
    radial_rate = jnp.clip(jnp.exp(jax.random.uniform(arg_keys[11], (K,), jnp.float32, math.log(0.5), math.log(4.0))), 0.5, 4.0)
    return dict(positions=positions, features=features, lever=lever, partner=partner, body_slot=body_slot, owner_dir=owner_dir, body_pose=body_pose, body_motion=body_motion, body_inverse=body_inverse, weight_u=weight_u, weight_v=weight_v, radial_rate=radial_rate)


STEP_DT = 0.25
CUT_SQUARE = 4.0

def rotation(quat):
    qw, qa, qb, qc = (quat[0], quat[1], quat[2], quat[3])
    first = jnp.stack([1 - 2 * (qb * qb + qc * qc), 2 * (qa * qb - qw * qc), 2 * (qa * qc + qw * qb)])
    second = jnp.stack([2 * (qa * qb + qw * qc), 1 - 2 * (qa * qa + qc * qc), 2 * (qb * qc - qw * qa)])
    third = jnp.stack([2 * (qa * qc - qw * qb), 2 * (qb * qc + qw * qa), 1 - 2 * (qa * qa + qb * qb)])
    return jnp.stack([first, second, third])

def integrate(pose, motion, inverse, totals):
    centre = pose[0:3]
    quat = pose[3:7]
    new_vel = motion[0:3] + STEP_DT * inverse[0] * totals[0:3]
    new_centre = centre + STEP_DT * new_vel
    new_ang = motion[3:6] + STEP_DT * totals[3:6]
    rot_old = rotation(quat)
    body_frame = lax.optimization_barrier(jnp.sum(rot_old * new_ang[:, None], axis=0)) * inverse[1:4]
    omega = lax.optimization_barrier(jnp.sum(rot_old * body_frame[None, :], axis=1))
    scalar = -lax.optimization_barrier(jnp.sum(omega * quat[1:4], axis=0))
    vector = quat[0] * omega + jnp.cross(omega, quat[1:4], axis=0)
    stepped = quat + 0.5 * STEP_DT * jnp.concatenate([scalar[None], vector], axis=0)
    new_quat = stepped / jnp.sqrt(lax.optimization_barrier(jnp.sum(stepped * stepped, axis=0)))
    rot_new = rotation(new_quat)
    relative = lax.optimization_barrier(jnp.sum(rot_new[:, None, :] * rot_old[None, :, :], axis=2))
    next_state = jnp.concatenate([new_centre, new_quat, new_vel, new_ang], axis=0)
    packed = jnp.concatenate([STEP_DT * new_vel, relative.reshape((9,) + relative.shape[2:])], axis=0)
    return (next_state, packed)

def tile_forces(u_row, p_row, v_part, p_part, offset, radial_rate):
    differ = p_row[:, :, :, None] - p_part[:, :, None, :] - offset[:, :, None, None]
    radius_sq = lax.optimization_barrier(jnp.sum(differ * differ, axis=1))
    envelope = jnp.square(jnp.maximum(1.0 - radius_sq / CUT_SQUARE, 0.0))
    scores = jnp.einsum('mkha,mhb->mkab', u_row.astype(jnp.float32), v_part.astype(jnp.float32))
    radial = jnp.exp(-radial_rate[None, :, None, None] * radius_sq[:, None])
    couple = envelope * lax.optimization_barrier(jnp.sum(radial * scores, axis=1)) / v_part.shape[1]
    weight_sum = lax.optimization_barrier(jnp.sum(couple, axis=2))
    pulled = jnp.einsum('mab,mcb->mca', couple, p_part, precision=lax.Precision.HIGHEST)
    return (p_row - offset[:, :, None]) * weight_sum[:, None, :] - pulled

def reference(positions, features, lever, partner, body_slot, owner_dir, body_pose, body_motion, body_inverse, weight_u, weight_v, radial_rate):
    weight_uf = weight_u.astype(jnp.float32)
    weight_vf = weight_v.astype(jnp.float32)

    def project_row(feat_row):
        return jnp.einsum('hf,yfb->yhb', weight_vf, feat_row.astype(jnp.float32)).astype(jnp.bfloat16)
    proj_v = lax.map(project_row, features)
    flat_v = proj_v.reshape(NXT * NYT, H, TILE)
    flat_pos = positions.astype(jnp.float32).reshape(NXT * NYT, 3, TILE)
    col_index = jnp.arange(NYT, dtype=jnp.int32)

    def row_forces(inputs):
        row_index, feat_row, pos_row, codes = inputs
        u_row = jnp.einsum('gf,yfb->ygb', weight_uf, feat_row.astype(jnp.float32)).astype(jnp.bfloat16)
        u_row = u_row.reshape(NYT, K, H, TILE)
        p_row = pos_row.astype(jnp.float32)
        total = jnp.zeros((NYT, 3, TILE), jnp.float32)
        for which in range(NB):
            code = codes[:, which]
            off_x = code // 3 - 1
            off_y = code % 3 - 1
            global_index = (row_index + off_x) % NXT * NYT + (col_index + off_y) % NYT
            v_part = flat_v[global_index]
            p_part = flat_pos[global_index]
            offset = jnp.stack([off_x, off_y, jnp.zeros_like(off_x)], axis=1).astype(jnp.float32)
            total = total + tile_forces(u_row, p_row, v_part, p_part, offset, radial_rate)
        return total
    forces = lax.map(row_forces, (jnp.arange(NXT, dtype=jnp.int32), features, positions, partner))
    torque = jnp.cross(lever, forces, axis=2)
    terms = jnp.concatenate([forces, torque], axis=2)
    grid_x = jnp.arange(NXT, dtype=jnp.int32)[:, None, None]
    grid_y = jnp.arange(NYT, dtype=jnp.int32)[None, :, None]
    owner_x = (grid_x // TX + owner_dir // 3 - 1) % N_GX
    owner_y = (grid_y // TY + owner_dir % 3 - 1) % N_GY
    body_ids = (owner_x * N_GY + owner_y) * BOD + body_slot
    flat_terms = jnp.moveaxis(terms, 2, 3).reshape(-1, 6)
    sums = jax.ops.segment_sum(flat_terms, body_ids.reshape(-1), num_segments=N_GX * N_GY * BOD)
    sums = sums.reshape(N_GX, N_GY, BOD, 6)
    next_state, packed = integrate(jnp.moveaxis(body_pose, 2, 0), jnp.moveaxis(body_motion, 2, 0), jnp.moveaxis(body_inverse, 2, 0), jnp.moveaxis(sums, 3, 0))
    body_next = jnp.moveaxis(next_state, 0, 2)
    table = jnp.moveaxis(packed, 0, -1).reshape(-1, 12)
    looked = jnp.moveaxis(table[body_ids], 3, 2)
    rotated = jnp.stack([lax.optimization_barrier(jnp.sum(looked[:, :, 3 + 3 * row:6 + 3 * row] * lever, axis=2)) for row in range(3)], axis=2)
    moved = positions.astype(jnp.float32) + looked[:, :, 0:3] + rotated - lever
    return (moved, body_next)
```

```python
import math
import jax
import jax.numpy as jnp
from jax import lax
from jax.experimental import pallas as pl
from jax.experimental.pallas import tpu as pltpu
from jax.sharding import PartitionSpec as P

STEP_DT = 0.25
CUT_SQUARE = 4.0
F32 = jnp.float32
BF16 = jnp.bfloat16
VMEM = pl.BlockSpec(memory_space=pltpu.VMEM)
SMEM = pl.BlockSpec(memory_space=pltpu.SMEM)
HBM = pl.BlockSpec(memory_space=pl.ANY)
LIMIT = 56 * 2**20
DIRS = [(-1, -1), (-1, 0), (-1, 1), (0, -1), (0, 1), (1, -1), (1, 0), (1, 1)]
EXTRA = 16


def rows_iota(rows, lanes):
    return lax.broadcasted_iota(jnp.int32, (rows, lanes), 0)


def split_two(value):
    high = value.astype(BF16)
    return high, (value - high.astype(F32)).astype(BF16)


def one_hot(keys, slots, base):
    hit = rows_iota(slots, keys.shape[-1]) == keys - base
    return jnp.where(hit, 1.0, 0.0).astype(BF16)


def project_kernel(feat, pos, weight_v, own, top, bottom, left, right, c0, c1, c2, c3):
    x = pl.program_id(0)
    last_x = pl.num_programs(0) - 1
    tiles_y, beads = feat.shape[1], feat.shape[3]
    row = rows_iota(8, beads)
    for y in range(0, tiles_y, 2):
        both = jnp.concatenate([feat[0, y], feat[0, y + 1]], axis=1)
        v = jnp.dot(weight_v[...], both, preferred_element_type=F32).astype(BF16)
        for e in range(2):
            own[0, y + e, 0:beads, :] = v[:, e * beads : (e + 1) * beads].T
            p = pos[0, y + e].astype(F32)
            px, py, pz = (jnp.broadcast_to(p[c : c + 1], (8, beads)) for c in range(3))
            norm = -0.25 * (px * px + py * py + pz * pz)
            n1 = norm.astype(BF16).astype(F32)
            n2 = (norm - n1).astype(BF16).astype(F32)
            n3 = norm - n1 - n2
            first = px
            for r, val in ((1, py), (2, pz), (3, px), (4, py), (5, n1), (6, n2), (7, n3)):
                first = jnp.where(row == r, val, first)
            second = jnp.where(row < 3, 1.0, 0.0)
            own[0, y + e, beads : beads + EXTRA, :] = jnp.concatenate(
                [first, second], axis=0
            ).astype(BF16)
    left[0] = own[0, 0]
    right[0] = own[0, tiles_y - 1]

    @pl.when(x == 0)
    def _():
        top[...] = own[0]
        c0[...] = own[0, 0]
        c1[...] = own[0, tiles_y - 1]

    @pl.when(x == last_x)
    def _():
        bottom[...] = own[0]
        c2[...] = own[0, 0]
        c3[...] = own[0, tiles_y - 1]


def project(features, positions, weight_v):
    tx, ty, f, beads = features.shape
    rows = beads + EXTRA
    fixed3 = lambda s: pl.BlockSpec(s, lambda i: (0, 0, 0))
    fixed2 = lambda s: pl.BlockSpec(s, lambda i: (0, 0))
    sds = lambda *s: jax.ShapeDtypeStruct(s, BF16)
    return pl.pallas_call(
        project_kernel,
        grid=(tx,),
        out_shape=[sds(tx, ty, rows, beads), sds(ty, rows, beads), sds(ty, rows, beads),
                   sds(tx, rows, beads), sds(tx, rows, beads)] + [sds(rows, beads)] * 4,
        in_specs=[
            pl.BlockSpec((1, ty, f, beads), lambda i: (i, 0, 0, 0)),
            pl.BlockSpec((1, ty, 3, beads), lambda i: (i, 0, 0, 0)),
            fixed2(weight_v.shape),
        ],
        out_specs=[
            pl.BlockSpec((1, ty, rows, beads), lambda i: (i, 0, 0, 0)),
            fixed3((ty, rows, beads)), fixed3((ty, rows, beads)),
            pl.BlockSpec((1, rows, beads), lambda i: (i, 0, 0)),
            pl.BlockSpec((1, rows, beads), lambda i: (i, 0, 0)),
        ] + [fixed2((rows, beads))] * 4,
        compiler_params=pltpu.CompilerParams(vmem_limit_bytes=LIMIT),
    )(features, positions, weight_v)


def pairs_kernel(tiles, halo, shape, *refs):
    n = len(tiles)
    tx, ty, beads, width_h, chans, nb, slots = shape
    refs = list(refs)
    take = lambda k: [refs.pop(0) for _ in range(k)]
    ids, partner, rate, features, weight_u, lever, slot, owner, own = take(9)
    around = take(8) if halo else []
    sums = refs.pop(0)
    sent = take(8) if halo else []
    feat, ub, sa, sb, za, zb, ca, cb, wz, fsem = take(10)
    terms, vp, vsem = take(3) if halo else (None, own, None)
    org = 1 if halo else 0
    side = chans * width_h

    for q, (i, j) in enumerate(tiles):
        pltpu.make_async_copy(features.at[i, j], feat.at[q], fsem.at[q]).start()
    if halo:
        places = [vp.at[0, 0], vp.at[0, 1 : ty + 1], vp.at[0, ty + 1], vp.at[1 : tx + 1, 0],
                  vp.at[1 : tx + 1, ty + 1], vp.at[tx + 1, 0], vp.at[tx + 1, 1 : ty + 1],
                  vp.at[tx + 1, ty + 1], vp.at[1 : tx + 1, 1 : ty + 1]]
        copies = [pltpu.make_async_copy(src, dst, vsem.at[q])
                  for q, (src, dst) in enumerate(zip(around + [own], places))]
        for copy in copies:
            copy.start()
    wz[...] = jnp.zeros_like(wz)
    sums[...] = jnp.zeros_like(sums)
    row8 = rows_iota(8, beads)
    row16 = rows_iota(16, beads)

    def wait_feat(t):
        pltpu.make_async_copy(features.at[0, 0], feat.at[t], fsem.at[t]).wait()

    def where_is(t):
        return ids[t] // ty, ids[t] % ty

    def codes(i, j, m):
        code = partner[i, j, m]
        a = lax.shift_right_logical(code * 11, 5)
        return a - 1, code - 3 * a - 1

    def make_u(s):
        both = jnp.concatenate([feat[2 * s], feat[2 * s + 1]], axis=1)
        u = jnp.dot(weight_u[...], both, preferred_element_type=F32).astype(BF16)
        for e in range(2):
            for k in range(chans):
                ub[e, :, k * beads : (k + 1) * beads] = u[
                    k * width_h : (k + 1) * width_h, e * beads : (e + 1) * beads]

    def scores(t, e, buf, zbuf):
        i, j = where_is(t)
        lhs, feats = [], []
        mine = vp[i + org, j + org, beads : beads + EXTRA, :].astype(F32)
        up = mine[0:8]
        bx, by = (jnp.broadcast_to(up[c : c + 1], (8, beads)) for c in (0, 1))
        bn = jnp.broadcast_to(up[5:6] + up[6:7] + up[7:8], (8, beads))
        fixed = jnp.where(row8 < 3, 0.5 * up, jnp.where(row8 >= 5, 1.0, 0.0))
        for m in range(nb):
            a, b = codes(i, j, m)
            lhs.append(vp[i + a + org, j + b + org, 0:beads, :])
            feats.append(vp[i + a + org, j + b + org, beads : beads + EXTRA, :])
            af, bf = a.astype(F32), b.astype(F32)
            high = jnp.where(row8 == 3, -0.5 * af, jnp.where(row8 == 4, -0.5 * bf, fixed))
            norm = bn + bx * (0.5 * af) + by * (0.5 * bf) - 0.25 * (af * af + bf * bf)
            n1 = norm.astype(BF16).astype(F32)
            rest = norm - n1
            n2 = rest.astype(BF16).astype(F32)
            low = jnp.where(row8 == 0, n1, jnp.where(row8 == 1, n2, jnp.where(row8 == 2, rest - n2, 0.0)))
            wz[m // 2, EXTRA * (m % 2) : EXTRA * (m % 2 + 1), (m % 2) * beads : (m % 2 + 1) * beads] = (
                jnp.concatenate([high, low], axis=0).astype(BF16))
        for h in range(nb // 2):
            left = jnp.concatenate([feats[2 * h], feats[2 * h + 1]], axis=0)
            zbuf[h] = lax.dot_general(left, wz[h], (((0,), (0,)), ((), ())), preferred_element_type=F32)
        buf[...] = jnp.dot(jnp.concatenate(lhs, axis=0), ub[e], preferred_element_type=F32)

    def couples(buf, zbuf, cbuf):
        step = 16
        for m in range(nb):
            for r in range(0, beads, step):
                z = zbuf[m // 2, r : r + step, (m % 2) * beads : (m % 2 + 1) * beads]
                env = jnp.maximum(1.0 + z, 0.0)
                total = None
                for k in range(chans):
                    part = jnp.exp2(z * (rate[k] * (CUT_SQUARE / math.log(2.0)))) * buf[
                        m * beads + r : m * beads + r + step, k * beads : (k + 1) * beads]
                    total = part if total is None else total + part
                cbuf[m * beads + r : m * beads + r + step, :] = ((env * env) * total).astype(BF16)

    def gather(t, cbuf):
        i, j = where_is(t)
        lhs = []
        for m in range(nb):
            a, b = codes(i, j, m)
            base = vp[i + a + org, j + b + org, beads : beads + EXTRA, :]
            extra = jnp.where(row16 == 11, a.astype(F32), jnp.where(row16 == 12, b.astype(F32), 0.0))
            lhs.append(base + extra.astype(BF16))
        out = jnp.dot(jnp.concatenate(lhs, axis=1), cbuf[...], preferred_element_type=F32)
        out = out * (1.0 / width_h)
        mine = vp[i + org, j + org, beads : beads + EXTRA, :].astype(F32)
        w = out[8:9]
        fx = mine[0:1] * w - out[0:1] - out[11:12]
        fy = mine[1:2] * w - out[1:2] - out[12:13]
        fz = mine[2:3] * w - out[2:3]
        lev = lever[i, j]
        lx, ly, lz = lev[0:1], lev[1:2], lev[2:3]
        value = jnp.concatenate(
            [fx, fy, fz, ly * fz - lz * fy, lz * fx - lx * fz, lx * fy - ly * fx,
             jnp.zeros((2, beads), F32)], axis=0)
        term = jnp.concatenate(split_two(value), axis=0)
        if halo:
            terms[t] = term
        key = owner[i, pl.ds(j, 1), :] * slots + slot[i, pl.ds(j, 1), :]
        got = lax.dot_general(term, one_hot(key, slots, 4 * slots), (((1,), (1,)), ((), ())),
                              preferred_element_type=F32)
        return got[0:8] + got[8:16]

    wait_feat(0)
    wait_feat(1)
    make_u(0)
    if halo:
        for copy in copies:
            copy.wait()
    scores(0, 0, sa, za)

    def body(s, carry):
        before = jnp.maximum(2 * s - 2, 0)
        later = jnp.minimum(s + 1, n // 2 - 1)

        @pl.when(s < n // 2 - 1)
        def _():
            wait_feat(2 * s + 2)
            wait_feat(2 * s + 3)

        old = gather(before, ca) + gather(before + 1, cb)
        sums[...] = jnp.where(s == 0, 0.0, sums[...] + old)
        scores(2 * s + 1, 1, sb, zb)
        couples(sa, za, ca)
        make_u(later)
        scores(2 * later, 0, sa, za)
        couples(sb, zb, cb)
        return carry

    lax.fori_loop(0, n // 2, body, 0)
    sums[...] = sums[...] + gather(n - 2, ca) + gather(n - 1, cb)
    if halo:
        for q, (a, b) in enumerate(DIRS):
            keep = [t for t, (i, j) in enumerate(tiles)
                    if (a == 0 or i == (0 if a < 0 else tx - 1)) and (b == 0 or j == (0 if b < 0 else ty - 1))]
            left, right = [], []
            for t in keep:
                i, j = tiles[t]
                key = owner[i, j : j + 1, :] * slots + slot[i, j : j + 1, :]
                left.append(terms[t])
                right.append(one_hot(key, slots, (3 * a + b + 4) * slots))
            got = lax.dot_general(jnp.concatenate(left, axis=1), jnp.concatenate(right, axis=1),
                                  (((1,), (1,)), ((), ())), preferred_element_type=F32)
            sent[q][...] = got[0:8] + got[8:16]


def pairs(tiles, halo, args, own, around):
    partner, rate, features, weight_u, lever, slot, owner, slots = args
    tx, ty, f, beads = features.shape
    nb = partner.shape[2]
    chans = rate.shape[0]
    width_h = weight_u.shape[0] // chans
    rows = beads + EXTRA
    n = len(tiles)
    total = jax.ShapeDtypeStruct((8, slots), F32)
    scratch = [
        pltpu.VMEM((n, f, beads), BF16),
        pltpu.VMEM((2, width_h, chans * beads), BF16),
        pltpu.VMEM((nb * beads, chans * beads), F32),
        pltpu.VMEM((nb * beads, chans * beads), F32),
        pltpu.VMEM((nb // 2, beads, 2 * beads), F32),
        pltpu.VMEM((nb // 2, beads, 2 * beads), F32),
        pltpu.VMEM((nb * beads, beads), BF16),
        pltpu.VMEM((nb * beads, beads), BF16),
        pltpu.VMEM((nb // 2, 2 * EXTRA, 2 * beads), BF16),
        pltpu.SemaphoreType.DMA((n,)),
    ]
    if halo:
        scratch += [pltpu.VMEM((n, 16, beads), BF16), pltpu.VMEM((tx + 2, ty + 2, rows, beads), BF16),
                    pltpu.SemaphoreType.DMA((9,))]
    ids = jnp.asarray([i * ty + j for i, j in tiles], jnp.int32)
    shape = (tx, ty, beads, width_h, chans, nb, slots)
    return pl.pallas_call(
        lambda *refs: pairs_kernel(tiles, halo, shape, *refs),
        out_shape=[total] * (9 if halo else 1),
        in_specs=[SMEM, SMEM, SMEM, HBM, VMEM, VMEM, VMEM, VMEM, HBM if halo else VMEM]
        + [HBM] * (8 if halo else 0),
        out_specs=[VMEM] * (9 if halo else 1),
        scratch_shapes=scratch,
        compiler_params=pltpu.CompilerParams(vmem_limit_bytes=LIMIT),
        cost_estimate=pl.CostEstimate(flops=n * 150_000_000, bytes_accessed=n * 100_000, transcendentals=0),
    )(ids, partner, rate, features, weight_u, lever, slot, owner, own, *(around if halo else []))


def rotation_rows(q):
    w, a, b, c = q
    return [
        [1 - 2 * (b * b + c * c), 2 * (a * b - w * c), 2 * (a * c + w * b)],
        [2 * (a * b + w * c), 1 - 2 * (a * a + c * c), 2 * (b * c - w * a)],
        [2 * (a * c - w * b), 2 * (b * c + w * a), 1 - 2 * (a * a + b * b)],
    ]


def integrate_kernel(*refs):
    sums, (pose, motion, inverse, state, packed) = refs[:-5], refs[-5:]
    total = sums[0][...]
    for other in sums[1:]:
        total = total + other[...]
    row = lambda ref, r: ref[0, 0, r : r + 1, :]
    f = [total[r : r + 1] for r in range(6)]
    q = [row(pose, 3 + r) for r in range(4)]
    vel = [row(motion, r) + STEP_DT * row(inverse, 0) * f[r] for r in range(3)]
    centre = [row(pose, r) + STEP_DT * vel[r] for r in range(3)]
    ang = [row(motion, 3 + r) + STEP_DT * f[3 + r] for r in range(3)]
    old = rotation_rows(q)
    frame = [sum(old[r][c] * ang[r] for r in range(3)) * row(inverse, 1 + c) for c in range(3)]
    om = [sum(old[r][c] * frame[c] for c in range(3)) for r in range(3)]
    w, x, y, z = q
    rate = [
        -(om[0] * x + om[1] * y + om[2] * z),
        w * om[0] + om[1] * z - om[2] * y,
        w * om[1] + om[2] * x - om[0] * z,
        w * om[2] + om[0] * y - om[1] * x,
    ]
    step = [q[r] + 0.5 * STEP_DT * rate[r] for r in range(4)]
    size = jnp.sqrt(sum(s * s for s in step))
    new = [s / size for s in step]
    turned = rotation_rows(new)
    rel = [sum(turned[r][k] * old[c][k] for k in range(3)) for r in range(3) for c in range(3)]
    for r, val in enumerate(centre + new + vel + ang):
        state[0, 0, r : r + 1, :] = val
    for r, val in enumerate([STEP_DT * v for v in vel] + rel):
        packed[r : r + 1, :] = val
    packed[12:16, :] = jnp.zeros((4, packed.shape[1]), F32)


def integrate(sums, pose, motion, inverse):
    slots = pose.shape[3]
    return pl.pallas_call(
        integrate_kernel,
        out_shape=[jax.ShapeDtypeStruct((1, 1, 13, slots), F32), jax.ShapeDtypeStruct((16, slots), F32)],
        in_specs=[VMEM] * (len(sums) + 3),
        out_specs=[VMEM] * 2,
    )(*sums, pose, motion, inverse)


def place(table, key, base, lev):
    slots = table.shape[1]
    got = jnp.dot(table, one_hot(key, slots, base), preferred_element_type=F32)
    got = got[0:16] + got[16:32]
    out = got[0:3]
    turned = [
        sum(got[3 + 3 * r + c : 4 + 3 * r + c] * lev[c : c + 1] for c in range(3)) for r in range(3)
    ]
    return out + jnp.concatenate(turned, axis=0)


def move_own_kernel(packed, pos, lever, slot, owner, moved):
    tx, ty = pos.shape[0], pos.shape[1]
    slots = packed.shape[1]
    table = jnp.concatenate(split_two(packed[...]), axis=0)

    def line(i, carry):
        for j in range(ty):
            key = owner[i, j : j + 1, :] * slots + slot[i, j : j + 1, :]
            lev = lever[i, j]
            moved[i, j] = pos[i, j].astype(F32) + place(table, key, 4 * slots, lev) - lev
        return carry

    lax.fori_loop(0, tx, line, 0)


def move_own(packed, pos, lever, slot, owner):
    return pl.pallas_call(
        move_own_kernel,
        out_shape=jax.ShapeDtypeStruct(lever.shape, F32),
        in_specs=[VMEM] * 5,
        out_specs=VMEM,
        compiler_params=pltpu.CompilerParams(vmem_limit_bytes=LIMIT),
    )(packed, pos, lever, slot, owner)


def move_rim_kernel(*refs):
    tables, (part, lever, slot, owner, moved) = refs[:8], refs[8:]
    tx, ty = part.shape[0], part.shape[1]
    slots = tables[0].shape[1]
    moved[...] = part[...]
    for q, (a, b) in enumerate(DIRS):
        table = jnp.concatenate(split_two(tables[q][...]), axis=0)
        for i in range(tx) if a == 0 else [0 if a < 0 else tx - 1]:
            for j in range(ty) if b == 0 else [0 if b < 0 else ty - 1]:
                key = owner[i, j : j + 1, :] * slots + slot[i, j : j + 1, :]
                moved[i, j] = moved[i, j] + place(table, key, (3 * a + b + 4) * slots, lever[i, j])


def move_rim(tables, part, lever, slot, owner):
    return pl.pallas_call(
        move_rim_kernel,
        out_shape=jax.ShapeDtypeStruct(lever.shape, F32),
        in_specs=[VMEM] * 12,
        out_specs=VMEM,
        compiler_params=pltpu.CompilerParams(vmem_limit_bytes=LIMIT),
    )(*tables, part, lever, slot, owner)


def shifted(value, a, b):
    nx, ny = lax.axis_size("gx"), lax.axis_size("gy")
    if a == 0:
        return lax.ppermute(value, "gy", [(y, (y + b) % ny) for y in range(ny)])
    if b == 0:
        return lax.ppermute(value, "gx", [(x, (x + a) % nx) for x in range(nx)])
    route = [(x * ny + y, (x + a) % nx * ny + (y + b) % ny) for x in range(nx) for y in range(ny)]
    return lax.ppermute(value, ("gx", "gy"), route)


def local(positions, features, lever, partner, body_slot, owner_dir, body_pose, body_motion,
          body_inverse, weight_u, weight_v, radial_rate):
    tx, ty = positions.shape[0], positions.shape[1]
    slots = body_pose.shape[3]
    own, top, bottom, left, right, c0, c1, c2, c3 = project(features, positions, weight_v)
    edge = {(-1, -1): c3, (-1, 0): bottom, (-1, 1): c2, (0, -1): right, (0, 1): left,
            (1, -1): c1, (1, 0): top, (1, 1): c0}
    around = [shifted(edge[d], -d[0], -d[1]) for d in DIRS]
    args = (partner, radial_rate, features, weight_u, lever, body_slot, owner_dir, slots)
    inner = [(i, j) for i in range(1, tx - 1) for j in range(1, ty - 1)]
    rim = [(i, j) for i in range(tx) for j in range(ty) if i in (0, tx - 1) or j in (0, ty - 1)]
    cut = 24
    (first,) = pairs(inner[:cut], False, args, own, None)
    second, *out = pairs(rim, True, args, own, around)
    got = [shifted(value, a, b) for value, (a, b) in zip(out, DIRS)]
    (third,) = pairs(inner[cut:], False, args, own, None)
    state, packed = integrate([first, second, third] + got, body_pose, body_motion, body_inverse)
    tables = [shifted(packed, -a, -b) for a, b in DIRS]
    part = move_own(packed, positions, lever, body_slot, owner_dir)
    moved = move_rim(tables, part, lever, body_slot, owner_dir)
    return (moved, state)


def solution(mesh):
    placed = (
        P("gx", "gy", None, None),
        P("gx", "gy", None, None),
        P("gx", "gy", None, None),
        P("gx", "gy", None),
        P("gx", "gy", None),
        P("gx", "gy", None),
        P("gx", "gy", None, None),
        P("gx", "gy", None, None),
        P("gx", "gy", None, None),
        P(),
        P(),
        P(),
    )
    return jax.shard_map(
        local,
        mesh=mesh,
        in_specs=placed,
        out_specs=(P("gx", "gy", None, None), P("gx", "gy", None, None)),
        check_vma=False,
    )
```

```python
import math
import jax
import jax.numpy as jnp
from jax import lax
from jax.experimental import pallas as pl
from jax.experimental.pallas import tpu as pltpu
from jax.sharding import PartitionSpec as P

STEP_DT = 0.25
CUT_SQUARE = 4.0
F32 = jnp.float32
BF16 = jnp.bfloat16
VMEM = pl.BlockSpec(memory_space=pltpu.VMEM)
SMEM = pl.BlockSpec(memory_space=pltpu.SMEM)
HBM = pl.BlockSpec(memory_space=pl.ANY)
LIMIT = 56 * 2**20
DIRS = [(-1, -1), (-1, 0), (-1, 1), (0, -1), (0, 1), (1, -1), (1, 0), (1, 1)]
EXTRA = 16
BODY = 48


def rows_iota(rows, lanes):
    return lax.broadcasted_iota(jnp.int32, (rows, lanes), 0)


def split_two(value):
    high = value.astype(BF16)
    return high, (value - high.astype(F32)).astype(BF16)


def one_hot(keys, slots, base):
    hit = rows_iota(slots, keys.shape[-1]) == keys - base
    return jnp.where(hit, 1.0, 0.0).astype(BF16)


def outward(axis):
    return lax.rem(lax.axis_index(axis), 2) == 1


def split_three(value):
    first = value.astype(BF16)
    rest = value - first.astype(F32)
    second = rest.astype(BF16)
    return first, second, (rest - second.astype(F32)).astype(BF16)


def project_kernel(feat, pos, weight_v, pose, motion, inverse, own, col_in, col_out, row_in, row_out):
    x = pl.program_id(0)
    tiles_x, tiles_y, beads = pl.num_programs(0), feat.shape[1], feat.shape[3]
    rows = beads + EXTRA
    row = rows_iota(8, beads)
    high_x, high_y = outward("gx"), outward("gy")
    for y in range(0, tiles_y, 2):
        both = jnp.concatenate([feat[0, y], feat[0, y + 1]], axis=1)
        v = jnp.dot(weight_v[...], both, preferred_element_type=F32).astype(BF16)
        for e in range(2):
            own[0, y + e, 0:beads, :] = v[:, e * beads : (e + 1) * beads].T
            px, py, pz = (jnp.broadcast_to(pos[0, c, y + e : y + e + 1, :].astype(F32), (8, beads)) for c in range(3))
            norm = -0.25 * (px * px + py * py + pz * pz)
            n1, n2, n3 = (part.astype(F32) for part in split_three(norm))
            first = px
            for r, val in ((1, py), (2, pz), (3, px), (4, py), (5, n1), (6, n2), (7, n3)):
                first = jnp.where(row == r, val, first)
            second = jnp.where(row < 3, 1.0, 0.0)
            own[0, y + e, beads:rows, :] = jnp.concatenate([first, second], axis=0).astype(BF16)
    at = pl.ds(pl.multiple_of(x * rows, 16), rows)
    low, high = own[0, 0], own[0, tiles_y - 1]
    col_in[at, :] = jnp.where(high_y, low, high)
    col_out[at, :] = jnp.where(high_y, high, low)

    @pl.when(x == jnp.where(high_x, 0, tiles_x - 1))
    def _():
        row_in[...] = own[0]

    @pl.when(x == jnp.where(high_x, tiles_x - 1, 0))
    def _():
        row_out[...] = own[0]

    @pl.when(x == 0)
    def _():
        body = jnp.concatenate(
            [pose[0, r] for r in range(3, 7)] + [motion[0, r] for r in range(6)]
            + [inverse[0, 0, r : r + 1, :] for r in range(4)] + [jnp.zeros((2, beads), F32)], axis=0)
        body = jnp.concatenate(split_three(body), axis=0)
        end = col_in.shape[0] - BODY
        col_in[end:, :] = body
        col_out[end:, :] = body


def project(features, pos, weight_v, pose, motion, inverse):
    tx, ty, f, beads = features.shape
    rows = beads + EXTRA
    whole = lambda s: pl.BlockSpec(s, lambda i: (0,) * len(s))
    sds = lambda *s: jax.ShapeDtypeStruct(s, BF16)
    col = (tx * rows + BODY, beads)
    return pl.pallas_call(
        project_kernel,
        grid=(tx,),
        out_shape=[sds(tx, ty, rows, beads), sds(*col), sds(*col), sds(ty, rows, beads), sds(ty, rows, beads)],
        in_specs=[
            pl.BlockSpec((1, ty, f, beads), lambda i: (i, 0, 0, 0)),
            pl.BlockSpec((1, 3, ty, beads), lambda i: (i, 0, 0, 0)),
            whole(weight_v.shape), whole(pose.shape), whole(motion.shape), whole(inverse.shape),
        ],
        out_specs=[
            pl.BlockSpec((1, ty, rows, beads), lambda i: (i, 0, 0, 0)),
            whole(col), whole(col), whole((ty, rows, beads)), whole((ty, rows, beads)),
        ],
        compiler_params=pltpu.CompilerParams(vmem_limit_bytes=LIMIT),
    )(features, pos, weight_v, pose, motion, inverse)


def pairs_kernel(strips, halo, shape, *refs):
    tiles = [(i, j) for rows, cols in strips for i in rows for j in cols]
    n = len(tiles)
    tx, ty, beads, width_h, chans, nb, slots = shape
    refs = list(refs)
    take = lambda k: [refs.pop(0) for _ in range(k)]
    ids, partner, rate, features, weight_u, lever, slot, owner, own = take(9)
    around = take(7) if halo else []
    sums = refs.pop(0)
    where_to, code_of = take(2)
    feat, ub, sa, sb, za, zb, ca, cb, wa, wb, high_of, norm_of, extra_of, fsem = take(14)
    terms, vp, vsem, total = take(4) if halo else (None, own, None, sums)
    wide = ty + 2
    here = lambda i, j: (i + 1) * wide + j + 1 if halo else i * ty + j
    side = chans * width_h

    at = 0
    loads = []
    for q, (i, j) in enumerate(strips):
        size = max(len(i), len(j))
        src = features.at[i[0], j[0] : j[-1] + 1] if len(i) == 1 else features.at[i[0] : i[-1] + 1, j[0]]
        loads.append(pltpu.make_async_copy(src, feat.at[at : at + size], fsem.at[q]))
        loads[-1].start()
        at += size
    if halo:
        rows = beads + EXTRA
        high_x, high_y = outward("gx"), outward("gy")
        x_in, x_out = jnp.where(high_x, 0, tx + 1), jnp.where(high_x, tx + 1, 0)
        y_in, y_out = jnp.where(high_y, 0, ty + 1), jnp.where(high_y, ty + 1, 0)
        line = lambda i: vp.at[pl.ds(i * wide + 1, ty)]
        cols, lines, ends = around[0:2], around[2:4], around[4:6]
        pairs_of = []
        for i in range(tx):
            for col, y in zip(cols, (y_in, y_out)):
                pairs_of.append((col.at[pl.ds(i * rows, rows)], vp.at[(i + 1) * wide + y]))
            pairs_of.append((own.at[i * ty : (i + 1) * ty], line(i + 1)))
        for src, end, x in zip(lines, ends, (x_in, x_out)):
            pairs_of.append((src, line(x)))
            pairs_of.append((end.at[pl.ds(0, rows)], vp.at[x * wide + y_in]))
            pairs_of.append((end.at[pl.ds(rows, rows)], vp.at[x * wide + y_out]))
        copies = [pltpu.make_async_copy(src, dst, vsem.at[q]) for q, (src, dst) in enumerate(pairs_of)]
        for copy in copies:
            copy.start()
    wa[...] = jnp.zeros_like(wa)
    wb[...] = jnp.zeros_like(wb)
    total[...] = around[6][...] if halo else jnp.zeros_like(total)

    def where_is(t):
        return lax.div(ids[t], jnp.int32(ty)), lax.rem(ids[t], jnp.int32(ty))

    def prepare(t, carry):
        i, j = where_is(t)
        for m in range(nb):
            code = partner[m, i, j]
            a = lax.shift_right_logical(code * 11, 5)
            where_to[t * nb + m] = here(i + a - 1, j + code - 3 * a - 1)
            code_of[t * nb + m] = code
        return carry

    row8 = rows_iota(8, beads)
    row16 = rows_iota(16, beads)
    for c in range(9):
        a, b = c // 3 - 1, c % 3 - 1
        high_of[c] = jnp.where(row8 == 3, -0.5 * a, jnp.where(row8 == 4, -0.5 * b, 0.0))
        for q, val in enumerate((0.5 * a, 0.5 * b, -0.25 * (a * a + b * b))):
            norm_of[c, q] = jnp.full((8, beads), val, F32)
        extra_of[c] = jnp.where(row16 == 11, 1.0 * a, jnp.where(row16 == 12, 1.0 * b, 0.0)).astype(BF16)

    def make_u(s):
        both = jnp.concatenate([feat[2 * s], feat[2 * s + 1]], axis=1)
        u = jnp.dot(weight_u[...], both, preferred_element_type=F32).astype(BF16)
        for e in range(2):
            for k in range(chans):
                ub[e, :, k * beads : (k + 1) * beads] = u[
                    k * width_h : (k + 1) * width_h, e * beads : (e + 1) * beads]

    def scores(t, e, buf, zbuf, wz):
        i, j = where_is(t)
        lhs, feats = [], []
        mine = vp[here(i, j), beads : beads + EXTRA, :].astype(F32)
        up = mine[0:8]
        bx, by = (jnp.broadcast_to(up[c : c + 1], (8, beads)) for c in (0, 1))
        bn = jnp.broadcast_to(up[5:6] + up[6:7] + up[7:8], (8, beads))
        fixed = jnp.where(row8 < 3, 0.5 * up, jnp.where(row8 >= 5, 1.0, 0.0))
        for m in range(nb):
            there, code = where_to[t * nb + m], code_of[t * nb + m]
            lhs.append(vp[there, 0:beads, :])
            feats.append(vp[there, beads : beads + EXTRA, :])
            high = fixed + high_of[code]
            norm = bn + bx * norm_of[code, 0] + by * norm_of[code, 1] + norm_of[code, 2]
            n1 = norm.astype(BF16).astype(F32)
            rest = norm - n1
            n2 = rest.astype(BF16).astype(F32)
            low = jnp.where(row8 == 0, n1, jnp.where(row8 == 1, n2, jnp.where(row8 == 2, rest - n2, 0.0)))
            wz[m // 2, EXTRA * (m % 2) : EXTRA * (m % 2 + 1), (m % 2) * beads : (m % 2 + 1) * beads] = (
                jnp.concatenate([high, low], axis=0).astype(BF16))
        for h in range(nb // 2):
            left = jnp.concatenate([feats[2 * h], feats[2 * h + 1]], axis=0)
            zbuf[h] = lax.dot_general(left, wz[h], (((0,), (0,)), ((), ())), preferred_element_type=F32)
        buf[...] = jnp.dot(jnp.concatenate(lhs, axis=0), ub[e], preferred_element_type=F32)

    def couples(buf, zbuf, cbuf):
        step = 16
        for m in range(nb):
            for r in range(0, beads, step):
                z = zbuf[m // 2, r : r + step, (m % 2) * beads : (m % 2 + 1) * beads]
                env = jnp.maximum(1.0 + z, 0.0)
                total = None
                for k in range(chans):
                    part = jnp.exp2(z * (rate[k] * (CUT_SQUARE / math.log(2.0)))) * buf[
                        m * beads + r : m * beads + r + step, k * beads : (k + 1) * beads]
                    total = part if total is None else total + part
                cbuf[m * beads + r : m * beads + r + step, :] = ((env * env) * total).astype(BF16)

    def gather(t, cbuf):
        i, j = where_is(t)
        lhs = []
        for m in range(nb):
            lhs.append(vp[where_to[t * nb + m], beads : beads + EXTRA, :] + extra_of[code_of[t * nb + m]])
        out = jnp.dot(jnp.concatenate(lhs, axis=1), cbuf[...], preferred_element_type=F32)
        out = out * (1.0 / width_h)
        mine = vp[here(i, j), beads : beads + EXTRA, :].astype(F32)
        w = out[8:9]
        fx = mine[0:1] * w - out[0:1] - out[11:12]
        fy = mine[1:2] * w - out[1:2] - out[12:13]
        fz = mine[2:3] * w - out[2:3]
        lx, ly, lz = (lever[i, c, pl.ds(j, 1), :] for c in range(3))
        value = jnp.concatenate(
            [fx, fy, fz, ly * fz - lz * fy, lz * fx - lx * fz, lx * fy - ly * fx,
             jnp.zeros((2, beads), F32)], axis=0)
        term = jnp.concatenate(split_two(value), axis=0)
        if halo:
            terms[t] = term
        key = owner[i, pl.ds(j, 1), :] * slots + slot[i, pl.ds(j, 1), :]
        got = lax.dot_general(term, one_hot(key, slots, 4 * slots), (((1,), (1,)), ((), ())),
                              preferred_element_type=F32)
        return got[0:8] + got[8:16]

    lax.fori_loop(0, n, prepare, 0)
    for load in loads:
        load.wait()
    make_u(0)
    if halo:
        for copy in copies:
            copy.wait()
    scores(0, 0, sa, za, wa)

    def body(s, carry):
        before = jnp.maximum(2 * s - 1, 0)
        later = jnp.minimum(s + 1, n // 2 - 1)

        scores(2 * s + 1, 1, sb, zb, wb)
        old = gather(before, cb)
        couples(sa, za, ca)
        make_u(later)
        scores(2 * later, 0, sa, za, wa)
        new = gather(2 * s, ca)
        couples(sb, zb, cb)
        total[...] = total[...] + jnp.where(s == 0, 0.0, old) + new
        return carry

    lax.fori_loop(0, n // 2, body, 0)
    total[...] = total[...] + gather(n - 1, cb)
    if halo:
        turn = lambda d, high: 1 + jnp.where(high, d, -d)
        sums[1, 1] = total[...]
        for a, b in DIRS:
            keep = [t for t, (i, j) in enumerate(tiles)
                    if (a == 0 or i == (0 if a < 0 else tx - 1)) and (b == 0 or j == (0 if b < 0 else ty - 1))]
            left, right = [], []
            for t in keep:
                i, j = tiles[t]
                key = owner[i, j : j + 1, :] * slots + slot[i, j : j + 1, :]
                left.append(terms[t])
                right.append(one_hot(key, slots, (3 * a + b + 4) * slots))
            got = lax.dot_general(jnp.concatenate(left, axis=1), jnp.concatenate(right, axis=1),
                                  (((1,), (1,)), ((), ())), preferred_element_type=F32)
            sums[turn(b, high_y), turn(a, high_x)] = got[0:8] + got[8:16]


def pairs(strips, halo, args, own, around):
    tiles = [(i, j) for rows, cols in strips for i in rows for j in cols]
    partner, rate, features, weight_u, lever, slot, owner, slots = args
    tx, ty, f, beads = features.shape
    nb = partner.shape[0]
    chans = rate.shape[0]
    width_h = weight_u.shape[0] // chans
    rows = beads + EXTRA
    n = len(tiles)
    out = (3, 3, 8, slots) if halo else (8, slots)
    scratch = [
        pltpu.SMEM((n * nb,), jnp.int32),
        pltpu.SMEM((n * nb,), jnp.int32),
        pltpu.VMEM((n, f, beads), BF16),
        pltpu.VMEM((2, width_h, chans * beads), BF16),
        pltpu.VMEM((nb * beads, chans * beads), F32),
        pltpu.VMEM((nb * beads, chans * beads), F32),
        pltpu.VMEM((nb // 2, beads, 2 * beads), F32),
        pltpu.VMEM((nb // 2, beads, 2 * beads), F32),
        pltpu.VMEM((nb * beads, beads), BF16),
        pltpu.VMEM((nb * beads, beads), BF16),
        pltpu.VMEM((nb // 2, 2 * EXTRA, 2 * beads), BF16),
        pltpu.VMEM((nb // 2, 2 * EXTRA, 2 * beads), BF16),
        pltpu.VMEM((9, 8, beads), F32),
        pltpu.VMEM((9, 3, 8, beads), F32),
        pltpu.VMEM((9, 16, beads), BF16),
        pltpu.SemaphoreType.DMA((len(strips),)),
    ]
    if halo:
        scratch += [pltpu.VMEM((n, 16, beads), BF16), pltpu.VMEM(((tx + 2) * (ty + 2), rows, beads), BF16),
                    pltpu.SemaphoreType.DMA((3 * tx + 6,)), pltpu.VMEM((8, slots), F32)]
    ids = jnp.asarray([i * ty + j for i, j in tiles], jnp.int32)
    shape = (tx, ty, beads, width_h, chans, nb, slots)
    return pl.pallas_call(
        lambda *refs: pairs_kernel(strips, halo, shape, *refs),
        out_shape=jax.ShapeDtypeStruct(out, F32),
        in_specs=[SMEM, SMEM, SMEM, HBM, VMEM, VMEM, VMEM, VMEM, HBM if halo else VMEM]
        + ([HBM] * 6 + [VMEM] if halo else []),
        out_specs=VMEM,
        scratch_shapes=scratch,
        compiler_params=pltpu.CompilerParams(vmem_limit_bytes=LIMIT),
        cost_estimate=pl.CostEstimate(flops=n * 150_000_000, bytes_accessed=n * 100_000, transcendentals=0),
    )(ids, partner, rate, features, weight_u, lever, slot, owner, own.reshape((tx * ty, rows, beads)), *(around if halo else []))


def rotation_rows(q):
    w, a, b, c = q
    return [
        [1 - 2 * (b * b + c * c), 2 * (a * b - w * c), 2 * (a * c + w * b)],
        [2 * (a * b + w * c), 1 - 2 * (a * a + c * c), 2 * (b * c - w * a)],
        [2 * (a * c - w * b), 2 * (b * c + w * a), 1 - 2 * (a * a + b * b)],
    ]


def integrate(q, motion, inverse, f):
    vel = [motion[r] + STEP_DT * inverse[0] * f[r] for r in range(3)]
    ang = [motion[3 + r] + STEP_DT * f[3 + r] for r in range(3)]
    old = rotation_rows(q)
    frame = [sum(old[r][c] * ang[r] for r in range(3)) * inverse[1 + c] for c in range(3)]
    om = [sum(old[r][c] * frame[c] for c in range(3)) for r in range(3)]
    w, x, y, z = q
    rate = [
        -(om[0] * x + om[1] * y + om[2] * z),
        w * om[0] + om[1] * z - om[2] * y,
        w * om[1] + om[2] * x - om[0] * z,
        w * om[2] + om[0] * y - om[1] * x,
    ]
    step = [q[r] + 0.5 * STEP_DT * rate[r] for r in range(4)]
    size = jnp.sqrt(sum(s * s for s in step))
    new = [s / size for s in step]
    turned = rotation_rows(new)
    rel = [sum(turned[r][k] * old[c][k] for k in range(3)) for r in range(3) for c in range(3)]
    return new, vel, ang, [STEP_DT * v for v in vel] + rel


def finish_kernel(totals, pose, motion, inverse, col_a, col_b, end_a, end_b, pos, lever, slot, owner,
                  moved, state, table):
    tx, ty = pos.shape[0], pos.shape[2]
    slots = totals.shape[3]
    high_x, high_y = outward("gx"), outward("gy")
    turn = lambda d, high: 1 + jnp.where(high, d, -d)
    rows_a, rows_b = end_a.shape[0] - 3 * BODY, col_a.shape[0] - BODY
    bodies = {(1, 0): (col_a, rows_b), (1, 2): (col_b, rows_b)}
    for a, end in ((0, end_a), (2, end_b)):
        for q, b in enumerate((1, 0, 2)):
            bodies[a, b] = (end, rows_a + q * BODY)
    for a in range(3):
        for b in range(3):
            f = totals[b, a]
            f = [f[r : r + 1] for r in range(6)]
            if (a, b) == (1, 1):
                q = [pose[0, 3 + r] for r in range(4)]
                mot = [motion[0, r] for r in range(6)]
                inv = [inverse[0, 0, r : r + 1, :] for r in range(4)]
            else:
                ref, at = bodies[a, b]
                third = BODY // 3
                body = sum(ref[at + k * third : at + (k + 1) * third, :].astype(F32) for k in range(3))
                body = [body[r : r + 1] for r in range(14)]
                q, mot, inv = body[0:4], body[4:10], body[10:14]
            new, vel, ang, packed = integrate(q, mot, inv, f)
            if (a, b) == (1, 1):
                centre = [pose[0, r] + STEP_DT * vel[r] for r in range(3)]
                for r, val in enumerate(centre + new + vel + ang):
                    state[0, r] = val
            packed = jnp.concatenate(packed + [jnp.zeros((4, slots), F32)], axis=0)
            table[a, b] = jnp.concatenate(split_two(packed), axis=0)

    def place(i, j, a, b):
        key = owner[i, pl.ds(j, 1), :] * slots + slot[i, pl.ds(j, 1), :]
        rows = table[1, 1] if a == 0 and b == 0 else table[turn(a, high_x), turn(b, high_y)]
        got = jnp.dot(rows, one_hot(key, slots, (3 * a + b + 4) * slots), preferred_element_type=F32)
        got = got[0:16] + got[16:32]
        lev = [lever[i, c, pl.ds(j, 1), :] for c in range(3)]
        return [got[r : r + 1] + sum(got[3 + 3 * r + c : 4 + 3 * r + c] * lev[c] for c in range(3)) for r in range(3)]

    def line(i, carry):
        for j in range(ty):
            for r, val in enumerate(place(i, j, 0, 0)):
                moved[i, r, j : j + 1, :] = pos[i, r, j : j + 1, :].astype(F32) + val - lever[i, r, j : j + 1, :]
        return carry

    lax.fori_loop(0, tx, line, 0)
    for a, b in DIRS:
        for i in range(tx) if a == 0 else [0 if a < 0 else tx - 1]:
            for j in range(ty) if b == 0 else [0 if b < 0 else ty - 1]:
                for r, val in enumerate(place(i, j, a, b)):
                    moved[i, r, j : j + 1, :] = moved[i, r, j : j + 1, :] + val


def finish(totals, pose, motion, inverse, cols, ends, pos, lever, slot, owner):
    slots = totals.shape[3]
    return pl.pallas_call(
        finish_kernel,
        out_shape=[jax.ShapeDtypeStruct(lever.shape, F32), jax.ShapeDtypeStruct((1, 13, 1, slots), F32)],
        in_specs=[VMEM] * 12,
        out_specs=[VMEM] * 2,
        scratch_shapes=[pltpu.VMEM((3, 3, 32, slots), BF16)],
        compiler_params=pltpu.CompilerParams(vmem_limit_bytes=LIMIT),
    )(totals, pose, motion, inverse, *cols, *ends, pos, lever, slot, owner)


def swap(value, axis, start):
    n = lax.axis_size(axis)
    route = []
    for c in range(start, n + start, 2):
        route += [(c % n, (c + 1) % n), ((c + 1) % n, c % n)]
    return lax.ppermute(value, axis, route)


def inside(value, axis):
    return swap(value, axis, 0)


def outside(value, axis):
    return swap(value, axis, 1)


def local(positions, features, lever, partner, body_slot, owner_dir, body_pose, body_motion,
          body_inverse, weight_u, weight_v, radial_rate):
    tx, ty = positions.shape[0], positions.shape[1]
    slots = body_pose.shape[3]
    rows = positions.shape[3] + EXTRA
    pos, lever = (jnp.transpose(v, (0, 2, 1, 3)) for v in (positions, lever))
    pose, motion = (jnp.transpose(v, (0, 2, 1, 3)) for v in (body_pose, body_motion))
    codes = jnp.transpose(partner, (2, 0, 1))
    own, col_in, col_out, row_in, row_out = project(features, pos, weight_v, pose, motion, body_inverse)
    line_a, line_b = inside(row_in, "gx"), outside(row_out, "gx")
    col_a, col_b = inside(col_in, "gy"), outside(col_out, "gy")
    high_x = outward("gx")
    bodies = [v[tx * rows :] for v in (col_in, col_a, col_b)]
    corner = lambda high: jnp.concatenate(
        [jnp.where(high, v[(tx - 1) * rows : tx * rows], v[:rows]) for v in (col_a, col_b)] + bodies, axis=0)
    end_a, end_b = inside(corner(~high_x), "gx"), outside(corner(high_x), "gx")
    args = (codes, radial_rate, features, weight_u, lever, body_slot, owner_dir, slots)
    inner = [((i,), range(1, ty - 1)) for i in range(1, tx - 1)]
    rim = [((0,), range(ty)), ((tx - 1,), range(ty)), (range(1, tx - 1), (0,)), (range(1, tx - 1), (ty - 1,))]
    first = pairs(inner, False, args, own, None)
    parts = pairs(rim, True, args, own, [col_a, col_b, line_a, line_b, end_a, end_b, first])
    mine = parts[1] + inside(parts[0], "gy")
    got = outside(jnp.stack([parts[2], mine]), "gy")
    mine = mine + got[0]
    cols = jnp.stack([inside(mine, "gy"), mine, got[1] + parts[2]])
    if lax.axis_size("gx") == 4:
        other = inside(cols, "gx")
        mine = cols[:, 1] + other[:, 0]
        got = outside(jnp.stack([cols[:, 2], mine, other[:, 2]]), "gx")
        mine = mine + got[0]
        beside = other[:, 1] + cols[:, 0] + got[2]
    else:
        mine = cols[:, 1] + inside(cols[:, 0], "gx")
        got = outside(jnp.stack([cols[:, 2], mine]), "gx")
        mine = mine + got[0]
        beside = inside(mine, "gx")
    totals = jnp.stack([beside, mine, got[1] + cols[:, 2]], axis=1)
    moved, state = finish(totals, pose, motion, body_inverse, (col_a, col_b), (end_a, end_b),
                          pos, lever, body_slot, owner_dir)
    return (jnp.transpose(moved, (0, 2, 1, 3)), jnp.transpose(state, (0, 2, 1, 3)))


def solution(mesh):
    placed = (
        P("gx", "gy", None, None),
        P("gx", "gy", None, None),
        P("gx", "gy", None, None),
        P("gx", "gy", None),
        P("gx", "gy", None),
        P("gx", "gy", None),
        P("gx", "gy", None, None),
        P("gx", "gy", None, None),
        P("gx", "gy", None, None),
        P(),
        P(),
        P(),
    )
    return jax.shard_map(
        local,
        mesh=mesh,
        in_specs=placed,
        out_specs=(P("gx", "gy", None, None), P("gx", "gy", None, None)),
        check_vma=False,
    )
```

```python
import math
import jax
import jax.numpy as jnp
from jax import lax
from jax.experimental import pallas as pl
from jax.experimental.pallas import tpu as pltpu
from jax.sharding import PartitionSpec as P

STEP_DT = 0.25
CUT_SQUARE = 4.0
F32 = jnp.float32
BF16 = jnp.bfloat16
VMEM = pl.BlockSpec(memory_space=pltpu.VMEM)
SMEM = pl.BlockSpec(memory_space=pltpu.SMEM)
HBM = pl.BlockSpec(memory_space=pl.ANY)
LIMIT = 24 * 2**20
DIRS = [(-1, -1), (-1, 0), (-1, 1), (0, -1), (0, 1), (1, -1), (1, 0), (1, 1)]
EXTRA = 16
BODY = 48
UNROLL = 4
STEP = 4


def rows_iota(rows, lanes):
    return lax.broadcasted_iota(jnp.int32, (rows, lanes), 0)


def split_two(value):
    high = value.astype(BF16)
    return high, (value - high.astype(F32)).astype(BF16)


def one_hot(keys, slots, base):
    hit = rows_iota(slots, keys.shape[-1]) == keys - base
    return jnp.where(hit, 1.0, 0.0).astype(BF16)


def outward(axis):
    return lax.rem(lax.axis_index(axis), 2) == 1


def split_three(value):
    first = value.astype(BF16)
    rest = value - first.astype(F32)
    second = rest.astype(BF16)
    return first, second, (rest - second.astype(F32)).astype(BF16)


def project_kernel(feat, pos, weight_v, pose, motion, inverse, own, col_in, col_out, row_in, row_out):
    x = pl.program_id(0)
    tiles_x, tiles_y, beads = pl.num_programs(0), feat.shape[1], feat.shape[3]
    rows = beads + EXTRA
    step = feat.shape[0]
    second = jnp.where(rows_iota(8, beads) < 3, 1.0, 0.0)
    high_x, high_y = outward("gx"), outward("gy")
    for z in range(step):
        for y in range(0, tiles_y, 2):
            both = jnp.concatenate([feat[z, y], feat[z, y + 1]], axis=1)
            v = jnp.dot(weight_v[...], both, preferred_element_type=F32).astype(BF16)
            for e in range(2):
                own[z, y + e, 0:beads, :] = v[:, e * beads : (e + 1) * beads].T
        px, py, pz = (pos[z, c].astype(F32) for c in range(3))
        norm = -0.25 * (px * px + py * py + pz * pz)
        none = jnp.zeros_like(px)
        parts = [px, py, pz, none, none] + [part.astype(F32) for part in split_three(norm)]
        for y in range(tiles_y):
            first = jnp.concatenate([part[y : y + 1] for part in parts], axis=0)
            own[z, y, beads:rows, :] = jnp.concatenate([first, second], axis=0).astype(BF16)
        at = pl.ds(pl.multiple_of((x * step + z) * rows, 16), rows)
        low, high = own[z, 0], own[z, tiles_y - 1]
        col_in[at, :] = jnp.where(high_y, low, high)
        col_out[at, :] = jnp.where(high_y, high, low)

    @pl.when(x == 0)
    def _():
        @pl.when(high_x)
        def _():
            row_in[...] = own[0]

        @pl.when(~high_x)
        def _():
            row_out[...] = own[0]

    @pl.when(x == tiles_x - 1)
    def _():
        @pl.when(high_x)
        def _():
            row_out[...] = own[step - 1]

        @pl.when(~high_x)
        def _():
            row_in[...] = own[step - 1]

    @pl.when(x == 0)
    def _():
        body = jnp.concatenate(
            [pose[0, r] for r in range(3, 7)] + [motion[0, r] for r in range(6)]
            + [inverse[0, 0, r : r + 1, :] for r in range(4)] + [jnp.zeros((2, beads), F32)], axis=0)
        body = jnp.concatenate(split_three(body), axis=0)
        end = col_in.shape[0] - BODY
        col_in[end:, :] = body
        col_out[end:, :] = body


def project(features, pos, weight_v, pose, motion, inverse):
    tx, ty, f, beads = features.shape
    rows = beads + EXTRA
    whole = lambda s: pl.BlockSpec(s, lambda i: (0,) * len(s))
    sds = lambda *s: jax.ShapeDtypeStruct(s, BF16)
    col = (tx * rows + BODY, beads)
    return pl.pallas_call(
        project_kernel,
        grid=(tx // STEP,),
        out_shape=[sds(tx, ty, rows, beads), sds(*col), sds(*col), sds(ty, rows, beads), sds(ty, rows, beads)],
        in_specs=[
            pl.BlockSpec((STEP, ty, f, beads), lambda i: (i, 0, 0, 0)),
            pl.BlockSpec((STEP, 3, ty, beads), lambda i: (i, 0, 0, 0)),
            whole(weight_v.shape), whole(pose.shape), whole(motion.shape), whole(inverse.shape),
        ],
        out_specs=[
            pl.BlockSpec((STEP, ty, rows, beads), lambda i: (i, 0, 0, 0)),
            whole(col), whole(col), whole((ty, rows, beads)), whole((ty, rows, beads)),
        ],
        compiler_params=pltpu.CompilerParams(vmem_limit_bytes=LIMIT),
    )(features, pos, weight_v, pose, motion, inverse)


def pairs_kernel(strips, halo, shape, *refs):
    tiles = [(i, j) for rows, cols in strips for i in rows for j in cols]
    n = len(tiles)
    tx, ty, beads, width_h, chans, nb, slots = shape
    refs = list(refs)
    take = lambda k: [refs.pop(0) for _ in range(k)]
    ids, partner, rate, features, weight_u, lever, slot, owner, own = take(9)
    around = take(7) if halo else []
    sums = take(3 if halo else 1)
    where_to, code_of = take(2)
    feat, shift_of, norm_of, terms, fsem = take(5)
    sets = [take(7), take(7)]
    vp, vsem, total, parts = take(4) if halo else (own, None, sums[0], None)
    wide = ty + 2
    here = lambda i, j: (i + 1) * wide + j + 1 if halo else i * ty + j
    side = chans * width_h

    at = 0
    loads = []
    for q, (i, j) in enumerate(strips):
        size = max(len(i), len(j))
        src = features.at[i[0], j[0] : j[-1] + 1] if len(i) == 1 else features.at[i[0] : i[-1] + 1, j[0]]
        loads.append(pltpu.make_async_copy(src, feat.at[at : at + size], fsem.at[q]))
        loads[-1].start()
        at += size
    if halo:
        rows = beads + EXTRA
        high_x, high_y = outward("gx"), outward("gy")
        x_in, x_out = jnp.where(high_x, 0, tx + 1), jnp.where(high_x, tx + 1, 0)
        y_in, y_out = jnp.where(high_y, 0, ty + 1), jnp.where(high_y, ty + 1, 0)
        line = lambda i: vp.at[pl.ds(i * wide + 1, ty)]
        cols, lines, ends = around[0:2], around[2:4], around[4:6]
        pairs_of = []
        for i in range(tx):
            for col, y in zip(cols, (y_in, y_out)):
                pairs_of.append((col.at[pl.ds(i * rows, rows)], vp.at[(i + 1) * wide + y]))
            pairs_of.append((own.at[i * ty : (i + 1) * ty], line(i + 1)))
        for src, end, x in zip(lines, ends, (x_in, x_out)):
            pairs_of.append((src, line(x)))
            pairs_of.append((end.at[pl.ds(0, rows)], vp.at[x * wide + y_in]))
            pairs_of.append((end.at[pl.ds(rows, rows)], vp.at[x * wide + y_out]))
        copies = [pltpu.make_async_copy(src, dst, vsem.at[q]) for q, (src, dst) in enumerate(pairs_of)]
        for copy in copies:
            copy.start()
    total[...] = around[6][...] if halo else jnp.zeros_like(total)

    def where_is(t):
        return lax.div(ids[t], jnp.int32(ty)), lax.rem(ids[t], jnp.int32(ty))

    def prepare(t, carry):
        i, j = where_is(t)
        for m in range(nb):
            code = partner[m, i, j]
            a = lax.shift_right_logical(code * 11, 5)
            where_to[t * nb + m] = here(i + a - 1, j + code - 3 * a - 1)
            code_of[t * nb + m] = code
        return carry

    row8 = rows_iota(8, beads)
    row16 = rows_iota(EXTRA, beads)
    for c in range(9):
        a, b = c // 3 - 1, c % 3 - 1
        shift_of[c] = jnp.where(row16 == 3, 1.0 * a, jnp.where(row16 == 4, 1.0 * b, 0.0)).astype(BF16)
        for q, val in enumerate((-0.5 * a, -0.5 * b, -0.25 * (a * a + b * b))):
            norm_of[c, q] = jnp.full((8, beads), val, F32)

    def make_u(s, ub):
        both = jnp.concatenate([feat[2 * s], feat[2 * s + 1]], axis=1)
        u = jnp.dot(weight_u[...], both, preferred_element_type=F32).astype(BF16)
        for e in range(2):
            for k in range(chans):
                ub[e, :, k * beads : (k + 1) * beads] = u[
                    k * width_h : (k + 1) * width_h, e * beads : (e + 1) * beads]

    def moved_block(t, m):
        return vp[where_to[t * nb + m], beads : beads + EXTRA, :] + shift_of[code_of[t * nb + m]]

    def products(t, ub, e, buf, g):
        cols = slice(2 * g * beads, 2 * (g + 1) * beads)
        lhs = jnp.concatenate([vp[where_to[t * nb + m], 0:beads, :] for m in range(nb)], axis=0)
        buf[:, cols] = jnp.dot(lhs, ub[e, :, cols], preferred_element_type=F32)

    def scores(t, ub, e, buf, zbuf):
        i, j = where_is(t)
        up = vp[here(i, j), beads : beads + EXTRA, :].astype(F32)[0:8]
        px, py = (jnp.broadcast_to(0.5 * up[c : c + 1], (8, beads)) for c in (0, 1))
        high = jnp.where(row8 < 3, 0.5 * up, jnp.where(row8 == 3, px, jnp.where(row8 == 4, py, 1.0)))
        low = jnp.where(row8 < 3, pltpu.roll(up, 3, 0), 0.0)
        mine = jnp.concatenate([high, low], axis=0).astype(BF16)
        none = jnp.zeros_like(mine)
        mine = jnp.concatenate([jnp.concatenate([mine, none], axis=1), jnp.concatenate([none, mine], axis=1)], axis=0)
        feats = []
        for m in range(nb):
            code = code_of[t * nb + m]
            block = moved_block(t, m).astype(F32)
            up = block[0:8]
            qx, qy = (jnp.broadcast_to(up[c : c + 1], (8, beads)) for c in (0, 1))
            norm = jnp.broadcast_to(up[5:6] + up[6:7] + up[7:8], (8, beads)) + norm_of[code, 2]
            norm = norm + qx * norm_of[code, 0] + qy * norm_of[code, 1]
            n1 = norm.astype(BF16).astype(F32)
            rest = norm - n1
            n2 = rest.astype(BF16).astype(F32)
            high = jnp.where(row8 < 5, up, jnp.where(row8 == 5, n1, jnp.where(row8 == 6, n2, rest - n2)))
            feats.append(jnp.concatenate([high, block[8:16]], axis=0).astype(BF16))
        left = jnp.concatenate([jnp.concatenate(feats[h::2], axis=1) for h in range(2)], axis=0)
        zbuf[...] = lax.dot_general(left, mine, (((0,), (0,)), ((), ())), preferred_element_type=F32)

    def couples(buf, zbuf, cbuf, which):
        step = 16
        for m in which:
            for r in range(0, beads, step):
                z = zbuf[m // 2 * beads + r : m // 2 * beads + r + step, (m % 2) * beads : (m % 2 + 1) * beads]
                env = jnp.maximum(1.0 + z, 0.0)
                total = None
                for k in range(chans):
                    part = jnp.exp2(z * (rate[k] * (CUT_SQUARE / math.log(2.0)))) * buf[
                        m * beads + r : m * beads + r + step, k * beads : (k + 1) * beads]
                    total = part if total is None else total + part
                cbuf[m * beads + r : m * beads + r + step, :] = ((env * env) * total).astype(BF16)

    def gather(t, cbuf):
        i, j = where_is(t)
        lhs = jnp.concatenate([moved_block(t, m) for m in range(nb)], axis=1)
        out = jnp.dot(lhs, cbuf[...], preferred_element_type=F32) * (1.0 / width_h)
        mine = vp[here(i, j), beads : beads + EXTRA, :].astype(F32)
        w = out[8:9]
        fx = mine[0:1] * w - out[0:1] - out[3:4]
        fy = mine[1:2] * w - out[1:2] - out[4:5]
        fz = mine[2:3] * w - out[2:3]
        lx, ly, lz = (lever[i, c, pl.ds(j, 1), :] for c in range(3))
        value = jnp.concatenate(
            [fx, fy, fz, ly * fz - lz * fy, lz * fx - lx * fz, lx * fy - ly * fx,
             jnp.zeros((2, beads), F32)], axis=0)
        term = jnp.concatenate(split_two(value), axis=0)
        terms[t] = term

    def add_up(s):
        left, right = [], []
        for t in (2 * s, 2 * s + 1):
            i, j = where_is(t)
            key = owner[i, pl.ds(j, 1), :] * slots + slot[i, pl.ds(j, 1), :]
            left.append(terms[t])
            right.append(one_hot(key, slots, 4 * slots))
        got = lax.dot_general(jnp.concatenate(left, axis=1), jnp.concatenate(right, axis=1),
                              (((1,), (1,)), ((), ())), preferred_element_type=F32)
        return got[0:8] + got[8:16]

    lax.fori_loop(0, n, prepare, 0)
    for load in loads:
        load.wait()
    last = n // 2 - 1

    def fill(s, into):
        ub, sa, sb, za, zb, _, _ = into
        scores(2 * s, ub, 0, sa, za)
        scores(2 * s + 1, ub, 1, sb, zb)
        for g in range(chans // 2):
            products(2 * s, ub, 0, sa, g)
            products(2 * s + 1, ub, 1, sb, g)

    def half(s, now, later):
        _, sa, sb, za, zb, ca, cb = now
        before = jnp.maximum(s - 1, 0)
        nxt = jnp.minimum(s + 1, last)
        scores(2 * nxt + 0, later[0], 0, later[1], later[3])
        products(2 * nxt + 0, later[0], 0, later[1], 0)
        couples(sa, za, ca, range(0, 3))
        products(2 * nxt + 0, later[0], 0, later[1], 1)
        couples(sa, za, ca, range(3, 6))
        scores(2 * nxt + 1, later[0], 1, later[2], later[4])
        products(2 * nxt + 1, later[0], 1, later[2], 0)
        couples(sb, zb, cb, range(0, 3))
        products(2 * nxt + 1, later[0], 1, later[2], 1)
        couples(sb, zb, cb, range(3, 6))
        make_u(jnp.minimum(s + 2, last), now[0])
        gather(2 * before, later[5])
        gather(2 * before + 1, later[6])
        total[...] = total[...] + jnp.where(s == 0, 0.0, add_up(before))

    make_u(0, sets[0][0])
    make_u(min(1, last), sets[1][0])
    if halo:
        for copy in copies:
            copy.wait()
    fill(0, sets[0])

    def body(g, carry):
        half(2 * g, sets[0], sets[1])
        half(2 * g + 1, sets[1], sets[0])
        return carry

    lax.fori_loop(0, n // 4, body, 0)
    gather(n - 2, sets[1][5])
    gather(n - 1, sets[1][6])
    total[...] = total[...] + add_up(last)
    if halo:
        turn = lambda d, high: 1 + jnp.where(high, d, -d)
        parts[1, 1] = total[...]
        for a, b in DIRS:
            keep = [t for t, (i, j) in enumerate(tiles)
                    if (a == 0 or i == (0 if a < 0 else tx - 1)) and (b == 0 or j == (0 if b < 0 else ty - 1))]
            left, right = [], []
            for t in keep:
                i, j = tiles[t]
                key = owner[i, j : j + 1, :] * slots + slot[i, j : j + 1, :]
                left.append(terms[t])
                right.append(one_hot(key, slots, (3 * a + b + 4) * slots))
            got = lax.dot_general(jnp.concatenate(left, axis=1), jnp.concatenate(right, axis=1),
                                  (((1,), (1,)), ((), ())), preferred_element_type=F32)
            parts[turn(b, high_y), turn(a, high_x)] = got[0:8] + got[8:16]
        for q in range(3):
            sums[q][...] = parts[q]


def pairs(strips, halo, args, own, around):
    tiles = [(i, j) for rows, cols in strips for i in rows for j in cols]
    partner, rate, features, weight_u, lever, slot, owner, slots = args
    tx, ty, f, beads = features.shape
    nb = partner.shape[0]
    chans = rate.shape[0]
    width_h = weight_u.shape[0] // chans
    rows = beads + EXTRA
    n = len(tiles)
    out = jax.ShapeDtypeStruct((3, 8, slots) if halo else (8, slots), F32)
    scratch = [
        pltpu.SMEM((n * nb,), jnp.int32),
        pltpu.SMEM((n * nb,), jnp.int32),
        pltpu.VMEM((n, f, beads), BF16),
        pltpu.VMEM((9, EXTRA, beads), BF16),
        pltpu.VMEM((9, 3, 8, beads), F32),
        pltpu.VMEM((n, 16, beads), BF16),
        pltpu.SemaphoreType.DMA((len(strips),)),
    ]
    scratch += 2 * [
        pltpu.VMEM((2, width_h, chans * beads), BF16),
        pltpu.VMEM((nb * beads, chans * beads), F32),
        pltpu.VMEM((nb * beads, chans * beads), F32),
        pltpu.VMEM((nb // 2 * beads, 2 * beads), F32),
        pltpu.VMEM((nb // 2 * beads, 2 * beads), F32),
        pltpu.VMEM((nb * beads, beads), BF16),
        pltpu.VMEM((nb * beads, beads), BF16),
    ]
    if halo:
        scratch += [pltpu.VMEM(((tx + 2) * (ty + 2), rows, beads), BF16),
                    pltpu.SemaphoreType.DMA((3 * tx + 6,)), pltpu.VMEM((8, slots), F32),
                    pltpu.VMEM((3, 3, 8, slots), F32)]
    ids = jnp.asarray([i * ty + j for i, j in tiles], jnp.int32)
    shape = (tx, ty, beads, width_h, chans, nb, slots)
    return pl.pallas_call(
        lambda *refs: pairs_kernel(strips, halo, shape, *refs),
        out_shape=[out] * (3 if halo else 1),
        in_specs=[SMEM, SMEM, SMEM, HBM, VMEM, VMEM, VMEM, VMEM, HBM if halo else VMEM]
        + ([HBM] * 6 + [VMEM] if halo else []),
        out_specs=[VMEM] * (3 if halo else 1),
        scratch_shapes=scratch,
        compiler_params=pltpu.CompilerParams(vmem_limit_bytes=LIMIT),
        cost_estimate=pl.CostEstimate(flops=n * 150_000_000, bytes_accessed=n * 100_000, transcendentals=0),
    )(ids, partner, rate, features, weight_u, lever, slot, owner, own.reshape((tx * ty, rows, beads)), *(around if halo else []))


def rotation_rows(q):
    w, a, b, c = q
    return [
        [1 - 2 * (b * b + c * c), 2 * (a * b - w * c), 2 * (a * c + w * b)],
        [2 * (a * b + w * c), 1 - 2 * (a * a + c * c), 2 * (b * c - w * a)],
        [2 * (a * c - w * b), 2 * (b * c + w * a), 1 - 2 * (a * a + b * b)],
    ]


def integrate(q, motion, inverse, f):
    vel = [motion[r] + STEP_DT * inverse[0] * f[r] for r in range(3)]
    ang = [motion[3 + r] + STEP_DT * f[3 + r] for r in range(3)]
    old = rotation_rows(q)
    frame = [sum(old[r][c] * ang[r] for r in range(3)) * inverse[1 + c] for c in range(3)]
    om = [sum(old[r][c] * frame[c] for c in range(3)) for r in range(3)]
    w, x, y, z = q
    rate = [
        -(om[0] * x + om[1] * y + om[2] * z),
        w * om[0] + om[1] * z - om[2] * y,
        w * om[1] + om[2] * x - om[0] * z,
        w * om[2] + om[0] * y - om[1] * x,
    ]
    step = [q[r] + 0.5 * STEP_DT * rate[r] for r in range(4)]
    size = jnp.sqrt(sum(s * s for s in step))
    new = [s / size for s in step]
    turned = rotation_rows(new)
    rel = [sum(turned[r][k] * old[c][k] for k in range(3)) for r in range(3) for c in range(3)]
    return new, vel, ang, [STEP_DT * v for v in vel] + rel


def finish_kernel(count, *refs):
    sums, refs = refs[:count], refs[count:]
    finish_body(sums, *refs)


def finish_body(sums, pose, motion, inverse, col_a, col_b, end_a, end_b, pos, lever, slot, owner,
                  moved, state, table):
    tx, ty = pos.shape[0], pos.shape[2]
    slots = owner.shape[2]
    high_x, high_y = outward("gx"), outward("gy")
    turn = lambda d, high: 1 + jnp.where(high, d, -d)
    rows_a, rows_b = end_a.shape[0] - 3 * BODY, col_a.shape[0] - BODY
    bodies = {(1, 0): (col_a, rows_b), (1, 2): (col_b, rows_b)}
    for a, end in ((0, end_a), (2, end_b)):
        for q, b in enumerate((1, 0, 2)):
            bodies[a, b] = (end, rows_a + q * BODY)
    if len(sums) == 1:
        totals = lambda b, a: sums[0][a, b]
    else:
        cols, other, got = sums
        totals = lambda b, a: (other[1, b] + cols[0, b] + got[2, b], cols[1, b] + other[0, b] + got[0, b],
                               got[1, b] + cols[2, b])[a]
    for a in range(3):
        for b in range(3):
            f = totals(b, a)
            f = [f[r : r + 1] for r in range(6)]
            if (a, b) == (1, 1):
                q = [pose[0, 3 + r] for r in range(4)]
                mot = [motion[0, r] for r in range(6)]
                inv = [inverse[0, 0, r : r + 1, :] for r in range(4)]
            else:
                ref, at = bodies[a, b]
                third = BODY // 3
                body = sum(ref[at + k * third : at + (k + 1) * third, :].astype(F32) for k in range(3))
                body = [body[r : r + 1] for r in range(14)]
                q, mot, inv = body[0:4], body[4:10], body[10:14]
            new, vel, ang, packed = integrate(q, mot, inv, f)
            if (a, b) == (1, 1):
                centre = [pose[0, r] + STEP_DT * vel[r] for r in range(3)]
                for r, val in enumerate(centre + new + vel + ang):
                    state[0, r] = val
            packed = jnp.concatenate(packed + [jnp.zeros((4, slots), F32)], axis=0)
            table[a, b] = jnp.concatenate(split_two(packed), axis=0)

    def place(i, j, a, b):
        key = owner[i, pl.ds(j, 1), :] * slots + slot[i, pl.ds(j, 1), :]
        rows = table[1, 1] if a == 0 and b == 0 else table[turn(a, high_x), turn(b, high_y)]
        got = jnp.dot(rows, one_hot(key, slots, (3 * a + b + 4) * slots), preferred_element_type=F32)
        got = got[0:16] + got[16:32]
        lev = [lever[i, c, pl.ds(j, 1), :] for c in range(3)]
        return [got[r : r + 1] + sum(got[3 + 3 * r + c : 4 + 3 * r + c] * lev[c] for c in range(3)) for r in range(3)]

    def line(i, carry):
        for j in range(ty):
            for r, val in enumerate(place(i, j, 0, 0)):
                moved[i, r, j : j + 1, :] = pos[i, r, j : j + 1, :].astype(F32) + val - lever[i, r, j : j + 1, :]
        return carry

    lax.fori_loop(0, tx, line, 0, unroll=UNROLL)
    for a, b in DIRS:
        for i in range(tx) if a == 0 else [0 if a < 0 else tx - 1]:
            for j in range(ty) if b == 0 else [0 if b < 0 else ty - 1]:
                for r, val in enumerate(place(i, j, a, b)):
                    moved[i, r, j : j + 1, :] = moved[i, r, j : j + 1, :] + val


def finish(sums, pose, motion, inverse, cols, ends, pos, lever, slot, owner):
    slots = pose.shape[3]
    return pl.pallas_call(
        lambda *refs: finish_kernel(len(sums), *refs),
        out_shape=[jax.ShapeDtypeStruct(lever.shape, F32), jax.ShapeDtypeStruct((1, 13, 1, slots), F32)],
        in_specs=[VMEM] * (11 + len(sums)),
        out_specs=[VMEM] * 2,
        scratch_shapes=[pltpu.VMEM((3, 3, 32, slots), BF16)],
        compiler_params=pltpu.CompilerParams(vmem_limit_bytes=LIMIT),
    )(*sums, pose, motion, inverse, *cols, *ends, pos, lever, slot, owner)


def swap(value, axis, start):
    n = lax.axis_size(axis)
    route = []
    for c in range(start, n + start, 2):
        route += [(c % n, (c + 1) % n), ((c + 1) % n, c % n)]
    return lax.ppermute(value, axis, route)


def inside(value, axis):
    return swap(value, axis, 0)


def outside(value, axis):
    return swap(value, axis, 1)


def local(positions, features, lever, partner, body_slot, owner_dir, body_pose, body_motion,
          body_inverse, weight_u, weight_v, radial_rate):
    tx, ty = positions.shape[0], positions.shape[1]
    slots = body_pose.shape[3]
    rows = positions.shape[3] + EXTRA
    pos, lever = (jnp.transpose(v, (0, 2, 1, 3)) for v in (positions, lever))
    pose, motion = (jnp.transpose(v, (0, 2, 1, 3)) for v in (body_pose, body_motion))
    codes = jnp.transpose(partner, (2, 0, 1))
    own, col_in, col_out, row_in, row_out = project(features, pos, weight_v, pose, motion, body_inverse)
    line_a, line_b = inside(row_in, "gx"), outside(row_out, "gx")
    col_a, col_b = inside(col_in, "gy"), outside(col_out, "gy")
    high_x = outward("gx")
    bodies = [v[tx * rows :] for v in (col_in, col_a, col_b)]
    corner = lambda high: jnp.concatenate(
        [jnp.where(high, v[(tx - 1) * rows : tx * rows], v[:rows]) for v in (col_a, col_b)] + bodies, axis=0)
    end_a, end_b = inside(corner(~high_x), "gx"), outside(corner(high_x), "gx")
    args = (codes, radial_rate, features, weight_u, lever, body_slot, owner_dir, slots)
    inner = [((i,), range(1, ty - 1)) for i in range(1, tx - 1)]
    rim = [((0,), range(ty)), ((tx - 1,), range(ty)), (range(1, tx - 1), (0,)), (range(1, tx - 1), (ty - 1,))]
    (first,) = pairs(inner, False, args, own, None)
    parts = pairs(rim, True, args, own, [col_a, col_b, line_a, line_b, end_a, end_b, first])
    mine = parts[1] + inside(parts[0], "gy")
    got = outside(jnp.stack([parts[2], mine]), "gy")
    mine = mine + got[0]
    cols = jnp.stack([inside(mine, "gy"), mine, got[1] + parts[2]], axis=1)
    if lax.axis_size("gx") == 4:
        other = inside(cols, "gx")
        got = outside(jnp.stack([cols[2], cols[1] + other[0], other[2]]), "gx")
        sums = [cols, other, got]
    else:
        mine = cols[1] + inside(cols[0], "gx")
        got = outside(jnp.stack([cols[2], mine]), "gx")
        mine = mine + got[0]
        sums = [jnp.stack([inside(mine, "gx"), mine, got[1] + cols[2]])]
    moved, state = finish(sums, pose, motion, body_inverse, (col_a, col_b), (end_a, end_b),
                          pos, lever, body_slot, owner_dir)
    return (jnp.transpose(moved, (0, 2, 1, 3)), jnp.transpose(state, (0, 2, 1, 3)))


def solution(mesh):
    placed = (
        P("gx", "gy", None, None),
        P("gx", "gy", None, None),
        P("gx", "gy", None, None),
        P("gx", "gy", None),
        P("gx", "gy", None),
        P("gx", "gy", None),
        P("gx", "gy", None, None),
        P("gx", "gy", None, None),
        P("gx", "gy", None, None),
        P(),
        P(),
        P(),
    )
    return jax.shard_map(
        local,
        mesh=mesh,
        in_specs=placed,
        out_specs=(P("gx", "gy", None, None), P("gx", "gy", None, None)),
        check_vma=False,
    )
```

```python
import math
import jax
import jax.numpy as jnp
from jax import lax
from jax.experimental import pallas as pl
from jax.experimental.pallas import tpu as pltpu
from jax.sharding import PartitionSpec as P

STEP_DT = 0.25
CUT_SQUARE = 4.0
F32 = jnp.float32
BF16 = jnp.bfloat16
VMEM = pl.BlockSpec(memory_space=pltpu.VMEM)
SMEM = pl.BlockSpec(memory_space=pltpu.SMEM)
HBM = pl.BlockSpec(memory_space=pl.ANY)
LIMIT = 56 * 2**20
SMALL = 16 * 2**20
DIRS = [(-1, -1), (-1, 0), (-1, 1), (0, -1), (0, 1), (1, -1), (1, 0), (1, 1)]
EXTRA = 16
BODY = 48
UNROLL = 4
STEP = 4


def rows_iota(rows, lanes):
    return lax.broadcasted_iota(jnp.int32, (rows, lanes), 0)


def split_two(value):
    high = value.astype(BF16)
    return high, (value - high.astype(F32)).astype(BF16)


def one_hot(keys, slots, base):
    hit = rows_iota(slots, keys.shape[-1]) == keys - base
    return jnp.where(hit, 1.0, 0.0).astype(BF16)


def outward(axis):
    return lax.rem(lax.axis_index(axis), 2) == 1


def split_three(value):
    first = value.astype(BF16)
    rest = value - first.astype(F32)
    second = rest.astype(BF16)
    return first, second, (rest - second.astype(F32)).astype(BF16)


def project_kernel(feat, pos, weight_v, pose, motion, inverse, own, col_in, col_out, row_in, row_out):
    x = pl.program_id(0)
    tiles_x, tiles_y, beads = pl.num_programs(0), feat.shape[1], feat.shape[3]
    rows = beads + EXTRA
    step = feat.shape[0]
    second = jnp.where(rows_iota(8, beads) < 3, 1.0, 0.0)
    high_x, high_y = outward("gx"), outward("gy")
    for z in range(step):
        for y in range(0, tiles_y, 2):
            both = jnp.concatenate([feat[z, y], feat[z, y + 1]], axis=1)
            v = jnp.dot(weight_v[...], both, preferred_element_type=F32).astype(BF16)
            for e in range(2):
                own[z, y + e, 0:beads, :] = v[:, e * beads : (e + 1) * beads].T
        px, py, pz = (pos[z, c].astype(F32) for c in range(3))
        norm = -0.25 * (px * px + py * py + pz * pz)
        none = jnp.zeros_like(px)
        parts = [px, py, pz, none, none] + [part.astype(F32) for part in split_three(norm)]
        for y in range(tiles_y):
            first = jnp.concatenate([part[y : y + 1] for part in parts], axis=0)
            own[z, y, beads:rows, :] = jnp.concatenate([first, second], axis=0).astype(BF16)
        at = pl.ds(pl.multiple_of((x * step + z) * rows, 16), rows)
        low, high = own[z, 0], own[z, tiles_y - 1]
        col_in[at, :] = jnp.where(high_y, low, high)
        col_out[at, :] = jnp.where(high_y, high, low)

    @pl.when(x == 0)
    def _():
        @pl.when(high_x)
        def _():
            row_in[...] = own[0]

        @pl.when(~high_x)
        def _():
            row_out[...] = own[0]

    @pl.when(x == tiles_x - 1)
    def _():
        @pl.when(high_x)
        def _():
            row_out[...] = own[step - 1]

        @pl.when(~high_x)
        def _():
            row_in[...] = own[step - 1]

    @pl.when(x == 0)
    def _():
        body = jnp.concatenate(
            [pose[0, r] for r in range(3, 7)] + [motion[0, r] for r in range(6)]
            + [inverse[0, 0, r : r + 1, :] for r in range(4)] + [jnp.zeros((2, beads), F32)], axis=0)
        body = jnp.concatenate(split_three(body), axis=0)
        end = col_in.shape[0] - BODY
        col_in[end:, :] = body
        col_out[end:, :] = body


def project(features, pos, weight_v, pose, motion, inverse):
    tx, ty, f, beads = features.shape
    rows = beads + EXTRA
    whole = lambda s: pl.BlockSpec(s, lambda i: (0,) * len(s))
    sds = lambda *s: jax.ShapeDtypeStruct(s, BF16)
    col = (tx * rows + BODY, beads)
    return pl.pallas_call(
        project_kernel,
        grid=(tx // STEP,),
        out_shape=[sds(tx, ty, rows, beads), sds(*col), sds(*col), sds(ty, rows, beads), sds(ty, rows, beads)],
        in_specs=[
            pl.BlockSpec((STEP, ty, f, beads), lambda i: (i, 0, 0, 0)),
            pl.BlockSpec((STEP, 3, ty, beads), lambda i: (i, 0, 0, 0)),
            whole(weight_v.shape), whole(pose.shape), whole(motion.shape), whole(inverse.shape),
        ],
        out_specs=[
            pl.BlockSpec((STEP, ty, rows, beads), lambda i: (i, 0, 0, 0)),
            whole(col), whole(col), whole((ty, rows, beads)), whole((ty, rows, beads)),
        ],
        compiler_params=pltpu.CompilerParams(vmem_limit_bytes=LIMIT),
    )(features, pos, weight_v, pose, motion, inverse)


def pairs_kernel(strips, halo, shape, *refs):
    tiles = [(i, j) for rows, cols in strips for i in rows for j in cols]
    n = len(tiles)
    tx, ty, beads, width_h, chans, nb, slots = shape
    refs = list(refs)
    take = lambda k: [refs.pop(0) for _ in range(k)]
    ids, partner, rate, features, weight_u, lever, slot, owner, own = take(9)
    around = take(7) if halo else []
    sums = take(3 if halo else 1)
    where_to, code_of = take(2)
    feat, shift_of, norm_of, terms, fsem = take(5)
    sets = [take(7), take(7)]
    vp, vsem = take(2)
    total, parts = take(2) if halo else (sums[0], None)
    wide = ty + 2
    here = lambda i, j: (i + 1) * wide + j + 1 if halo else i * ty + j
    side = chans * width_h

    at = 0
    loads = []
    for q, (i, j) in enumerate(strips):
        size = max(len(i), len(j))
        src = features.at[i[0], j[0] : j[-1] + 1] if len(i) == 1 else features.at[i[0] : i[-1] + 1, j[0]]
        loads.append(pltpu.make_async_copy(src, feat.at[at : at + size], fsem.at[q]))
        loads[-1].start()
        at += size
    if halo:
        rows = beads + EXTRA
        high_x, high_y = outward("gx"), outward("gy")
        x_in, x_out = jnp.where(high_x, 0, tx + 1), jnp.where(high_x, tx + 1, 0)
        y_in, y_out = jnp.where(high_y, 0, ty + 1), jnp.where(high_y, ty + 1, 0)
        line = lambda i: vp.at[pl.ds(i * wide + 1, ty)]
        cols, lines, ends = around[0:2], around[2:4], around[4:6]
        pairs_of = []
        for i in range(tx):
            for col, y in zip(cols, (y_in, y_out)):
                pairs_of.append((col.at[pl.ds(i * rows, rows)], vp.at[(i + 1) * wide + y]))
            pairs_of.append((own.at[i * ty : (i + 1) * ty], line(i + 1)))
        for src, end, x in zip(lines, ends, (x_in, x_out)):
            pairs_of.append((src, line(x)))
            pairs_of.append((end.at[pl.ds(0, rows)], vp.at[x * wide + y_in]))
            pairs_of.append((end.at[pl.ds(rows, rows)], vp.at[x * wide + y_out]))
    else:
        pairs_of = [(own, vp)]
    copies = [pltpu.make_async_copy(src, dst, vsem.at[q]) for q, (src, dst) in enumerate(pairs_of)]
    for copy in copies:
        copy.start()
    total[...] = around[6][...] if halo else jnp.zeros_like(total)

    def where_is(t):
        return lax.div(ids[t], jnp.int32(ty)), lax.rem(ids[t], jnp.int32(ty))

    def prepare(t, carry):
        i, j = where_is(t)
        for m in range(nb):
            code = partner[m, i, j]
            a = lax.shift_right_logical(code * 11, 5)
            where_to[t * nb + m] = here(i + a - 1, j + code - 3 * a - 1)
            code_of[t * nb + m] = code
        return carry

    row8 = rows_iota(8, beads)
    row16 = rows_iota(EXTRA, beads)
    for c in range(9):
        a, b = c // 3 - 1, c % 3 - 1
        shift_of[c] = jnp.where(row16 == 3, 1.0 * a, jnp.where(row16 == 4, 1.0 * b, 0.0)).astype(BF16)
        for q, val in enumerate((-0.5 * a, -0.5 * b, -0.25 * (a * a + b * b))):
            norm_of[c, q] = jnp.full((8, beads), val, F32)

    def make_u(s, ub):
        both = jnp.concatenate([feat[2 * s], feat[2 * s + 1]], axis=1)
        u = jnp.dot(weight_u[...], both, preferred_element_type=F32).astype(BF16)
        for e in range(2):
            for k in range(chans):
                ub[e, :, k * beads : (k + 1) * beads] = u[
                    k * width_h : (k + 1) * width_h, e * beads : (e + 1) * beads]

    def moved_block(t, m):
        return vp[where_to[t * nb + m], beads : beads + EXTRA, :] + shift_of[code_of[t * nb + m]]

    def products(t, ub, e, buf, g):
        cols = slice(2 * g * beads, 2 * (g + 1) * beads)
        lhs = jnp.concatenate([vp[where_to[t * nb + m], 0:beads, :] for m in range(nb)], axis=0)
        buf[:, cols] = jnp.dot(lhs, ub[e, :, cols], preferred_element_type=F32)

    def scores(t, ub, e, buf, zbuf):
        i, j = where_is(t)
        up = vp[here(i, j), beads : beads + EXTRA, :].astype(F32)[0:8]
        px, py = (jnp.broadcast_to(0.5 * up[c : c + 1], (8, beads)) for c in (0, 1))
        high = jnp.where(row8 < 3, 0.5 * up, jnp.where(row8 == 3, px, jnp.where(row8 == 4, py, 1.0)))
        low = jnp.where(row8 < 3, pltpu.roll(up, 3, 0), 0.0)
        mine = jnp.concatenate([high, low], axis=0).astype(BF16)
        none = jnp.zeros_like(mine)
        mine = jnp.concatenate([jnp.concatenate([mine, none], axis=1), jnp.concatenate([none, mine], axis=1)], axis=0)
        feats = []
        for m in range(nb):
            code = code_of[t * nb + m]
            block = moved_block(t, m).astype(F32)
            up = block[0:8]
            qx, qy = (jnp.broadcast_to(up[c : c + 1], (8, beads)) for c in (0, 1))
            norm = jnp.broadcast_to(up[5:6] + up[6:7] + up[7:8], (8, beads)) + norm_of[code, 2]
            norm = norm + qx * norm_of[code, 0] + qy * norm_of[code, 1]
            n1 = norm.astype(BF16).astype(F32)
            rest = norm - n1
            n2 = rest.astype(BF16).astype(F32)
            high = jnp.where(row8 < 5, up, jnp.where(row8 == 5, n1, jnp.where(row8 == 6, n2, rest - n2)))
            feats.append(jnp.concatenate([high, block[8:16]], axis=0).astype(BF16))
        left = jnp.concatenate([jnp.concatenate(feats[h::2], axis=1) for h in range(2)], axis=0)
        zbuf[...] = lax.dot_general(left, mine, (((0,), (0,)), ((), ())), preferred_element_type=F32)

    def couples(buf, zbuf, cbuf, which):
        step = 16
        for m in which:
            for r in range(0, beads, step):
                z = zbuf[m // 2 * beads + r : m // 2 * beads + r + step, (m % 2) * beads : (m % 2 + 1) * beads]
                env = jnp.maximum(1.0 + z, 0.0)
                total = None
                for k in range(chans):
                    part = jnp.exp2(z * (rate[k] * (CUT_SQUARE / math.log(2.0)))) * buf[
                        m * beads + r : m * beads + r + step, k * beads : (k + 1) * beads]
                    total = part if total is None else total + part
                cbuf[m * beads + r : m * beads + r + step, :] = ((env * env) * total).astype(BF16)

    def gather(t, cbuf):
        i, j = where_is(t)
        lhs = jnp.concatenate([moved_block(t, m) for m in range(nb)], axis=1)
        out = jnp.dot(lhs, cbuf[...], preferred_element_type=F32) * (1.0 / width_h)
        mine = vp[here(i, j), beads : beads + EXTRA, :].astype(F32)
        w = out[8:9]
        fx = mine[0:1] * w - out[0:1] - out[3:4]
        fy = mine[1:2] * w - out[1:2] - out[4:5]
        fz = mine[2:3] * w - out[2:3]
        lx, ly, lz = (lever[i, c, pl.ds(j, 1), :] for c in range(3))
        value = jnp.concatenate(
            [fx, fy, fz, ly * fz - lz * fy, lz * fx - lx * fz, lx * fy - ly * fx,
             jnp.zeros((2, beads), F32)], axis=0)
        term = jnp.concatenate(split_two(value), axis=0)
        terms[t] = term

    def add_up(s):
        left, right = [], []
        for t in (2 * s, 2 * s + 1):
            i, j = where_is(t)
            key = owner[i, pl.ds(j, 1), :] * slots + slot[i, pl.ds(j, 1), :]
            left.append(terms[t])
            right.append(one_hot(key, slots, 4 * slots))
        got = lax.dot_general(jnp.concatenate(left, axis=1), jnp.concatenate(right, axis=1),
                              (((1,), (1,)), ((), ())), preferred_element_type=F32)
        return got[0:8] + got[8:16]

    lax.fori_loop(0, n, prepare, 0)
    last = n // 2 - 1

    def fill(s, into):
        ub, sa, sb, za, zb, _, _ = into
        scores(2 * s, ub, 0, sa, za)
        scores(2 * s + 1, ub, 1, sb, zb)
        for g in range(chans // 2):
            products(2 * s, ub, 0, sa, g)
            products(2 * s + 1, ub, 1, sb, g)

    def half(s, now, later):
        _, sa, sb, za, zb, ca, cb = now
        before = jnp.maximum(s - 1, 0)
        nxt = jnp.minimum(s + 1, last)
        scores(2 * nxt + 0, later[0], 0, later[1], later[3])
        products(2 * nxt + 0, later[0], 0, later[1], 0)
        couples(sa, za, ca, range(0, 3))
        products(2 * nxt + 0, later[0], 0, later[1], 1)
        couples(sa, za, ca, range(3, 6))
        scores(2 * nxt + 1, later[0], 1, later[2], later[4])
        products(2 * nxt + 1, later[0], 1, later[2], 0)
        couples(sb, zb, cb, range(0, 3))
        products(2 * nxt + 1, later[0], 1, later[2], 1)
        couples(sb, zb, cb, range(3, 6))
        make_u(jnp.minimum(s + 2, last), now[0])
        gather(2 * before, later[5])
        gather(2 * before + 1, later[6])
        total[...] = total[...] + jnp.where(s == 0, 0.0, add_up(before))

    loads[0].wait()
    make_u(0, sets[0][0])
    make_u(min(1, last), sets[1][0])
    for copy in copies:
        copy.wait()
    fill(0, sets[0])
    for load in loads[1:]:
        load.wait()

    def body(g, carry):
        half(2 * g, sets[0], sets[1])
        half(2 * g + 1, sets[1], sets[0])
        return carry

    lax.fori_loop(0, n // 4, body, 0)
    gather(n - 2, sets[1][5])
    gather(n - 1, sets[1][6])
    total[...] = total[...] + add_up(last)
    if halo:
        turn = lambda d, high: 1 + jnp.where(high, d, -d)
        parts[1, 1] = total[...]
        for a, b in DIRS:
            keep = [t for t, (i, j) in enumerate(tiles)
                    if (a == 0 or i == (0 if a < 0 else tx - 1)) and (b == 0 or j == (0 if b < 0 else ty - 1))]
            left, right = [], []
            for t in keep:
                i, j = tiles[t]
                key = owner[i, j : j + 1, :] * slots + slot[i, j : j + 1, :]
                left.append(terms[t])
                right.append(one_hot(key, slots, (3 * a + b + 4) * slots))
            got = lax.dot_general(jnp.concatenate(left, axis=1), jnp.concatenate(right, axis=1),
                                  (((1,), (1,)), ((), ())), preferred_element_type=F32)
            parts[turn(b, high_y), turn(a, high_x)] = got[0:8] + got[8:16]
        for q in range(3):
            sums[q][...] = parts[q]


def pairs(strips, halo, args, own, around):
    tiles = [(i, j) for rows, cols in strips for i in rows for j in cols]
    partner, rate, features, weight_u, lever, slot, owner, slots = args
    tx, ty, f, beads = features.shape
    nb = partner.shape[0]
    chans = rate.shape[0]
    width_h = weight_u.shape[0] // chans
    rows = beads + EXTRA
    n = len(tiles)
    out = jax.ShapeDtypeStruct((3, 8, slots) if halo else (8, slots), F32)
    scratch = [
        pltpu.SMEM((n * nb,), jnp.int32),
        pltpu.SMEM((n * nb,), jnp.int32),
        pltpu.VMEM((n, f, beads), BF16),
        pltpu.VMEM((9, EXTRA, beads), BF16),
        pltpu.VMEM((9, 3, 8, beads), F32),
        pltpu.VMEM((n, 16, beads), BF16),
        pltpu.SemaphoreType.DMA((len(strips),)),
    ]
    scratch += 2 * [
        pltpu.VMEM((2, width_h, chans * beads), BF16),
        pltpu.VMEM((nb * beads, chans * beads), F32),
        pltpu.VMEM((nb * beads, chans * beads), F32),
        pltpu.VMEM((nb // 2 * beads, 2 * beads), F32),
        pltpu.VMEM((nb // 2 * beads, 2 * beads), F32),
        pltpu.VMEM((nb * beads, beads), BF16),
        pltpu.VMEM((nb * beads, beads), BF16),
    ]
    spread = (tx + 2) * (ty + 2) if halo else tx * ty
    scratch += [pltpu.VMEM((spread, rows, beads), BF16), pltpu.SemaphoreType.DMA((3 * tx + 6 if halo else 1,))]
    if halo:
        scratch += [pltpu.VMEM((8, slots), F32), pltpu.VMEM((3, 3, 8, slots), F32)]
    ids = jnp.asarray([i * ty + j for i, j in tiles], jnp.int32)
    shape = (tx, ty, beads, width_h, chans, nb, slots)
    return pl.pallas_call(
        lambda *refs: pairs_kernel(strips, halo, shape, *refs),
        out_shape=[out] * (3 if halo else 1),
        in_specs=[SMEM, SMEM, SMEM, HBM, VMEM, VMEM, VMEM, VMEM, HBM]
        + ([HBM] * 6 + [VMEM] if halo else []),
        out_specs=[VMEM] * (3 if halo else 1),
        scratch_shapes=scratch,
        compiler_params=pltpu.CompilerParams(vmem_limit_bytes=LIMIT),
        cost_estimate=pl.CostEstimate(flops=n * 150_000_000, bytes_accessed=n * 100_000, transcendentals=0),
    )(ids, partner, rate, features, weight_u, lever, slot, owner, own.reshape((tx * ty, rows, beads)), *(around if halo else []))


def rotation_rows(q):
    w, a, b, c = q
    return [
        [1 - 2 * (b * b + c * c), 2 * (a * b - w * c), 2 * (a * c + w * b)],
        [2 * (a * b + w * c), 1 - 2 * (a * a + c * c), 2 * (b * c - w * a)],
        [2 * (a * c - w * b), 2 * (b * c + w * a), 1 - 2 * (a * a + b * b)],
    ]


def integrate(q, motion, inverse, f):
    vel = [motion[r] + STEP_DT * inverse[0] * f[r] for r in range(3)]
    ang = [motion[3 + r] + STEP_DT * f[3 + r] for r in range(3)]
    old = rotation_rows(q)
    frame = [sum(old[r][c] * ang[r] for r in range(3)) * inverse[1 + c] for c in range(3)]
    om = [sum(old[r][c] * frame[c] for c in range(3)) for r in range(3)]
    w, x, y, z = q
    rate = [
        -(om[0] * x + om[1] * y + om[2] * z),
        w * om[0] + om[1] * z - om[2] * y,
        w * om[1] + om[2] * x - om[0] * z,
        w * om[2] + om[0] * y - om[1] * x,
    ]
    step = [q[r] + 0.5 * STEP_DT * rate[r] for r in range(4)]
    size = jnp.sqrt(sum(s * s for s in step))
    new = [s / size for s in step]
    turned = rotation_rows(new)
    rel = [sum(turned[r][k] * old[c][k] for k in range(3)) for r in range(3) for c in range(3)]
    return new, vel, ang, [STEP_DT * v for v in vel] + rel


def finish_kernel(count, *refs):
    sums, refs = refs[:count], refs[count:]
    finish_body(sums, *refs)


def finish_body(sums, pose, motion, inverse, col_a, col_b, end_a, end_b, pos, lever, slot, owner,
                  moved, state, table):
    tx, ty = pos.shape[0], pos.shape[2]
    slots = owner.shape[2]
    high_x, high_y = outward("gx"), outward("gy")
    turn = lambda d, high: 1 + jnp.where(high, d, -d)
    rows_a, rows_b = end_a.shape[0] - 3 * BODY, col_a.shape[0] - BODY
    bodies = {(1, 0): (col_a, rows_b), (1, 2): (col_b, rows_b)}
    for a, end in ((0, end_a), (2, end_b)):
        for q, b in enumerate((1, 0, 2)):
            bodies[a, b] = (end, rows_a + q * BODY)
    if len(sums) == 1:
        totals = lambda b, a: sums[0][a, b]
    else:
        cols, other, got = sums
        totals = lambda b, a: (other[1, b] + cols[0, b] + got[2, b], cols[1, b] + other[0, b] + got[0, b],
                               got[1, b] + cols[2, b])[a]
    for a in range(3):
        for b in range(3):
            f = totals(b, a)
            f = [f[r : r + 1] for r in range(6)]
            if (a, b) == (1, 1):
                q = [pose[0, 3 + r] for r in range(4)]
                mot = [motion[0, r] for r in range(6)]
                inv = [inverse[0, 0, r : r + 1, :] for r in range(4)]
            else:
                ref, at = bodies[a, b]
                third = BODY // 3
                body = sum(ref[at + k * third : at + (k + 1) * third, :].astype(F32) for k in range(3))
                body = [body[r : r + 1] for r in range(14)]
                q, mot, inv = body[0:4], body[4:10], body[10:14]
            new, vel, ang, packed = integrate(q, mot, inv, f)
            if (a, b) == (1, 1):
                centre = [pose[0, r] + STEP_DT * vel[r] for r in range(3)]
                for r, val in enumerate(centre + new + vel + ang):
                    state[0, r] = val
            packed = jnp.concatenate(packed + [jnp.zeros((4, slots), F32)], axis=0)
            table[a, b] = jnp.concatenate(split_two(packed), axis=0)

    def place(i, j, a, b):
        key = owner[i, pl.ds(j, 1), :] * slots + slot[i, pl.ds(j, 1), :]
        rows = table[1, 1] if a == 0 and b == 0 else table[turn(a, high_x), turn(b, high_y)]
        got = jnp.dot(rows, one_hot(key, slots, (3 * a + b + 4) * slots), preferred_element_type=F32)
        got = got[0:16] + got[16:32]
        lev = [lever[i, c, pl.ds(j, 1), :] for c in range(3)]
        return [got[r : r + 1] + sum(got[3 + 3 * r + c : 4 + 3 * r + c] * lev[c] for c in range(3)) for r in range(3)]

    def line(i, carry):
        for j in range(ty):
            for r, val in enumerate(place(i, j, 0, 0)):
                moved[i, r, j : j + 1, :] = pos[i, r, j : j + 1, :].astype(F32) + val - lever[i, r, j : j + 1, :]
        return carry

    lax.fori_loop(0, tx, line, 0, unroll=UNROLL)
    for a, b in DIRS:
        for i in range(tx) if a == 0 else [0 if a < 0 else tx - 1]:
            for j in range(ty) if b == 0 else [0 if b < 0 else ty - 1]:
                for r, val in enumerate(place(i, j, a, b)):
                    moved[i, r, j : j + 1, :] = moved[i, r, j : j + 1, :] + val


def finish(sums, pose, motion, inverse, cols, ends, pos, lever, slot, owner):
    slots = pose.shape[3]
    return pl.pallas_call(
        lambda *refs: finish_kernel(len(sums), *refs),
        out_shape=[jax.ShapeDtypeStruct(lever.shape, F32), jax.ShapeDtypeStruct((1, 13, 1, slots), F32)],
        in_specs=[VMEM] * (11 + len(sums)),
        out_specs=[VMEM] * 2,
        scratch_shapes=[pltpu.VMEM((3, 3, 32, slots), BF16)],
        compiler_params=pltpu.CompilerParams(vmem_limit_bytes=SMALL),
    )(*sums, pose, motion, inverse, *cols, *ends, pos, lever, slot, owner)


def swap(value, axis, start):
    n = lax.axis_size(axis)
    route = []
    for c in range(start, n + start, 2):
        route += [(c % n, (c + 1) % n), ((c + 1) % n, c % n)]
    return lax.ppermute(value, axis, route)


def inside(value, axis):
    return swap(value, axis, 0)


def outside(value, axis):
    return swap(value, axis, 1)


def local(positions, features, lever, partner, body_slot, owner_dir, body_pose, body_motion,
          body_inverse, weight_u, weight_v, radial_rate):
    tx, ty = positions.shape[0], positions.shape[1]
    slots = body_pose.shape[3]
    rows = positions.shape[3] + EXTRA
    pos, lever = (jnp.transpose(v, (0, 2, 1, 3)) for v in (positions, lever))
    pose, motion = (jnp.transpose(v, (0, 2, 1, 3)) for v in (body_pose, body_motion))
    codes = jnp.transpose(partner, (2, 0, 1))
    own, col_in, col_out, row_in, row_out = project(features, pos, weight_v, pose, motion, body_inverse)
    line_a, line_b = inside(row_in, "gx"), outside(row_out, "gx")
    col_a, col_b = inside(col_in, "gy"), outside(col_out, "gy")
    high_x = outward("gx")
    bodies = [v[tx * rows :] for v in (col_in, col_a, col_b)]
    corner = lambda high: jnp.concatenate(
        [jnp.where(high, v[(tx - 1) * rows : tx * rows], v[:rows]) for v in (col_a, col_b)] + bodies, axis=0)
    end_a, end_b = inside(corner(~high_x), "gx"), outside(corner(high_x), "gx")
    args = (codes, radial_rate, features, weight_u, lever, body_slot, owner_dir, slots)
    inner = [((i,), range(1, ty - 1)) for i in range(1, tx - 1)]
    rim = [((0,), range(ty)), ((tx - 1,), range(ty)), (range(1, tx - 1), (0,)), (range(1, tx - 1), (ty - 1,))]
    (first,) = pairs(inner, False, args, own, None)
    parts = pairs(rim, True, args, own, [col_a, col_b, line_a, line_b, end_a, end_b, first])
    mine = parts[1] + inside(parts[0], "gy")
    got = outside(jnp.stack([parts[2], mine]), "gy")
    mine = mine + got[0]
    cols = jnp.stack([inside(mine, "gy"), mine, got[1] + parts[2]], axis=1)
    if lax.axis_size("gx") == 4:
        other = inside(cols, "gx")
        got = outside(jnp.stack([cols[2], cols[1] + other[0], other[2]]), "gx")
        sums = [cols, other, got]
    else:
        mine = cols[1] + inside(cols[0], "gx")
        got = outside(jnp.stack([cols[2], mine]), "gx")
        mine = mine + got[0]
        sums = [jnp.stack([inside(mine, "gx"), mine, got[1] + cols[2]])]
    moved, state = finish(sums, pose, motion, body_inverse, (col_a, col_b), (end_a, end_b),
                          pos, lever, body_slot, owner_dir)
    return (jnp.transpose(moved, (0, 2, 1, 3)), jnp.transpose(state, (0, 2, 1, 3)))


def solution(mesh):
    placed = (
        P("gx", "gy", None, None),
        P("gx", "gy", None, None),
        P("gx", "gy", None, None),
        P("gx", "gy", None),
        P("gx", "gy", None),
        P("gx", "gy", None),
        P("gx", "gy", None, None),
        P("gx", "gy", None, None),
        P("gx", "gy", None, None),
        P(),
        P(),
        P(),
    )
    return jax.shard_map(
        local,
        mesh=mesh,
        in_specs=placed,
        out_specs=(P("gx", "gy", None, None), P("gx", "gy", None, None)),
        check_vma=False,
    )
```

```python
import math
import jax
import jax.numpy as jnp
from jax import lax
from jax.experimental import pallas as pl
from jax.experimental.pallas import tpu as pltpu
from jax.sharding import PartitionSpec as P

STEP_DT = 0.25
CUT_SQUARE = 4.0
F32 = jnp.float32
BF16 = jnp.bfloat16
VMEM = pl.BlockSpec(memory_space=pltpu.VMEM)
SMEM = pl.BlockSpec(memory_space=pltpu.SMEM)
HBM = pl.BlockSpec(memory_space=pl.ANY)
LIMIT = 56 * 2**20
MEDIUM = 24 * 2**20
SMALL = 16 * 2**20
DIRS = [(-1, -1), (-1, 0), (-1, 1), (0, -1), (0, 1), (1, -1), (1, 0), (1, 1)]
EXTRA = 16
BODY = 48
UNROLL = 4
STEP = 4


def rows_iota(rows, lanes):
    return lax.broadcasted_iota(jnp.int32, (rows, lanes), 0)


def split_two(value):
    high = value.astype(BF16)
    return high, (value - high.astype(F32)).astype(BF16)


def one_hot(keys, slots, base):
    hit = rows_iota(slots, keys.shape[-1]) == keys - base
    return jnp.where(hit, 1.0, 0.0).astype(BF16)


def outward(axis):
    return lax.rem(lax.axis_index(axis), 2) == 1


def split_three(value):
    first = value.astype(BF16)
    rest = value - first.astype(F32)
    second = rest.astype(BF16)
    return first, second, (rest - second.astype(F32)).astype(BF16)


def project_kernel(feat, pos, weight_v, pose, motion, inverse, own, col_in, col_out, row_in, row_out):
    x = pl.program_id(0)
    tiles_x, tiles_y, beads = pl.num_programs(0), feat.shape[1], feat.shape[3]
    rows = beads + EXTRA
    step = feat.shape[0]
    second = jnp.where(rows_iota(8, beads) < 3, 1.0, 0.0)
    high_x, high_y = outward("gx"), outward("gy")
    for z in range(step):
        for y in range(0, tiles_y, 2):
            both = jnp.concatenate([feat[z, y], feat[z, y + 1]], axis=1)
            v = jnp.dot(weight_v[...], both, preferred_element_type=F32).astype(BF16)
            for e in range(2):
                own[z, y + e, 0:beads, :] = v[:, e * beads : (e + 1) * beads].T
        px, py, pz = (pos[z, c].astype(F32) for c in range(3))
        norm = -0.25 * (px * px + py * py + pz * pz)
        none = jnp.zeros_like(px)
        parts = [px, py, pz, none, none] + [part.astype(F32) for part in split_three(norm)]
        for y in range(tiles_y):
            first = jnp.concatenate([part[y : y + 1] for part in parts], axis=0)
            own[z, y, beads:rows, :] = jnp.concatenate([first, second], axis=0).astype(BF16)
        at = pl.ds(pl.multiple_of((x * step + z) * rows, 16), rows)
        low, high = own[z, 0], own[z, tiles_y - 1]
        col_in[at, :] = jnp.where(high_y, low, high)
        col_out[at, :] = jnp.where(high_y, high, low)

    @pl.when(x == 0)
    def _():
        @pl.when(high_x)
        def _():
            row_in[...] = own[0]

        @pl.when(~high_x)
        def _():
            row_out[...] = own[0]

    @pl.when(x == tiles_x - 1)
    def _():
        @pl.when(high_x)
        def _():
            row_out[...] = own[step - 1]

        @pl.when(~high_x)
        def _():
            row_in[...] = own[step - 1]

    @pl.when(x == 0)
    def _():
        body = jnp.concatenate(
            [pose[0, r] for r in range(3, 7)] + [motion[0, r] for r in range(6)]
            + [inverse[0, 0, r : r + 1, :] for r in range(4)] + [jnp.zeros((2, beads), F32)], axis=0)
        body = jnp.concatenate(split_three(body), axis=0)
        end = col_in.shape[0] - BODY
        col_in[end:, :] = body
        col_out[end:, :] = body


def project(features, pos, weight_v, pose, motion, inverse):
    tx, ty, f, beads = features.shape
    rows = beads + EXTRA
    whole = lambda s: pl.BlockSpec(s, lambda i: (0,) * len(s))
    sds = lambda *s: jax.ShapeDtypeStruct(s, BF16)
    col = (tx * rows + BODY, beads)
    return pl.pallas_call(
        project_kernel,
        grid=(tx // STEP,),
        out_shape=[sds(tx, ty, rows, beads), sds(*col), sds(*col), sds(ty, rows, beads), sds(ty, rows, beads)],
        in_specs=[
            pl.BlockSpec((STEP, ty, f, beads), lambda i: (i, 0, 0, 0)),
            pl.BlockSpec((STEP, 3, ty, beads), lambda i: (i, 0, 0, 0)),
            whole(weight_v.shape), whole(pose.shape), whole(motion.shape), whole(inverse.shape),
        ],
        out_specs=[
            pl.BlockSpec((STEP, ty, rows, beads), lambda i: (i, 0, 0, 0)),
            whole(col), whole(col), whole((ty, rows, beads)), whole((ty, rows, beads)),
        ],
        compiler_params=pltpu.CompilerParams(vmem_limit_bytes=LIMIT),
    )(features, pos, weight_v, pose, motion, inverse)


def pairs_kernel(strips, halo, shape, *refs):
    tiles = [(i, j) for rows, cols in strips for i in rows for j in cols]
    n = len(tiles)
    tx, ty, beads, width_h, chans, nb, slots = shape
    refs = list(refs)
    take = lambda k: [refs.pop(0) for _ in range(k)]
    ids, partner, codes, rate, features, weight_u, lever, slot, owner, own = take(10)
    around = take(7) if halo else []
    sums = take(3 if halo else 1)
    table, where_to, tsem = take(3)
    feat, shift_of, norm_of, terms, fsem = take(5)
    sets = [take(7), take(7)]
    vp, vsem = take(2)
    total, parts = take(2) if halo else (sums[0], None)
    wide = ty + 2
    here = lambda i, j: (i + 1) * wide + j + 1 if halo else i * ty + j
    side = chans * width_h

    at = 0
    loads = []
    for q, (i, j) in enumerate(strips):
        size = max(len(i), len(j))
        src = features.at[i[0], j[0] : j[-1] + 1] if len(i) == 1 else features.at[i[0] : i[-1] + 1, j[0]]
        loads.append(pltpu.make_async_copy(src, feat.at[at : at + size], fsem.at[q]))
        loads[-1].start()
        at += size
    if halo:
        rows = beads + EXTRA
        high_x, high_y = outward("gx"), outward("gy")
        x_in, x_out = jnp.where(high_x, 0, tx + 1), jnp.where(high_x, tx + 1, 0)
        y_in, y_out = jnp.where(high_y, 0, ty + 1), jnp.where(high_y, ty + 1, 0)
        line = lambda i: vp.at[pl.ds(i * wide + 1, ty)]
        cols, lines, ends = around[0:2], around[2:4], around[4:6]
        pairs_of = []
        for i in range(tx):
            for col, y in zip(cols, (y_in, y_out)):
                pairs_of.append((col.at[pl.ds(i * rows, rows)], vp.at[(i + 1) * wide + y]))
            pairs_of.append((own.at[i * ty : (i + 1) * ty], line(i + 1)))
        for src, end, x in zip(lines, ends, (x_in, x_out)):
            pairs_of.append((src, line(x)))
            pairs_of.append((end.at[pl.ds(0, rows)], vp.at[x * wide + y_in]))
            pairs_of.append((end.at[pl.ds(rows, rows)], vp.at[x * wide + y_out]))
    else:
        pairs_of = [(own, vp)]
    copies = [pltpu.make_async_copy(src, dst, vsem.at[q]) for q, (src, dst) in enumerate(pairs_of)]
    for copy in copies:
        copy.start()
    total[...] = around[6][...] if halo else jnp.zeros_like(total)

    def where_is(t):
        return lax.div(ids[t], jnp.int32(ty)), lax.rem(ids[t], jnp.int32(ty))

    both = codes.shape
    code = codes[...]
    a = lax.shift_right_logical(code * 11, 5)
    pitch = wide if halo else ty
    first = lax.broadcasted_iota(jnp.int32, both, 1) * pitch + lax.broadcasted_iota(jnp.int32, both, 2)
    table[:, :, 0:ty] = first + (a - 1) * pitch + code - 3 * a - 1 + (wide + 1 if halo else 0)
    tables = pltpu.make_async_copy(table, where_to, tsem)
    tables.start()

    row8 = rows_iota(8, beads)
    row16 = rows_iota(EXTRA, beads)
    for c in range(9):
        a, b = c // 3 - 1, c % 3 - 1
        shift_of[c] = jnp.where(row16 == 3, 1.0 * a, jnp.where(row16 == 4, 1.0 * b, 0.0)).astype(BF16)
        for q, val in enumerate((-0.5 * a, -0.5 * b, -0.25 * (a * a + b * b))):
            norm_of[c, q] = jnp.full((8, beads), val, F32)

    def make_u(s, ub):
        both = jnp.concatenate([feat[2 * s], feat[2 * s + 1]], axis=1)
        u = jnp.dot(weight_u[...], both, preferred_element_type=F32).astype(BF16)
        for e in range(2):
            for k in range(chans):
                ub[e, :, k * beads : (k + 1) * beads] = u[
                    k * width_h : (k + 1) * width_h, e * beads : (e + 1) * beads]

    def moved_block(i, j, m):
        return vp[where_to[m, i, j], beads : beads + EXTRA, :] + shift_of[partner[m, i, j]]

    def products(t, ub, e, buf, g):
        cols = slice(2 * g * beads, 2 * (g + 1) * beads)
        i, j = where_is(t)
        lhs = jnp.concatenate([vp[where_to[m, i, j], 0:beads, :] for m in range(nb)], axis=0)
        buf[:, cols] = jnp.dot(lhs, ub[e, :, cols], preferred_element_type=F32)

    def scores(t, ub, e, buf, zbuf):
        i, j = where_is(t)
        up = vp[here(i, j), beads : beads + EXTRA, :].astype(F32)[0:8]
        px, py = (jnp.broadcast_to(0.5 * up[c : c + 1], (8, beads)) for c in (0, 1))
        high = jnp.where(row8 < 3, 0.5 * up, jnp.where(row8 == 3, px, jnp.where(row8 == 4, py, 1.0)))
        low = jnp.where(row8 < 3, pltpu.roll(up, 3, 0), 0.0)
        mine = jnp.concatenate([high, low], axis=0).astype(BF16)
        none = jnp.zeros_like(mine)
        mine = jnp.concatenate([jnp.concatenate([mine, none], axis=1), jnp.concatenate([none, mine], axis=1)], axis=0)
        feats = []
        for m in range(nb):
            code = partner[m, i, j]
            block = moved_block(i, j, m).astype(F32)
            up = block[0:8]
            qx, qy = (jnp.broadcast_to(up[c : c + 1], (8, beads)) for c in (0, 1))
            norm = jnp.broadcast_to(up[5:6] + up[6:7] + up[7:8], (8, beads)) + norm_of[code, 2]
            norm = norm + qx * norm_of[code, 0] + qy * norm_of[code, 1]
            n1 = norm.astype(BF16).astype(F32)
            rest = norm - n1
            n2 = rest.astype(BF16).astype(F32)
            high = jnp.where(row8 < 5, up, jnp.where(row8 == 5, n1, jnp.where(row8 == 6, n2, rest - n2)))
            feats.append(jnp.concatenate([high, block[8:16]], axis=0).astype(BF16))
        left = jnp.concatenate([jnp.concatenate(feats[h::2], axis=1) for h in range(2)], axis=0)
        zbuf[...] = lax.dot_general(left, mine, (((0,), (0,)), ((), ())), preferred_element_type=F32)

    def couples(buf, zbuf, cbuf, which):
        step = 16
        for m in which:
            for r in range(0, beads, step):
                z = zbuf[m // 2 * beads + r : m // 2 * beads + r + step, (m % 2) * beads : (m % 2 + 1) * beads]
                env = jnp.maximum(1.0 + z, 0.0)
                total = None
                for k in range(chans):
                    part = jnp.exp2(z * (rate[k] * (CUT_SQUARE / math.log(2.0)))) * buf[
                        m * beads + r : m * beads + r + step, k * beads : (k + 1) * beads]
                    total = part if total is None else total + part
                cbuf[m * beads + r : m * beads + r + step, :] = ((env * env) * total).astype(BF16)

    def gather(t, cbuf):
        i, j = where_is(t)
        lhs = jnp.concatenate([moved_block(i, j, m) for m in range(nb)], axis=1)
        out = jnp.dot(lhs, cbuf[...], preferred_element_type=F32) * (1.0 / width_h)
        mine = vp[here(i, j), beads : beads + EXTRA, :].astype(F32)
        w = out[8:9]
        fx = mine[0:1] * w - out[0:1] - out[3:4]
        fy = mine[1:2] * w - out[1:2] - out[4:5]
        fz = mine[2:3] * w - out[2:3]
        lx, ly, lz = (lever[i, c, pl.ds(j, 1), :] for c in range(3))
        value = jnp.concatenate(
            [fx, fy, fz, ly * fz - lz * fy, lz * fx - lx * fz, lx * fy - ly * fx,
             jnp.zeros((2, beads), F32)], axis=0)
        term = jnp.concatenate(split_two(value), axis=0)
        terms[t] = term

    def add_up(s):
        left, right = [], []
        for t in (2 * s, 2 * s + 1):
            i, j = where_is(t)
            key = owner[i, pl.ds(j, 1), :] * slots + slot[i, pl.ds(j, 1), :]
            left.append(terms[t])
            right.append(one_hot(key, slots, 4 * slots))
        got = lax.dot_general(jnp.concatenate(left, axis=1), jnp.concatenate(right, axis=1),
                              (((1,), (1,)), ((), ())), preferred_element_type=F32)
        return got[0:8] + got[8:16]

    last = n // 2 - 1

    def fill(s, into):
        ub, sa, sb, za, zb, _, _ = into
        scores(2 * s, ub, 0, sa, za)
        scores(2 * s + 1, ub, 1, sb, zb)
        for g in range(chans // 2):
            products(2 * s, ub, 0, sa, g)
            products(2 * s + 1, ub, 1, sb, g)

    def half(s, now, later):
        _, sa, sb, za, zb, ca, cb = now
        before = jnp.maximum(s - 1, 0)
        nxt = jnp.minimum(s + 1, last)
        scores(2 * nxt + 0, later[0], 0, later[1], later[3])
        products(2 * nxt + 0, later[0], 0, later[1], 0)
        couples(sa, za, ca, range(0, 3))
        products(2 * nxt + 0, later[0], 0, later[1], 1)
        couples(sa, za, ca, range(3, 6))
        scores(2 * nxt + 1, later[0], 1, later[2], later[4])
        products(2 * nxt + 1, later[0], 1, later[2], 0)
        couples(sb, zb, cb, range(0, 3))
        products(2 * nxt + 1, later[0], 1, later[2], 1)
        couples(sb, zb, cb, range(3, 6))
        make_u(jnp.minimum(s + 2, last), now[0])
        gather(2 * before, later[5])
        gather(2 * before + 1, later[6])
        total[...] = total[...] + jnp.where(s == 0, 0.0, add_up(before))

    loads[0].wait()
    make_u(0, sets[0][0])
    make_u(min(1, last), sets[1][0])
    for copy in copies:
        copy.wait()
    tables.wait()
    fill(0, sets[0])
    for load in loads[1:]:
        load.wait()

    def body(g, carry):
        half(2 * g, sets[0], sets[1])
        half(2 * g + 1, sets[1], sets[0])
        return carry

    lax.fori_loop(0, n // 4, body, 0)
    gather(n - 2, sets[1][5])
    gather(n - 1, sets[1][6])
    total[...] = total[...] + add_up(last)
    if halo:
        turn = lambda d, high: 1 + jnp.where(high, d, -d)
        parts[1, 1] = total[...]
        for a, b in DIRS:
            keep = [t for t, (i, j) in enumerate(tiles)
                    if (a == 0 or i == (0 if a < 0 else tx - 1)) and (b == 0 or j == (0 if b < 0 else ty - 1))]
            left, right = [], []
            for t in keep:
                i, j = tiles[t]
                key = owner[i, j : j + 1, :] * slots + slot[i, j : j + 1, :]
                left.append(terms[t])
                right.append(one_hot(key, slots, (3 * a + b + 4) * slots))
            got = lax.dot_general(jnp.concatenate(left, axis=1), jnp.concatenate(right, axis=1),
                                  (((1,), (1,)), ((), ())), preferred_element_type=F32)
            parts[turn(b, high_y), turn(a, high_x)] = got[0:8] + got[8:16]
        for q in range(3):
            sums[q][...] = parts[q]


def pairs(strips, halo, args, own, around):
    tiles = [(i, j) for rows, cols in strips for i in rows for j in cols]
    partner, rate, features, weight_u, lever, slot, owner, slots = args
    tx, ty, f, beads = features.shape
    nb = partner.shape[0]
    chans = rate.shape[0]
    width_h = weight_u.shape[0] // chans
    rows = beads + EXTRA
    n = len(tiles)
    out = jax.ShapeDtypeStruct((3, 8, slots) if halo else (8, slots), F32)
    scratch = [
        pltpu.VMEM((nb, tx, beads), jnp.int32),
        pltpu.SMEM((nb, tx, beads), jnp.int32),
        pltpu.SemaphoreType.DMA,
        pltpu.VMEM((n, f, beads), BF16),
        pltpu.VMEM((9, EXTRA, beads), BF16),
        pltpu.VMEM((9, 3, 8, beads), F32),
        pltpu.VMEM((n, 16, beads), BF16),
        pltpu.SemaphoreType.DMA((len(strips),)),
    ]
    scratch += 2 * [
        pltpu.VMEM((2, width_h, chans * beads), BF16),
        pltpu.VMEM((nb * beads, chans * beads), F32),
        pltpu.VMEM((nb * beads, chans * beads), F32),
        pltpu.VMEM((nb // 2 * beads, 2 * beads), F32),
        pltpu.VMEM((nb // 2 * beads, 2 * beads), F32),
        pltpu.VMEM((nb * beads, beads), BF16),
        pltpu.VMEM((nb * beads, beads), BF16),
    ]
    spread = (tx + 2) * (ty + 2) if halo else tx * ty
    scratch += [pltpu.VMEM((spread, rows, beads), BF16), pltpu.SemaphoreType.DMA((3 * tx + 6 if halo else 1,))]
    if halo:
        scratch += [pltpu.VMEM((8, slots), F32), pltpu.VMEM((3, 3, 8, slots), F32)]
    ids = jnp.asarray([i * ty + j for i, j in tiles], jnp.int32)
    shape = (tx, ty, beads, width_h, chans, nb, slots)
    return pl.pallas_call(
        lambda *refs: pairs_kernel(strips, halo, shape, *refs),
        out_shape=[out] * (3 if halo else 1),
        in_specs=[SMEM, SMEM, VMEM, SMEM, HBM, VMEM, VMEM, VMEM, VMEM, HBM]
        + ([HBM] * 6 + [VMEM] if halo else []),
        out_specs=[VMEM] * (3 if halo else 1),
        scratch_shapes=scratch,
        compiler_params=pltpu.CompilerParams(vmem_limit_bytes=MEDIUM if halo else LIMIT),
        cost_estimate=pl.CostEstimate(flops=n * 150_000_000, bytes_accessed=n * 100_000, transcendentals=0),
    )(ids, partner, partner, rate, features, weight_u, lever, slot, owner, own.reshape((tx * ty, rows, beads)), *(around if halo else []))


def rotation_rows(q):
    w, a, b, c = q
    return [
        [1 - 2 * (b * b + c * c), 2 * (a * b - w * c), 2 * (a * c + w * b)],
        [2 * (a * b + w * c), 1 - 2 * (a * a + c * c), 2 * (b * c - w * a)],
        [2 * (a * c - w * b), 2 * (b * c + w * a), 1 - 2 * (a * a + b * b)],
    ]


def integrate(q, motion, inverse, f):
    vel = [motion[r] + STEP_DT * inverse[0] * f[r] for r in range(3)]
    ang = [motion[3 + r] + STEP_DT * f[3 + r] for r in range(3)]
    old = rotation_rows(q)
    frame = [sum(old[r][c] * ang[r] for r in range(3)) * inverse[1 + c] for c in range(3)]
    om = [sum(old[r][c] * frame[c] for c in range(3)) for r in range(3)]
    w, x, y, z = q
    rate = [
        -(om[0] * x + om[1] * y + om[2] * z),
        w * om[0] + om[1] * z - om[2] * y,
        w * om[1] + om[2] * x - om[0] * z,
        w * om[2] + om[0] * y - om[1] * x,
    ]
    step = [q[r] + 0.5 * STEP_DT * rate[r] for r in range(4)]
    size = jnp.sqrt(sum(s * s for s in step))
    new = [s / size for s in step]
    turned = rotation_rows(new)
    rel = [sum(turned[r][k] * old[c][k] for k in range(3)) for r in range(3) for c in range(3)]
    return new, vel, ang, [STEP_DT * v for v in vel] + rel


def finish_kernel(count, *refs):
    sums, refs = refs[:count], refs[count:]
    finish_body(sums, *refs)


def finish_body(sums, pose, motion, inverse, col_a, col_b, end_a, end_b, pos, lever, slot, owner,
                  moved, state, table):
    tx, ty = pos.shape[0], pos.shape[2]
    slots = owner.shape[2]
    high_x, high_y = outward("gx"), outward("gy")
    turn = lambda d, high: 1 + jnp.where(high, d, -d)
    rows_a, rows_b = end_a.shape[0] - 3 * BODY, col_a.shape[0] - BODY
    bodies = {(1, 0): (col_a, rows_b), (1, 2): (col_b, rows_b)}
    for a, end in ((0, end_a), (2, end_b)):
        for q, b in enumerate((1, 0, 2)):
            bodies[a, b] = (end, rows_a + q * BODY)
    if len(sums) == 1:
        totals = lambda b, a: sums[0][a, b]
    else:
        cols, other, got = sums
        totals = lambda b, a: (other[1, b] + cols[0, b] + got[2, b], cols[1, b] + other[0, b] + got[0, b],
                               got[1, b] + cols[2, b])[a]
    for a in range(3):
        for b in range(3):
            f = totals(b, a)
            f = [f[r : r + 1] for r in range(6)]
            if (a, b) == (1, 1):
                q = [pose[0, 3 + r] for r in range(4)]
                mot = [motion[0, r] for r in range(6)]
                inv = [inverse[0, 0, r : r + 1, :] for r in range(4)]
            else:
                ref, at = bodies[a, b]
                third = BODY // 3
                body = sum(ref[at + k * third : at + (k + 1) * third, :].astype(F32) for k in range(3))
                body = [body[r : r + 1] for r in range(14)]
                q, mot, inv = body[0:4], body[4:10], body[10:14]
            new, vel, ang, packed = integrate(q, mot, inv, f)
            if (a, b) == (1, 1):
                centre = [pose[0, r] + STEP_DT * vel[r] for r in range(3)]
                for r, val in enumerate(centre + new + vel + ang):
                    state[0, r] = val
            packed = jnp.concatenate(packed + [jnp.zeros((4, slots), F32)], axis=0)
            table[a, b] = jnp.concatenate(split_two(packed), axis=0)

    def place(i, j, a, b):
        key = owner[i, pl.ds(j, 1), :] * slots + slot[i, pl.ds(j, 1), :]
        rows = table[1, 1] if a == 0 and b == 0 else table[turn(a, high_x), turn(b, high_y)]
        got = jnp.dot(rows, one_hot(key, slots, (3 * a + b + 4) * slots), preferred_element_type=F32)
        got = got[0:16] + got[16:32]
        lev = [lever[i, c, pl.ds(j, 1), :] for c in range(3)]
        return [got[r : r + 1] + sum(got[3 + 3 * r + c : 4 + 3 * r + c] * lev[c] for c in range(3)) for r in range(3)]

    def line(i, carry):
        for j in range(ty):
            for r, val in enumerate(place(i, j, 0, 0)):
                moved[i, r, j : j + 1, :] = pos[i, r, j : j + 1, :].astype(F32) + val - lever[i, r, j : j + 1, :]
        return carry

    lax.fori_loop(0, tx, line, 0, unroll=UNROLL)
    for a, b in DIRS:
        for i in range(tx) if a == 0 else [0 if a < 0 else tx - 1]:
            for j in range(ty) if b == 0 else [0 if b < 0 else ty - 1]:
                for r, val in enumerate(place(i, j, a, b)):
                    moved[i, r, j : j + 1, :] = moved[i, r, j : j + 1, :] + val


def finish(sums, pose, motion, inverse, cols, ends, pos, lever, slot, owner):
    slots = pose.shape[3]
    return pl.pallas_call(
        lambda *refs: finish_kernel(len(sums), *refs),
        out_shape=[jax.ShapeDtypeStruct(lever.shape, F32), jax.ShapeDtypeStruct((1, 13, 1, slots), F32)],
        in_specs=[VMEM] * (11 + len(sums)),
        out_specs=[VMEM] * 2,
        scratch_shapes=[pltpu.VMEM((3, 3, 32, slots), BF16)],
        compiler_params=pltpu.CompilerParams(vmem_limit_bytes=SMALL),
    )(*sums, pose, motion, inverse, *cols, *ends, pos, lever, slot, owner)


def swap(value, axis, start):
    n = lax.axis_size(axis)
    route = []
    for c in range(start, n + start, 2):
        route += [(c % n, (c + 1) % n), ((c + 1) % n, c % n)]
    return lax.ppermute(value, axis, route)


def inside(value, axis):
    return swap(value, axis, 0)


def outside(value, axis):
    return swap(value, axis, 1)


def local(positions, features, lever, partner, body_slot, owner_dir, body_pose, body_motion,
          body_inverse, weight_u, weight_v, radial_rate):
    tx, ty = positions.shape[0], positions.shape[1]
    slots = body_pose.shape[3]
    rows = positions.shape[3] + EXTRA
    pos, lever = (jnp.transpose(v, (0, 2, 1, 3)) for v in (positions, lever))
    pose, motion = (jnp.transpose(v, (0, 2, 1, 3)) for v in (body_pose, body_motion))
    codes = jnp.transpose(partner, (2, 0, 1))
    own, col_in, col_out, row_in, row_out = project(features, pos, weight_v, pose, motion, body_inverse)
    line_a, line_b = inside(row_in, "gx"), outside(row_out, "gx")
    col_a, col_b = inside(col_in, "gy"), outside(col_out, "gy")
    high_x = outward("gx")
    bodies = [v[tx * rows :] for v in (col_in, col_a, col_b)]
    corner = lambda high: jnp.concatenate(
        [jnp.where(high, v[(tx - 1) * rows : tx * rows], v[:rows]) for v in (col_a, col_b)] + bodies, axis=0)
    end_a, end_b = inside(corner(~high_x), "gx"), outside(corner(high_x), "gx")
    args = (codes, radial_rate, features, weight_u, lever, body_slot, owner_dir, slots)
    inner = [((i,), range(1, ty - 1)) for i in range(1, tx - 1)]
    rim = [((0,), range(ty)), ((tx - 1,), range(ty)), (range(1, tx - 1), (0,)), (range(1, tx - 1), (ty - 1,))]
    (first,) = pairs(inner, False, args, own, None)
    parts = pairs(rim, True, args, own, [col_a, col_b, line_a, line_b, end_a, end_b, first])
    mine = parts[1] + inside(parts[0], "gy")
    got = outside(jnp.stack([parts[2], mine]), "gy")
    mine = mine + got[0]
    cols = jnp.stack([inside(mine, "gy"), mine, got[1] + parts[2]], axis=1)
    if lax.axis_size("gx") == 4:
        other = inside(cols, "gx")
        got = outside(jnp.stack([cols[2], cols[1] + other[0], other[2]]), "gx")
        sums = [cols, other, got]
    else:
        mine = cols[1] + inside(cols[0], "gx")
        got = outside(jnp.stack([cols[2], mine]), "gx")
        mine = mine + got[0]
        sums = [jnp.stack([inside(mine, "gx"), mine, got[1] + cols[2]])]
    moved, state = finish(sums, pose, motion, body_inverse, (col_a, col_b), (end_a, end_b),
                          pos, lever, body_slot, owner_dir)
    return (jnp.transpose(moved, (0, 2, 1, 3)), jnp.transpose(state, (0, 2, 1, 3)))


def solution(mesh):
    placed = (
        P("gx", "gy", None, None),
        P("gx", "gy", None, None),
        P("gx", "gy", None, None),
        P("gx", "gy", None),
        P("gx", "gy", None),
        P("gx", "gy", None),
        P("gx", "gy", None, None),
        P("gx", "gy", None, None),
        P("gx", "gy", None, None),
        P(),
        P(),
        P(),
    )
    return jax.shard_map(
        local,
        mesh=mesh,
        in_specs=placed,
        out_specs=(P("gx", "gy", None, None), P("gx", "gy", None, None)),
        check_vma=False,
    )
```

```python
import math
import jax
import jax.numpy as jnp
from jax import lax
from jax.experimental import pallas as pl
from jax.experimental.pallas import tpu as pltpu
from jax.sharding import PartitionSpec as P

STEP_DT = 0.25
CUT_SQUARE = 4.0
F32 = jnp.float32
BF16 = jnp.bfloat16
VMEM = pl.BlockSpec(memory_space=pltpu.VMEM)
SMEM = pl.BlockSpec(memory_space=pltpu.SMEM)
HBM = pl.BlockSpec(memory_space=pl.ANY)
LIMIT = 56 * 2**20
MEDIUM = 24 * 2**20
SMALL = 16 * 2**20
DIRS = [(-1, -1), (-1, 0), (-1, 1), (0, -1), (0, 1), (1, -1), (1, 0), (1, 1)]
EXTRA = 16
BODY = 48
UNROLL = 4
STEP = 4


def rows_iota(rows, lanes):
    return lax.broadcasted_iota(jnp.int32, (rows, lanes), 0)


def split_two(value):
    high = value.astype(BF16)
    return high, (value - high.astype(F32)).astype(BF16)


def one_hot(keys, slots, base):
    hit = rows_iota(slots, keys.shape[-1]) == keys - base
    return jnp.where(hit, 1.0, 0.0).astype(BF16)


def outward(axis):
    return lax.rem(lax.axis_index(axis), 2) == 1


def split_three(value):
    first = value.astype(BF16)
    rest = value - first.astype(F32)
    second = rest.astype(BF16)
    return first, second, (rest - second.astype(F32)).astype(BF16)


def project_kernel(feat, pos, weight_v, pose, motion, inverse, own, col_in, col_out, row_in, row_out):
    x = pl.program_id(0)
    tiles_x, tiles_y, beads = pl.num_programs(0), feat.shape[1], feat.shape[3]
    rows = beads + EXTRA
    step = feat.shape[0]
    second = jnp.where(rows_iota(8, beads) < 3, 1.0, 0.0)
    high_x, high_y = outward("gx"), outward("gy")
    for z in range(step):
        for y in range(0, tiles_y, 2):
            both = jnp.concatenate([feat[z, y], feat[z, y + 1]], axis=1)
            v = jnp.dot(weight_v[...], both, preferred_element_type=F32).astype(BF16)
            for e in range(2):
                own[z, y + e, 0:beads, :] = v[:, e * beads : (e + 1) * beads].T
        px, py, pz = (pos[z, c].astype(F32) for c in range(3))
        norm = -0.25 * (px * px + py * py + pz * pz)
        none = jnp.zeros_like(px)
        parts = [px, py, pz, none, none] + [part.astype(F32) for part in split_three(norm)]
        for y in range(tiles_y):
            first = jnp.concatenate([part[y : y + 1] for part in parts], axis=0)
            own[z, y, beads:rows, :] = jnp.concatenate([first, second], axis=0).astype(BF16)
        at = pl.ds(pl.multiple_of((x * step + z) * rows, 16), rows)
        low, high = own[z, 0], own[z, tiles_y - 1]
        col_in[at, :] = jnp.where(high_y, low, high)
        col_out[at, :] = jnp.where(high_y, high, low)

    def put(row, z):
        for y in range(tiles_y):
            row[y * rows : (y + 1) * rows, :] = own[z, y]

    @pl.when(x == 0)
    def _():
        @pl.when(high_x)
        def _():
            put(row_in, 0)

        @pl.when(~high_x)
        def _():
            put(row_out, 0)

    @pl.when(x == tiles_x - 1)
    def _():
        @pl.when(high_x)
        def _():
            put(row_out, step - 1)

        @pl.when(~high_x)
        def _():
            put(row_in, step - 1)

    @pl.when(x == 0)
    def _():
        body = jnp.concatenate(
            [pose[0, r] for r in range(3, 7)] + [motion[0, r] for r in range(6)]
            + [inverse[0, 0, r : r + 1, :] for r in range(4)] + [jnp.zeros((2, beads), F32)], axis=0)
        body = jnp.concatenate(split_three(body), axis=0)
        for message in (col_in, col_out, row_in, row_out):
            message[message.shape[0] - BODY :, :] = body


def project(features, pos, weight_v, pose, motion, inverse):
    tx, ty, f, beads = features.shape
    rows = beads + EXTRA
    whole = lambda s: pl.BlockSpec(s, lambda i: (0,) * len(s))
    sds = lambda *s: jax.ShapeDtypeStruct(s, BF16)
    col, line = (tx * rows + BODY, beads), (ty * rows + BODY, beads)
    return pl.pallas_call(
        project_kernel,
        grid=(tx // STEP,),
        out_shape=[sds(tx, ty, rows, beads), sds(*col), sds(*col), sds(*line), sds(*line)],
        in_specs=[
            pl.BlockSpec((STEP, ty, f, beads), lambda i: (i, 0, 0, 0)),
            pl.BlockSpec((STEP, 3, ty, beads), lambda i: (i, 0, 0, 0)),
            whole(weight_v.shape), whole(pose.shape), whole(motion.shape), whole(inverse.shape),
        ],
        out_specs=[
            pl.BlockSpec((STEP, ty, rows, beads), lambda i: (i, 0, 0, 0)),
            whole(col), whole(col), whole(line), whole(line),
        ],
        compiler_params=pltpu.CompilerParams(vmem_limit_bytes=LIMIT),
    )(features, pos, weight_v, pose, motion, inverse)


def pairs_kernel(strips, halo, shape, *refs):
    tiles = [(i, j) for rows, cols in strips for i in rows for j in cols]
    n = len(tiles)
    tx, ty, beads, width_h, chans, nb, slots = shape
    refs = list(refs)
    take = lambda k: [refs.pop(0) for _ in range(k)]
    ids, partner, codes, rate, features, weight_u, lever, slot, owner, own = take(10)
    around = take(7) if halo else []
    sums = take(3 if halo else 1)
    table, where_to, tsem = take(3)
    shift_of, norm_of, terms = take(3)
    sets = [take(7), take(7)]
    vp, vsem, total, parts = take(4) if halo else (own, None, sums[0], None)
    wide = ty + 2
    here = lambda i, j: (i + 1) * wide + j + 1 if halo else i * ty + j
    side = chans * width_h

    if halo:
        rows = beads + EXTRA
        high_x, high_y = outward("gx"), outward("gy")
        x_in, x_out = jnp.where(high_x, 0, tx + 1), jnp.where(high_x, tx + 1, 0)
        y_in, y_out = jnp.where(high_y, 0, ty + 1), jnp.where(high_y, ty + 1, 0)
        line = lambda i: vp.at[pl.ds(i * wide + 1, ty)]
        cols, lines, ends = around[0:2], around[2:4], around[4:6]
        pairs_of = []
        for i in range(tx):
            for col, y in zip(cols, (y_in, y_out)):
                pairs_of.append((col.at[pl.ds(i * rows, rows)], vp.at[(i + 1) * wide + y]))
            pairs_of.append((own.at[i * ty : (i + 1) * ty], line(i + 1)))
        for src, end, x in zip(lines, ends, (x_in, x_out)):
            for y in range(ty):
                pairs_of.append((src.at[pl.ds(y * rows, rows)], vp.at[x * wide + 1 + y]))
            pairs_of.append((end.at[pl.ds(0, rows)], vp.at[x * wide + y_in]))
            pairs_of.append((end.at[pl.ds(rows, rows)], vp.at[x * wide + y_out]))
        copies = [pltpu.make_async_copy(src, dst, vsem.at[q]) for q, (src, dst) in enumerate(pairs_of)]
        for copy in copies:
            copy.start()
    total[...] = around[6][...] if halo else jnp.zeros_like(total)

    def where_is(t):
        return lax.div(ids[t], jnp.int32(ty)), lax.rem(ids[t], jnp.int32(ty))

    both = codes.shape
    code = codes[...]
    a = lax.shift_right_logical(code * 11, 5)
    pitch = wide if halo else ty
    first = lax.broadcasted_iota(jnp.int32, both, 1) * pitch + lax.broadcasted_iota(jnp.int32, both, 2)
    table[:, :, 0:ty] = first + (a - 1) * pitch + code - 3 * a - 1 + (wide + 1 if halo else 0)
    tables = pltpu.make_async_copy(table, where_to, tsem)
    tables.start()

    row8 = rows_iota(8, beads)
    row16 = rows_iota(EXTRA, beads)
    for c in range(9):
        a, b = c // 3 - 1, c % 3 - 1
        shift_of[c] = jnp.where(row16 == 3, 1.0 * a, jnp.where(row16 == 4, 1.0 * b, 0.0)).astype(BF16)
        for q, val in enumerate((-0.5 * a, -0.5 * b, -0.25 * (a * a + b * b))):
            norm_of[c, q] = jnp.full((8, beads), val, F32)

    def make_u(s, ub):
        (i, j), (k, l) = where_is(2 * s), where_is(2 * s + 1)
        both = jnp.concatenate([features[i, j], features[k, l]], axis=1)
        u = jnp.dot(weight_u[...], both, preferred_element_type=F32).astype(BF16)
        for e in range(2):
            for k in range(chans):
                ub[e, :, k * beads : (k + 1) * beads] = u[
                    k * width_h : (k + 1) * width_h, e * beads : (e + 1) * beads]

    def moved_block(i, j, m):
        return vp[where_to[m, i, j], beads : beads + EXTRA, :] + shift_of[partner[m, i, j]]

    def products(t, ub, e, buf, g):
        cols = slice(2 * g * beads, 2 * (g + 1) * beads)
        i, j = where_is(t)
        lhs = jnp.concatenate([vp[where_to[m, i, j], 0:beads, :] for m in range(nb)], axis=0)
        buf[:, cols] = jnp.dot(lhs, ub[e, :, cols], preferred_element_type=F32)

    def scores(t, ub, e, buf, zbuf):
        i, j = where_is(t)
        up = vp[here(i, j), beads : beads + EXTRA, :].astype(F32)[0:8]
        px, py = (jnp.broadcast_to(0.5 * up[c : c + 1], (8, beads)) for c in (0, 1))
        high = jnp.where(row8 < 3, 0.5 * up, jnp.where(row8 == 3, px, jnp.where(row8 == 4, py, 1.0)))
        low = jnp.where(row8 < 3, pltpu.roll(up, 3, 0), 0.0)
        mine = jnp.concatenate([high, low], axis=0).astype(BF16)
        none = jnp.zeros_like(mine)
        mine = jnp.concatenate([jnp.concatenate([mine, none], axis=1), jnp.concatenate([none, mine], axis=1)], axis=0)
        feats = []
        for m in range(nb):
            code = partner[m, i, j]
            block = moved_block(i, j, m).astype(F32)
            up = block[0:8]
            qx, qy = (jnp.broadcast_to(up[c : c + 1], (8, beads)) for c in (0, 1))
            norm = jnp.broadcast_to(up[5:6] + up[6:7] + up[7:8], (8, beads)) + norm_of[code, 2]
            norm = norm + qx * norm_of[code, 0] + qy * norm_of[code, 1]
            n1 = norm.astype(BF16).astype(F32)
            rest = norm - n1
            n2 = rest.astype(BF16).astype(F32)
            high = jnp.where(row8 < 5, up, jnp.where(row8 == 5, n1, jnp.where(row8 == 6, n2, rest - n2)))
            feats.append(jnp.concatenate([high, block[8:16]], axis=0).astype(BF16))
        left = jnp.concatenate([jnp.concatenate(feats[h::2], axis=1) for h in range(2)], axis=0)
        zbuf[...] = lax.dot_general(left, mine, (((0,), (0,)), ((), ())), preferred_element_type=F32)

    def couples(buf, zbuf, cbuf, which):
        step = 16
        for m in which:
            for r in range(0, beads, step):
                z = zbuf[m // 2 * beads + r : m // 2 * beads + r + step, (m % 2) * beads : (m % 2 + 1) * beads]
                env = jnp.maximum(1.0 + z, 0.0)
                total = None
                for k in range(chans):
                    part = jnp.exp2(z * (rate[k] * (CUT_SQUARE / math.log(2.0)))) * buf[
                        m * beads + r : m * beads + r + step, k * beads : (k + 1) * beads]
                    total = part if total is None else total + part
                cbuf[m * beads + r : m * beads + r + step, :] = ((env * env) * total).astype(BF16)

    def gather(t, cbuf):
        i, j = where_is(t)
        lhs = jnp.concatenate([moved_block(i, j, m) for m in range(nb)], axis=1)
        out = jnp.dot(lhs, cbuf[...], preferred_element_type=F32) * (1.0 / width_h)
        mine = vp[here(i, j), beads : beads + EXTRA, :].astype(F32)
        w = out[8:9]
        fx = mine[0:1] * w - out[0:1] - out[3:4]
        fy = mine[1:2] * w - out[1:2] - out[4:5]
        fz = mine[2:3] * w - out[2:3]
        lx, ly, lz = (lever[i, c, pl.ds(j, 1), :] for c in range(3))
        value = jnp.concatenate(
            [fx, fy, fz, ly * fz - lz * fy, lz * fx - lx * fz, lx * fy - ly * fx,
             jnp.zeros((2, beads), F32)], axis=0)
        term = jnp.concatenate(split_two(value), axis=0)
        terms[t] = term

    def add_up(s):
        left, right = [], []
        for t in (2 * s, 2 * s + 1):
            i, j = where_is(t)
            key = owner[i, pl.ds(j, 1), :] * slots + slot[i, pl.ds(j, 1), :]
            left.append(terms[t])
            right.append(one_hot(key, slots, 4 * slots))
        got = lax.dot_general(jnp.concatenate(left, axis=1), jnp.concatenate(right, axis=1),
                              (((1,), (1,)), ((), ())), preferred_element_type=F32)
        return got[0:8] + got[8:16]

    last = n // 2 - 1

    def fill(s, into):
        ub, sa, sb, za, zb, _, _ = into
        scores(2 * s, ub, 0, sa, za)
        scores(2 * s + 1, ub, 1, sb, zb)
        for g in range(chans // 2):
            products(2 * s, ub, 0, sa, g)
            products(2 * s + 1, ub, 1, sb, g)

    def half(s, now, later):
        _, sa, sb, za, zb, ca, cb = now
        before = jnp.maximum(s - 1, 0)
        nxt = jnp.minimum(s + 1, last)
        scores(2 * nxt + 0, later[0], 0, later[1], later[3])
        products(2 * nxt + 0, later[0], 0, later[1], 0)
        couples(sa, za, ca, range(0, 3))
        products(2 * nxt + 0, later[0], 0, later[1], 1)
        couples(sa, za, ca, range(3, 6))
        scores(2 * nxt + 1, later[0], 1, later[2], later[4])
        products(2 * nxt + 1, later[0], 1, later[2], 0)
        couples(sb, zb, cb, range(0, 3))
        products(2 * nxt + 1, later[0], 1, later[2], 1)
        couples(sb, zb, cb, range(3, 6))
        make_u(jnp.minimum(s + 2, last), now[0])
        gather(2 * before, later[5])
        gather(2 * before + 1, later[6])
        total[...] = total[...] + jnp.where(s == 0, 0.0, add_up(before))

    make_u(0, sets[0][0])
    make_u(min(1, last), sets[1][0])
    if halo:
        for copy in copies:
            copy.wait()
    tables.wait()
    fill(0, sets[0])

    def body(g, carry):
        half(2 * g, sets[0], sets[1])
        half(2 * g + 1, sets[1], sets[0])
        return carry

    lax.fori_loop(0, n // 4, body, 0)
    gather(n - 2, sets[1][5])
    gather(n - 1, sets[1][6])
    total[...] = total[...] + add_up(last)
    if halo:
        turn = lambda d, high: 1 + jnp.where(high, d, -d)
        parts[1, 1] = total[...]
        for a, b in DIRS:
            keep = [t for t, (i, j) in enumerate(tiles)
                    if (a == 0 or i == (0 if a < 0 else tx - 1)) and (b == 0 or j == (0 if b < 0 else ty - 1))]
            left, right = [], []
            for t in keep:
                i, j = tiles[t]
                key = owner[i, j : j + 1, :] * slots + slot[i, j : j + 1, :]
                left.append(terms[t])
                right.append(one_hot(key, slots, (3 * a + b + 4) * slots))
            got = lax.dot_general(jnp.concatenate(left, axis=1), jnp.concatenate(right, axis=1),
                                  (((1,), (1,)), ((), ())), preferred_element_type=F32)
            parts[turn(b, high_y), turn(a, high_x)] = got[0:8] + got[8:16]
        for q in range(3):
            sums[q][...] = parts[q]


def pairs(strips, halo, args, own, around):
    tiles = [(i, j) for rows, cols in strips for i in rows for j in cols]
    partner, rate, features, weight_u, lever, slot, owner, slots = args
    tx, ty, f, beads = features.shape
    nb = partner.shape[0]
    chans = rate.shape[0]
    width_h = weight_u.shape[0] // chans
    rows = beads + EXTRA
    n = len(tiles)
    out = jax.ShapeDtypeStruct((3, 8, slots) if halo else (8, slots), F32)
    scratch = [
        pltpu.VMEM((nb, tx, beads), jnp.int32),
        pltpu.SMEM((nb, tx, beads), jnp.int32),
        pltpu.SemaphoreType.DMA,
        pltpu.VMEM((9, EXTRA, beads), BF16),
        pltpu.VMEM((9, 3, 8, beads), F32),
        pltpu.VMEM((n, 16, beads), BF16),
    ]
    scratch += 2 * [
        pltpu.VMEM((2, width_h, chans * beads), BF16),
        pltpu.VMEM((nb * beads, chans * beads), F32),
        pltpu.VMEM((nb * beads, chans * beads), F32),
        pltpu.VMEM((nb // 2 * beads, 2 * beads), F32),
        pltpu.VMEM((nb // 2 * beads, 2 * beads), F32),
        pltpu.VMEM((nb * beads, beads), BF16),
        pltpu.VMEM((nb * beads, beads), BF16),
    ]
    if halo:
        scratch += [pltpu.VMEM(((tx + 2) * (ty + 2), rows, beads), BF16), pltpu.SemaphoreType.DMA((3 * tx + 2 * ty + 4,)),
                    pltpu.VMEM((8, slots), F32), pltpu.VMEM((3, 3, 8, slots), F32)]
    ids = jnp.asarray([i * ty + j for i, j in tiles], jnp.int32)
    shape = (tx, ty, beads, width_h, chans, nb, slots)
    return pl.pallas_call(
        lambda *refs: pairs_kernel(strips, halo, shape, *refs),
        out_shape=[out] * (3 if halo else 1),
        in_specs=[SMEM, SMEM, VMEM, SMEM, VMEM, VMEM, VMEM, VMEM, VMEM, HBM if halo else VMEM]
        + ([HBM] * 6 + [VMEM] if halo else []),
        out_specs=[VMEM] * (3 if halo else 1),
        scratch_shapes=scratch,
        compiler_params=pltpu.CompilerParams(vmem_limit_bytes=MEDIUM),
        cost_estimate=pl.CostEstimate(flops=n * 150_000_000, bytes_accessed=n * 100_000, transcendentals=0),
    )(ids, partner, partner, rate, features, weight_u, lever, slot, owner, own.reshape((tx * ty, rows, beads)), *(around if halo else []))


def rotation_rows(q):
    w, a, b, c = q
    return [
        [1 - 2 * (b * b + c * c), 2 * (a * b - w * c), 2 * (a * c + w * b)],
        [2 * (a * b + w * c), 1 - 2 * (a * a + c * c), 2 * (b * c - w * a)],
        [2 * (a * c - w * b), 2 * (b * c + w * a), 1 - 2 * (a * a + b * b)],
    ]


def integrate(q, motion, inverse, f):
    vel = [motion[r] + STEP_DT * inverse[0] * f[r] for r in range(3)]
    ang = [motion[3 + r] + STEP_DT * f[3 + r] for r in range(3)]
    old = rotation_rows(q)
    frame = [sum(old[r][c] * ang[r] for r in range(3)) * inverse[1 + c] for c in range(3)]
    om = [sum(old[r][c] * frame[c] for c in range(3)) for r in range(3)]
    w, x, y, z = q
    rate = [
        -(om[0] * x + om[1] * y + om[2] * z),
        w * om[0] + om[1] * z - om[2] * y,
        w * om[1] + om[2] * x - om[0] * z,
        w * om[2] + om[0] * y - om[1] * x,
    ]
    step = [q[r] + 0.5 * STEP_DT * rate[r] for r in range(4)]
    size = jnp.sqrt(sum(s * s for s in step))
    new = [s / size for s in step]
    turned = rotation_rows(new)
    rel = [sum(turned[r][k] * old[c][k] for k in range(3)) for r in range(3) for c in range(3)]
    return new, vel, ang, [STEP_DT * v for v in vel] + rel


def finish_kernel(count, *refs):
    sums, refs = refs[:count], refs[count:]
    finish_body(sums, *refs)


def finish_body(sums, pose, motion, inverse, col_a, col_b, line_a, line_b, end_a, end_b, pos, lever, slot, owner,
                moved, state, table):
    tx, ty = pos.shape[0], pos.shape[2]
    slots = owner.shape[2]
    high_x, high_y = outward("gx"), outward("gy")
    turn = lambda d, high: 1 + jnp.where(high, d, -d)
    bodies = {}
    for (a, b), ref in {(1, 0): col_a, (1, 2): col_b, (0, 1): line_a, (2, 1): line_b, (0, 2): end_a, (2, 2): end_b}.items():
        bodies[a, b] = (ref, ref.shape[0] - BODY)
    for a, ref in ((0, end_a), (2, end_b)):
        bodies[a, 0] = (ref, ref.shape[0] - 2 * BODY)
    if len(sums) == 1:
        totals = lambda b, a: sums[0][a, b]
    else:
        cols, other, got = sums
        totals = lambda b, a: (other[1, b] + cols[0, b] + got[2, b], cols[1, b] + other[0, b] + got[0, b],
                               got[1, b] + cols[2, b])[a]
    for a in range(3):
        for b in range(3):
            f = totals(b, a)
            f = [f[r : r + 1] for r in range(6)]
            if (a, b) == (1, 1):
                q = [pose[0, 3 + r] for r in range(4)]
                mot = [motion[0, r] for r in range(6)]
                inv = [inverse[0, 0, r : r + 1, :] for r in range(4)]
            else:
                ref, at = bodies[a, b]
                third = BODY // 3
                body = sum(ref[at + k * third : at + (k + 1) * third, :].astype(F32) for k in range(3))
                body = [body[r : r + 1] for r in range(14)]
                q, mot, inv = body[0:4], body[4:10], body[10:14]
            new, vel, ang, packed = integrate(q, mot, inv, f)
            if (a, b) == (1, 1):
                centre = [pose[0, r] + STEP_DT * vel[r] for r in range(3)]
                for r, val in enumerate(centre + new + vel + ang):
                    state[0, r] = val
            packed = jnp.concatenate(packed + [jnp.zeros((4, slots), F32)], axis=0)
            table[a, b] = jnp.concatenate(split_two(packed), axis=0)

    def place(i, j, a, b):
        key = owner[i, pl.ds(j, 1), :] * slots + slot[i, pl.ds(j, 1), :]
        rows = table[1, 1] if a == 0 and b == 0 else table[turn(a, high_x), turn(b, high_y)]
        got = jnp.dot(rows, one_hot(key, slots, (3 * a + b + 4) * slots), preferred_element_type=F32)
        got = got[0:16] + got[16:32]
        lev = [lever[i, c, pl.ds(j, 1), :] for c in range(3)]
        return [got[r : r + 1] + sum(got[3 + 3 * r + c : 4 + 3 * r + c] * lev[c] for c in range(3)) for r in range(3)]

    def line(i, carry):
        for j in range(ty):
            for r, val in enumerate(place(i, j, 0, 0)):
                moved[i, r, j : j + 1, :] = pos[i, r, j : j + 1, :].astype(F32) + val - lever[i, r, j : j + 1, :]
        return carry

    lax.fori_loop(0, tx, line, 0, unroll=UNROLL)
    for a, b in DIRS:
        for i in range(tx) if a == 0 else [0 if a < 0 else tx - 1]:
            for j in range(ty) if b == 0 else [0 if b < 0 else ty - 1]:
                for r, val in enumerate(place(i, j, a, b)):
                    moved[i, r, j : j + 1, :] = moved[i, r, j : j + 1, :] + val


def finish(sums, pose, motion, inverse, cols, lines, ends, pos, lever, slot, owner):
    slots = pose.shape[3]
    return pl.pallas_call(
        lambda *refs: finish_kernel(len(sums), *refs),
        out_shape=[jax.ShapeDtypeStruct(lever.shape, F32), jax.ShapeDtypeStruct((1, 13, 1, slots), F32)],
        in_specs=[VMEM] * (13 + len(sums)),
        out_specs=[VMEM] * 2,
        scratch_shapes=[pltpu.VMEM((3, 3, 32, slots), BF16)],
        compiler_params=pltpu.CompilerParams(vmem_limit_bytes=SMALL),
    )(*sums, pose, motion, inverse, *cols, *lines, *ends, pos, lever, slot, owner)


def corner_kernel(col_a, col_b, end_in, end_out):
    rows = (end_in.shape[0] - 2 * BODY) // 2
    last = col_a.shape[0] - BODY - rows
    high = outward("gx")
    for q, col in enumerate((col_a, col_b)):
        first, final = col[0:rows, :], col[last : last + rows, :]
        end_in[q * rows : (q + 1) * rows, :] = jnp.where(high, first, final)
        end_out[q * rows : (q + 1) * rows, :] = jnp.where(high, final, first)
    for q, col in enumerate((col_a, col_b)):
        body = col[last + rows :, :]
        at = 2 * rows + q * BODY
        end_in[at : at + BODY, :] = body
        end_out[at : at + BODY, :] = body


def corners(col_a, col_b, rows):
    out = jax.ShapeDtypeStruct((2 * (rows + BODY), col_a.shape[1]), BF16)
    return pl.pallas_call(
        corner_kernel,
        out_shape=[out] * 2,
        in_specs=[VMEM] * 2,
        out_specs=[VMEM] * 2,
        compiler_params=pltpu.CompilerParams(vmem_limit_bytes=SMALL),
    )(col_a, col_b)


def swap(value, axis, start):
    n = lax.axis_size(axis)
    route = []
    for c in range(start, n + start, 2):
        route += [(c % n, (c + 1) % n), ((c + 1) % n, c % n)]
    return lax.ppermute(value, axis, route)


def inside(value, axis):
    return swap(value, axis, 0)


def outside(value, axis):
    return swap(value, axis, 1)


def local(positions, features, lever, partner, body_slot, owner_dir, body_pose, body_motion,
          body_inverse, weight_u, weight_v, radial_rate):
    tx, ty = positions.shape[0], positions.shape[1]
    slots = body_pose.shape[3]
    rows = positions.shape[3] + EXTRA
    pos, lever = (jnp.transpose(v, (0, 2, 1, 3)) for v in (positions, lever))
    pose, motion = (jnp.transpose(v, (0, 2, 1, 3)) for v in (body_pose, body_motion))
    codes = jnp.transpose(partner, (2, 0, 1))
    own, col_in, col_out, row_in, row_out = project(features, pos, weight_v, pose, motion, body_inverse)
    line_a, line_b = inside(row_in, "gx"), outside(row_out, "gx")
    col_a, col_b = inside(col_in, "gy"), outside(col_out, "gy")
    end_in, end_out = corners(col_a, col_b, rows)
    end_a, end_b = inside(end_in, "gx"), outside(end_out, "gx")
    args = (codes, radial_rate, features, weight_u, lever, body_slot, owner_dir, slots)
    inner = [((i,), range(1, ty - 1)) for i in range(1, tx - 1)]
    rim = [((0,), range(ty)), ((tx - 1,), range(ty)), (range(1, tx - 1), (0,)), (range(1, tx - 1), (ty - 1,))]
    (first,) = pairs(inner, False, args, own, None)
    parts = pairs(rim, True, args, own, [col_a, col_b, line_a, line_b, end_a, end_b, first])
    mine = parts[1] + inside(parts[0], "gy")
    got = outside(jnp.stack([parts[2], mine]), "gy")
    mine = mine + got[0]
    cols = jnp.stack([inside(mine, "gy"), mine, got[1] + parts[2]], axis=1)
    if lax.axis_size("gx") == 4:
        other = inside(cols, "gx")
        got = outside(jnp.stack([cols[2], cols[1] + other[0], other[2]]), "gx")
        sums = [cols, other, got]
    else:
        mine = cols[1] + inside(cols[0], "gx")
        got = outside(jnp.stack([cols[2], mine]), "gx")
        mine = mine + got[0]
        sums = [jnp.stack([inside(mine, "gx"), mine, got[1] + cols[2]])]
    moved, state = finish(sums, pose, motion, body_inverse, (col_a, col_b), (line_a, line_b), (end_a, end_b),
                          pos, lever, body_slot, owner_dir)
    return (jnp.transpose(moved, (0, 2, 1, 3)), jnp.transpose(state, (0, 2, 1, 3)))


def solution(mesh):
    placed = (
        P("gx", "gy", None, None),
        P("gx", "gy", None, None),
        P("gx", "gy", None, None),
        P("gx", "gy", None),
        P("gx", "gy", None),
        P("gx", "gy", None),
        P("gx", "gy", None, None),
        P("gx", "gy", None, None),
        P("gx", "gy", None, None),
        P(),
        P(),
        P(),
    )
    return jax.shard_map(
        local,
        mesh=mesh,
        in_specs=placed,
        out_specs=(P("gx", "gy", None, None), P("gx", "gy", None, None)),
        check_vma=False,
    )
```

```python
import math
import jax
import jax.numpy as jnp
from jax import lax
from jax.experimental import pallas as pl
from jax.experimental.pallas import tpu as pltpu
from jax.sharding import PartitionSpec as P

STEP_DT = 0.25
CUT_SQUARE = 4.0
F32 = jnp.float32
BF16 = jnp.bfloat16
VMEM = pl.BlockSpec(memory_space=pltpu.VMEM)
SMEM = pl.BlockSpec(memory_space=pltpu.SMEM)
HBM = pl.BlockSpec(memory_space=pl.ANY)
LIMIT = 56 * 2**20
MEDIUM = 24 * 2**20
SMALL = 16 * 2**20
DIRS = [(-1, -1), (-1, 0), (-1, 1), (0, -1), (0, 1), (1, -1), (1, 0), (1, 1)]
EXTRA = 16
BODY = 48
UNROLL = 4
STEP = 4


def rows_iota(rows, lanes):
    return lax.broadcasted_iota(jnp.int32, (rows, lanes), 0)


def split_two(value):
    high = value.astype(BF16)
    return high, (value - high.astype(F32)).astype(BF16)


def one_hot(keys, slots, base):
    hit = rows_iota(slots, keys.shape[-1]) == keys - base
    return jnp.where(hit, 1.0, 0.0).astype(BF16)


def outward(axis):
    return lax.rem(lax.axis_index(axis), 2) == 1


def split_three(value):
    first = value.astype(BF16)
    rest = value - first.astype(F32)
    second = rest.astype(BF16)
    return first, second, (rest - second.astype(F32)).astype(BF16)


def project_kernel(feat, pos, weight_v, pose, motion, inverse, own, col_in, col_out, row_in, row_out):
    x = pl.program_id(0)
    tiles_x, tiles_y, beads = pl.num_programs(0), feat.shape[1], feat.shape[3]
    rows = beads + EXTRA
    step = feat.shape[0]
    second = jnp.where(rows_iota(8, beads) < 3, 1.0, 0.0)
    high_x, high_y = outward("gx"), outward("gy")
    for z in range(step):
        for y in range(0, tiles_y, 2):
            both = jnp.concatenate([feat[z, y], feat[z, y + 1]], axis=1)
            v = jnp.dot(weight_v[...], both, preferred_element_type=F32).astype(BF16)
            for e in range(2):
                own[z, y + e, 0:beads, :] = v[:, e * beads : (e + 1) * beads].T
        px, py, pz = (pos[z, c].astype(F32) for c in range(3))
        norm = -0.25 * (px * px + py * py + pz * pz)
        none = jnp.zeros_like(px)
        parts = [px, py, pz, none, none] + [part.astype(F32) for part in split_three(norm)]
        for y in range(tiles_y):
            first = jnp.concatenate([part[y : y + 1] for part in parts], axis=0)
            own[z, y, beads:rows, :] = jnp.concatenate([first, second], axis=0).astype(BF16)
        at = pl.ds(pl.multiple_of((x * step + z) * rows, 16), rows)
        low, high = own[z, 0], own[z, tiles_y - 1]
        col_in[at, :] = jnp.where(high_y, low, high)
        col_out[at, :] = jnp.where(high_y, high, low)

    def put(row, z):
        for y in range(tiles_y):
            row[y * rows : (y + 1) * rows, :] = own[z, y]

    @pl.when(x == 0)
    def _():
        @pl.when(high_x)
        def _():
            put(row_in, 0)

        @pl.when(~high_x)
        def _():
            put(row_out, 0)

    @pl.when(x == tiles_x - 1)
    def _():
        @pl.when(high_x)
        def _():
            put(row_out, step - 1)

        @pl.when(~high_x)
        def _():
            put(row_in, step - 1)

    @pl.when(x == 0)
    def _():
        body = jnp.concatenate(
            [pose[0, r] for r in range(3, 7)] + [motion[0, r] for r in range(6)]
            + [inverse[0, 0, r : r + 1, :] for r in range(4)] + [jnp.zeros((2, beads), F32)], axis=0)
        body = jnp.concatenate(split_three(body), axis=0)
        for message in (col_in, col_out, row_in, row_out):
            message[message.shape[0] - BODY :, :] = body


def project(features, pos, weight_v, pose, motion, inverse):
    tx, ty, f, beads = features.shape
    rows = beads + EXTRA
    whole = lambda s: pl.BlockSpec(s, lambda i: (0,) * len(s))
    sds = lambda *s: jax.ShapeDtypeStruct(s, BF16)
    col, line = (tx * rows + BODY, beads), (ty * rows + BODY, beads)
    return pl.pallas_call(
        project_kernel,
        grid=(tx // STEP,),
        out_shape=[sds(tx, ty, rows, beads), sds(*col), sds(*col), sds(*line), sds(*line)],
        in_specs=[
            pl.BlockSpec((STEP, ty, f, beads), lambda i: (i, 0, 0, 0)),
            pl.BlockSpec((STEP, 3, ty, beads), lambda i: (i, 0, 0, 0)),
            whole(weight_v.shape), whole(pose.shape), whole(motion.shape), whole(inverse.shape),
        ],
        out_specs=[
            pl.BlockSpec((STEP, ty, rows, beads), lambda i: (i, 0, 0, 0)),
            whole(col), whole(col), whole(line), whole(line),
        ],
        compiler_params=pltpu.CompilerParams(vmem_limit_bytes=LIMIT),
    )(features, pos, weight_v, pose, motion, inverse)


def pairs_kernel(strips, halo, shape, *refs):
    tiles = [(i, j) for rows, cols in strips for i in rows for j in cols]
    n = len(tiles)
    tx, ty, beads, width_h, chans, nb, slots = shape
    refs = list(refs)
    take = lambda k: [refs.pop(0) for _ in range(k)]
    ids, partner, codes, rate, features, weight_u, lever, slot, owner, own = take(10)
    around = take(7) if halo else []
    sums = take(3 if halo else 1)
    table, where_to, tsem = take(3)
    shift_of, norm_of, terms = take(3)
    sets = [take(7), take(7)]
    vp, vsem, total, parts = take(4) if halo else (own, None, sums[0], None)
    wide = ty + 2
    here = lambda i, j: (i + 1) * wide + j + 1 if halo else i * ty + j
    side = chans * width_h

    if halo:
        rows = beads + EXTRA
        high_x, high_y = outward("gx"), outward("gy")
        x_in, x_out = jnp.where(high_x, 0, tx + 1), jnp.where(high_x, tx + 1, 0)
        y_in, y_out = jnp.where(high_y, 0, ty + 1), jnp.where(high_y, ty + 1, 0)
        line = lambda i: vp.at[pl.ds(i * wide + 1, ty)]
        cols, lines, ends = around[0:2], around[2:4], around[4:6]
        pairs_of = []
        for i in range(tx):
            for col, y in zip(cols, (y_in, y_out)):
                pairs_of.append((col.at[pl.ds(i * rows, rows)], vp.at[(i + 1) * wide + y]))
            pairs_of.append((own.at[i * ty : (i + 1) * ty], line(i + 1)))
        for src, end, x in zip(lines, ends, (x_in, x_out)):
            for y in range(ty):
                pairs_of.append((src.at[pl.ds(y * rows, rows)], vp.at[x * wide + 1 + y]))
            pairs_of.append((end.at[pl.ds(0, rows)], vp.at[x * wide + y_in]))
            pairs_of.append((end.at[pl.ds(rows, rows)], vp.at[x * wide + y_out]))
        copies = [pltpu.make_async_copy(src, dst, vsem.at[q]) for q, (src, dst) in enumerate(pairs_of)]
        for copy in copies:
            copy.start()
    total[...] = around[6][...] if halo else jnp.zeros_like(total)

    def where_is(t):
        return lax.div(ids[t], jnp.int32(ty)), lax.rem(ids[t], jnp.int32(ty))

    both = codes.shape
    code = codes[...]
    a = lax.shift_right_logical(code * 11, 5)
    pitch = wide if halo else ty
    first = lax.broadcasted_iota(jnp.int32, both, 1) * pitch + lax.broadcasted_iota(jnp.int32, both, 2)
    table[:, :, 0:ty] = first + (a - 1) * pitch + code - 3 * a - 1 + (wide + 1 if halo else 0)
    tables = pltpu.make_async_copy(table, where_to, tsem)
    tables.start()

    row8 = rows_iota(8, beads)
    row16 = rows_iota(EXTRA, beads)
    for c in range(9):
        a, b = c // 3 - 1, c % 3 - 1
        shift_of[c] = jnp.where(row16 == 3, 1.0 * a, jnp.where(row16 == 4, 1.0 * b, 0.0)).astype(BF16)
        for q, val in enumerate((-0.5 * a, -0.5 * b, -0.25 * (a * a + b * b))):
            norm_of[c, q] = jnp.full((8, beads), val, F32)

    def make_u(s, ub):
        (i, j), (k, l) = where_is(2 * s), where_is(2 * s + 1)
        both = jnp.concatenate([features[i, j], features[k, l]], axis=1)
        u = jnp.dot(weight_u[...], both, preferred_element_type=F32).astype(BF16)
        for e in range(2):
            for k in range(chans):
                ub[e, :, k * beads : (k + 1) * beads] = u[
                    k * width_h : (k + 1) * width_h, e * beads : (e + 1) * beads]

    def moved_block(i, j, m):
        return vp[where_to[m, i, j], beads : beads + EXTRA, :] + shift_of[partner[m, i, j]]

    def products(t, ub, e, buf, g):
        cols = slice(2 * g * beads, 2 * (g + 1) * beads)
        i, j = where_is(t)
        lhs = jnp.concatenate([vp[where_to[m, i, j], 0:beads, :] for m in range(nb)], axis=0)
        buf[:, cols] = jnp.dot(lhs, ub[e, :, cols], preferred_element_type=F32)

    def scores(t, ub, e, buf, zbuf):
        i, j = where_is(t)
        up = vp[here(i, j), beads : beads + EXTRA, :].astype(F32)[0:8]
        px, py = (jnp.broadcast_to(0.5 * up[c : c + 1], (8, beads)) for c in (0, 1))
        high = jnp.where(row8 < 3, 0.5 * up, jnp.where(row8 == 3, px, jnp.where(row8 == 4, py, 1.0)))
        low = jnp.where(row8 < 3, pltpu.roll(up, 3, 0), 0.0)
        mine = jnp.concatenate([high, low], axis=0).astype(BF16)
        none = jnp.zeros_like(mine)
        mine = jnp.concatenate([jnp.concatenate([mine, none], axis=1), jnp.concatenate([none, mine], axis=1)], axis=0)
        feats = []
        for m in range(nb):
            code = partner[m, i, j]
            block = moved_block(i, j, m).astype(F32)
            up = block[0:8]
            qx, qy = (jnp.broadcast_to(up[c : c + 1], (8, beads)) for c in (0, 1))
            norm = jnp.broadcast_to(up[5:6] + up[6:7] + up[7:8], (8, beads)) + norm_of[code, 2]
            norm = norm + qx * norm_of[code, 0] + qy * norm_of[code, 1]
            n1 = norm.astype(BF16).astype(F32)
            rest = norm - n1
            n2 = rest.astype(BF16).astype(F32)
            high = jnp.where(row8 < 5, up, jnp.where(row8 == 5, n1, jnp.where(row8 == 6, n2, rest - n2)))
            feats.append(jnp.concatenate([high, block[8:16]], axis=0).astype(BF16))
        left = jnp.concatenate([jnp.concatenate(feats[h::2], axis=1) for h in range(2)], axis=0)
        zbuf[...] = lax.dot_general(left, mine, (((0,), (0,)), ((), ())), preferred_element_type=F32)

    def couples(buf, zbuf, cbuf, which):
        step = 16
        for m in which:
            for r in range(0, beads, step):
                z = zbuf[m // 2 * beads + r : m // 2 * beads + r + step, (m % 2) * beads : (m % 2 + 1) * beads]
                env = jnp.maximum(1.0 + z, 0.0)
                total = None
                for k in range(chans):
                    part = jnp.exp2(z * (rate[k] * (CUT_SQUARE / math.log(2.0)))) * buf[
                        m * beads + r : m * beads + r + step, k * beads : (k + 1) * beads]
                    total = part if total is None else total + part
                cbuf[m * beads + r : m * beads + r + step, :] = ((env * env) * total).astype(BF16)

    def gather(t, cbuf):
        i, j = where_is(t)
        lhs = jnp.concatenate([moved_block(i, j, m) for m in range(nb)], axis=1)
        out = jnp.dot(lhs, cbuf[...], preferred_element_type=F32) * (1.0 / width_h)
        mine = vp[here(i, j), beads : beads + EXTRA, :].astype(F32)
        w = out[8:9]
        fx = mine[0:1] * w - out[0:1] - out[3:4]
        fy = mine[1:2] * w - out[1:2] - out[4:5]
        fz = mine[2:3] * w - out[2:3]
        lx, ly, lz = (lever[i, c, pl.ds(j, 1), :] for c in range(3))
        value = jnp.concatenate(
            [fx, fy, fz, ly * fz - lz * fy, lz * fx - lx * fz, lx * fy - ly * fx,
             jnp.zeros((2, beads), F32)], axis=0)
        term = jnp.concatenate(split_two(value), axis=0)
        terms[t] = term

    def add_up(s):
        left, right = [], []
        for t in (2 * s, 2 * s + 1):
            i, j = where_is(t)
            key = owner[i, pl.ds(j, 1), :] * slots + slot[i, pl.ds(j, 1), :]
            left.append(terms[t])
            right.append(one_hot(key, slots, 4 * slots))
        got = lax.dot_general(jnp.concatenate(left, axis=1), jnp.concatenate(right, axis=1),
                              (((1,), (1,)), ((), ())), preferred_element_type=F32)
        return got[0:8] + got[8:16]

    last = n // 2 - 1

    def fill(s, into):
        ub, sa, sb, za, zb, _, _ = into
        scores(2 * s, ub, 0, sa, za)
        scores(2 * s + 1, ub, 1, sb, zb)
        for g in range(chans // 2):
            products(2 * s, ub, 0, sa, g)
            products(2 * s + 1, ub, 1, sb, g)

    def half(s, now, later):
        _, sa, sb, za, zb, ca, cb = now
        before = jnp.maximum(s - 1, 0)
        nxt = jnp.minimum(s + 1, last)
        scores(2 * nxt + 0, later[0], 0, later[1], later[3])
        products(2 * nxt + 0, later[0], 0, later[1], 0)
        couples(sa, za, ca, range(0, 3))
        products(2 * nxt + 0, later[0], 0, later[1], 1)
        couples(sa, za, ca, range(3, 6))
        scores(2 * nxt + 1, later[0], 1, later[2], later[4])
        products(2 * nxt + 1, later[0], 1, later[2], 0)
        couples(sb, zb, cb, range(0, 3))
        products(2 * nxt + 1, later[0], 1, later[2], 1)
        couples(sb, zb, cb, range(3, 6))
        make_u(jnp.minimum(s + 2, last), now[0])
        gather(2 * before, later[5])
        gather(2 * before + 1, later[6])
        total[...] = total[...] + jnp.where(s == 0, 0.0, add_up(before))

    make_u(0, sets[0][0])
    make_u(min(1, last), sets[1][0])
    if halo:
        for copy in copies:
            copy.wait()
    tables.wait()
    fill(0, sets[0])

    def body(g, carry):
        half(2 * g, sets[0], sets[1])
        half(2 * g + 1, sets[1], sets[0])
        return carry

    lax.fori_loop(0, n // 4, body, 0)
    gather(n - 2, sets[1][5])
    gather(n - 1, sets[1][6])
    total[...] = total[...] + add_up(last)
    if halo:
        turn = lambda d, high: 1 + jnp.where(high, d, -d)
        parts[1, 1] = total[...]
        for a, b in DIRS:
            keep = [t for t, (i, j) in enumerate(tiles)
                    if (a == 0 or i == (0 if a < 0 else tx - 1)) and (b == 0 or j == (0 if b < 0 else ty - 1))]
            left, right = [], []
            for t in keep:
                i, j = tiles[t]
                key = owner[i, j : j + 1, :] * slots + slot[i, j : j + 1, :]
                left.append(terms[t])
                right.append(one_hot(key, slots, (3 * a + b + 4) * slots))
            got = lax.dot_general(jnp.concatenate(left, axis=1), jnp.concatenate(right, axis=1),
                                  (((1,), (1,)), ((), ())), preferred_element_type=F32)
            parts[turn(b, high_y), turn(a, high_x)] = got[0:8] + got[8:16]
        for q in range(3):
            sums[q][...] = parts[q]


def pairs(strips, halo, args, own, around):
    tiles = [(i, j) for rows, cols in strips for i in rows for j in cols]
    partner, rate, features, weight_u, lever, slot, owner, slots = args
    tx, ty, f, beads = features.shape
    nb = partner.shape[0]
    chans = rate.shape[0]
    width_h = weight_u.shape[0] // chans
    rows = beads + EXTRA
    n = len(tiles)
    out = jax.ShapeDtypeStruct((3, 8, slots) if halo else (8, slots), F32)
    scratch = [
        pltpu.VMEM((nb, tx, beads), jnp.int32),
        pltpu.SMEM((nb, tx, beads), jnp.int32),
        pltpu.SemaphoreType.DMA,
        pltpu.VMEM((9, EXTRA, beads), BF16),
        pltpu.VMEM((9, 3, 8, beads), F32),
        pltpu.VMEM((n, 16, beads), BF16),
    ]
    scratch += 2 * [
        pltpu.VMEM((2, width_h, chans * beads), BF16),
        pltpu.VMEM((nb * beads, chans * beads), F32),
        pltpu.VMEM((nb * beads, chans * beads), F32),
        pltpu.VMEM((nb // 2 * beads, 2 * beads), F32),
        pltpu.VMEM((nb // 2 * beads, 2 * beads), F32),
        pltpu.VMEM((nb * beads, beads), BF16),
        pltpu.VMEM((nb * beads, beads), BF16),
    ]
    if halo:
        scratch += [pltpu.VMEM(((tx + 2) * (ty + 2), rows, beads), BF16), pltpu.SemaphoreType.DMA((3 * tx + 2 * ty + 4,)),
                    pltpu.VMEM((8, slots), F32), pltpu.VMEM((3, 3, 8, slots), F32)]
    ids = jnp.asarray([i * ty + j for i, j in tiles], jnp.int32)
    shape = (tx, ty, beads, width_h, chans, nb, slots)
    return pl.pallas_call(
        lambda *refs: pairs_kernel(strips, halo, shape, *refs),
        out_shape=[out] * (3 if halo else 1),
        in_specs=[SMEM, SMEM, VMEM, SMEM, VMEM, VMEM, VMEM, VMEM, VMEM, HBM if halo else VMEM]
        + ([HBM] * 6 + [VMEM] if halo else []),
        out_specs=[VMEM] * (3 if halo else 1),
        scratch_shapes=scratch,
        compiler_params=pltpu.CompilerParams(vmem_limit_bytes=MEDIUM),
        cost_estimate=pl.CostEstimate(flops=n * 150_000_000, bytes_accessed=n * 100_000, transcendentals=0),
    )(ids, partner, partner, rate, features, weight_u, lever, slot, owner, own.reshape((tx * ty, rows, beads)), *(around if halo else []))


def rotation_rows(q):
    w, a, b, c = q
    return [
        [1 - 2 * (b * b + c * c), 2 * (a * b - w * c), 2 * (a * c + w * b)],
        [2 * (a * b + w * c), 1 - 2 * (a * a + c * c), 2 * (b * c - w * a)],
        [2 * (a * c - w * b), 2 * (b * c + w * a), 1 - 2 * (a * a + b * b)],
    ]


def integrate(q, motion, inverse, f):
    vel = [motion[r] + STEP_DT * inverse[0] * f[r] for r in range(3)]
    ang = [motion[3 + r] + STEP_DT * f[3 + r] for r in range(3)]
    old = rotation_rows(q)
    frame = [sum(old[r][c] * ang[r] for r in range(3)) * inverse[1 + c] for c in range(3)]
    om = [sum(old[r][c] * frame[c] for c in range(3)) for r in range(3)]
    w, x, y, z = q
    rate = [
        -(om[0] * x + om[1] * y + om[2] * z),
        w * om[0] + om[1] * z - om[2] * y,
        w * om[1] + om[2] * x - om[0] * z,
        w * om[2] + om[0] * y - om[1] * x,
    ]
    step = [q[r] + 0.5 * STEP_DT * rate[r] for r in range(4)]
    size = jnp.sqrt(sum(s * s for s in step))
    new = [s / size for s in step]
    turned = rotation_rows(new)
    rel = [sum(turned[r][k] * old[c][k] for k in range(3)) for r in range(3) for c in range(3)]
    return new, vel, ang, [STEP_DT * v for v in vel] + rel


def finish_kernel(count, *refs):
    sums, refs = refs[:count], refs[count:]
    finish_body(sums, *refs)


def finish_body(sums, pose, motion, inverse, col_a, col_b, line_a, line_b, end_a, end_b, pos, lever, slot, owner,
                moved, state, table):
    tx, ty = pos.shape[0], pos.shape[2]
    slots = owner.shape[2]
    high_x, high_y = outward("gx"), outward("gy")
    turn = lambda d, high: 1 + jnp.where(high, d, -d)
    bodies = {}
    for (a, b), ref in {(1, 0): col_a, (1, 2): col_b, (0, 1): line_a, (2, 1): line_b, (0, 2): end_a, (2, 2): end_b}.items():
        bodies[a, b] = (ref, ref.shape[0] - BODY)
    for a, ref in ((0, end_a), (2, end_b)):
        bodies[a, 0] = (ref, ref.shape[0] - 2 * BODY)
    if len(sums) == 1:
        totals = lambda b, a: sums[0][a, b]
    else:
        cols, other, got = sums
        totals = lambda b, a: (other[1, b] + cols[0, b] + got[2, b], cols[1, b] + other[0, b] + got[0, b],
                               got[1, b] + cols[2, b])[a]
    for a in range(3):
        for b in range(3):
            f = totals(b, a)
            f = [f[r : r + 1] for r in range(6)]
            if (a, b) == (1, 1):
                q = [pose[0, 3 + r] for r in range(4)]
                mot = [motion[0, r] for r in range(6)]
                inv = [inverse[0, 0, r : r + 1, :] for r in range(4)]
            else:
                ref, at = bodies[a, b]
                third = BODY // 3
                body = sum(ref[at + k * third : at + (k + 1) * third, :].astype(F32) for k in range(3))
                body = [body[r : r + 1] for r in range(14)]
                q, mot, inv = body[0:4], body[4:10], body[10:14]
            new, vel, ang, packed = integrate(q, mot, inv, f)
            if (a, b) == (1, 1):
                centre = [pose[0, r] + STEP_DT * vel[r] for r in range(3)]
                for r, val in enumerate(centre + new + vel + ang):
                    state[0, r] = val
            packed = jnp.concatenate(packed + [jnp.zeros((4, slots), F32)], axis=0)
            table[a, b] = jnp.concatenate(split_two(packed), axis=0)

    def place(i, j, a, b):
        key = owner[i, pl.ds(j, 1), :] * slots + slot[i, pl.ds(j, 1), :]
        rows = table[1, 1] if a == 0 and b == 0 else table[turn(a, high_x), turn(b, high_y)]
        got = jnp.dot(rows, one_hot(key, slots, (3 * a + b + 4) * slots), preferred_element_type=F32)
        got = got[0:16] + got[16:32]
        lev = [lever[i, c, pl.ds(j, 1), :] for c in range(3)]
        return [got[r : r + 1] + sum(got[3 + 3 * r + c : 4 + 3 * r + c] * lev[c] for c in range(3)) for r in range(3)]

    def line(i, carry):
        for j in range(ty):
            for r, val in enumerate(place(i, j, 0, 0)):
                moved[i, r, j : j + 1, :] = pos[i, r, j : j + 1, :].astype(F32) + val - lever[i, r, j : j + 1, :]
        return carry

    lax.fori_loop(0, tx, line, 0, unroll=UNROLL)
    for a, b in DIRS:
        for i in range(tx) if a == 0 else [0 if a < 0 else tx - 1]:
            for j in range(ty) if b == 0 else [0 if b < 0 else ty - 1]:
                for r, val in enumerate(place(i, j, a, b)):
                    moved[i, r, j : j + 1, :] = moved[i, r, j : j + 1, :] + val


def finish(sums, pose, motion, inverse, cols, lines, ends, pos, lever, slot, owner):
    slots = pose.shape[3]
    return pl.pallas_call(
        lambda *refs: finish_kernel(len(sums), *refs),
        out_shape=[jax.ShapeDtypeStruct(lever.shape, F32), jax.ShapeDtypeStruct((1, 13, 1, slots), F32)],
        in_specs=[VMEM] * (13 + len(sums)),
        out_specs=[VMEM] * 2,
        scratch_shapes=[pltpu.VMEM((3, 3, 32, slots), BF16)],
        compiler_params=pltpu.CompilerParams(vmem_limit_bytes=SMALL),
    )(*sums, pose, motion, inverse, *cols, *lines, *ends, pos, lever, slot, owner)


def corner_kernel(col_a, col_b, end_in, end_out):
    rows = (end_in.shape[0] - 2 * BODY) // 2
    last = col_a.shape[0] - BODY - rows
    high = outward("gx")
    for q, col in enumerate((col_a, col_b)):
        first, final = col[0:rows, :], col[last : last + rows, :]
        end_in[q * rows : (q + 1) * rows, :] = jnp.where(high, first, final)
        end_out[q * rows : (q + 1) * rows, :] = jnp.where(high, final, first)
    for q, col in enumerate((col_a, col_b)):
        body = col[last + rows :, :]
        at = 2 * rows + q * BODY
        end_in[at : at + BODY, :] = body
        end_out[at : at + BODY, :] = body


def corners(col_a, col_b, rows):
    out = jax.ShapeDtypeStruct((2 * (rows + BODY), col_a.shape[1]), BF16)
    return pl.pallas_call(
        corner_kernel,
        out_shape=[out] * 2,
        in_specs=[VMEM] * 2,
        out_specs=[VMEM] * 2,
        compiler_params=pltpu.CompilerParams(vmem_limit_bytes=SMALL),
        cost_estimate=pl.CostEstimate(flops=8_000_000_000, bytes_accessed=20_000_000, transcendentals=0),
    )(col_a, col_b)


def swap(value, axis, start):
    n = lax.axis_size(axis)
    route = []
    for c in range(start, n + start, 2):
        route += [(c % n, (c + 1) % n), ((c + 1) % n, c % n)]
    return lax.ppermute(value, axis, route)


def inside(value, axis):
    return swap(value, axis, 0)


def outside(value, axis):
    return swap(value, axis, 1)


def local(positions, features, lever, partner, body_slot, owner_dir, body_pose, body_motion,
          body_inverse, weight_u, weight_v, radial_rate):
    tx, ty = positions.shape[0], positions.shape[1]
    slots = body_pose.shape[3]
    rows = positions.shape[3] + EXTRA
    pos, lever = (jnp.transpose(v, (0, 2, 1, 3)) for v in (positions, lever))
    pose, motion = (jnp.transpose(v, (0, 2, 1, 3)) for v in (body_pose, body_motion))
    codes = jnp.transpose(partner, (2, 0, 1))
    own, col_in, col_out, row_in, row_out = project(features, pos, weight_v, pose, motion, body_inverse)
    line_a, line_b = inside(row_in, "gx"), outside(row_out, "gx")
    col_a, col_b = inside(col_in, "gy"), outside(col_out, "gy")
    end_in, end_out = corners(col_a, col_b, rows)
    end_a, end_b = inside(end_in, "gx"), outside(end_out, "gx")
    args = (codes, radial_rate, features, weight_u, lever, body_slot, owner_dir, slots)
    inner = [((i,), range(1, ty - 1)) for i in range(1, tx - 1)]
    rim = [((0,), range(ty)), ((tx - 1,), range(ty)), (range(1, tx - 1), (0,)), (range(1, tx - 1), (ty - 1,))]
    (first,) = pairs(inner, False, args, own, None)
    parts = pairs(rim, True, args, own, [col_a, col_b, line_a, line_b, end_a, end_b, first])
    mine = parts[1] + inside(parts[0], "gy")
    got = outside(jnp.stack([parts[2], mine]), "gy")
    mine = mine + got[0]
    cols = jnp.stack([inside(mine, "gy"), mine, got[1] + parts[2]], axis=1)
    if lax.axis_size("gx") == 4:
        other = inside(cols, "gx")
        got = outside(jnp.stack([cols[2], cols[1] + other[0], other[2]]), "gx")
        sums = [cols, other, got]
    else:
        mine = cols[1] + inside(cols[0], "gx")
        got = outside(jnp.stack([cols[2], mine]), "gx")
        mine = mine + got[0]
        sums = [jnp.stack([inside(mine, "gx"), mine, got[1] + cols[2]])]
    moved, state = finish(sums, pose, motion, body_inverse, (col_a, col_b), (line_a, line_b), (end_a, end_b),
                          pos, lever, body_slot, owner_dir)
    return (jnp.transpose(moved, (0, 2, 1, 3)), jnp.transpose(state, (0, 2, 1, 3)))


def solution(mesh):
    placed = (
        P("gx", "gy", None, None),
        P("gx", "gy", None, None),
        P("gx", "gy", None, None),
        P("gx", "gy", None),
        P("gx", "gy", None),
        P("gx", "gy", None),
        P("gx", "gy", None, None),
        P("gx", "gy", None, None),
        P("gx", "gy", None, None),
        P(),
        P(),
        P(),
    )
    return jax.shard_map(
        local,
        mesh=mesh,
        in_specs=placed,
        out_specs=(P("gx", "gy", None, None), P("gx", "gy", None, None)),
        check_vma=False,
    )
```

```python
import math
import jax
import jax.numpy as jnp
from jax import lax
from jax.experimental import pallas as pl
from jax.experimental.pallas import tpu as pltpu
from jax.sharding import PartitionSpec as P

STEP_DT = 0.25
CUT_SQUARE = 4.0
F32 = jnp.float32
BF16 = jnp.bfloat16
VMEM = pl.BlockSpec(memory_space=pltpu.VMEM)
SMEM = pl.BlockSpec(memory_space=pltpu.SMEM)
HBM = pl.BlockSpec(memory_space=pl.ANY)
LIMIT = 56 * 2**20
MEDIUM = 24 * 2**20
SMALL = 16 * 2**20
DIRS = [(-1, -1), (-1, 0), (-1, 1), (0, -1), (0, 1), (1, -1), (1, 0), (1, 1)]
EXTRA = 16
BODY = 48
UNROLL = 4
STEP = 4


def rows_iota(rows, lanes):
    return lax.broadcasted_iota(jnp.int32, (rows, lanes), 0)


def split_two(value):
    high = value.astype(BF16)
    return high, (value - high.astype(F32)).astype(BF16)


def one_hot(keys, slots, base):
    hit = rows_iota(slots, keys.shape[-1]) == keys - base
    return jnp.where(hit, 1.0, 0.0).astype(BF16)


def outward(axis):
    return lax.rem(lax.axis_index(axis), 2) == 1


def split_three(value):
    first = value.astype(BF16)
    rest = value - first.astype(F32)
    second = rest.astype(BF16)
    return first, second, (rest - second.astype(F32)).astype(BF16)


def project_kernel(feat, pos, weight_v, pose, motion, inverse, own, col_in, ends_out, col_out, row_in, row_out):
    x = pl.program_id(0)
    tiles_x, tiles_y, beads = pl.num_programs(0), feat.shape[1], feat.shape[3]
    rows = beads + EXTRA
    step = feat.shape[0]
    second = jnp.where(rows_iota(8, beads) < 3, 1.0, 0.0)
    high_x, high_y = outward("gx"), outward("gy")
    for z in range(step):
        for y in range(0, tiles_y, 2):
            both = jnp.concatenate([feat[z, y], feat[z, y + 1]], axis=1)
            v = jnp.dot(weight_v[...], both, preferred_element_type=F32).astype(BF16)
            for e in range(2):
                own[z, y + e, 0:beads, :] = v[:, e * beads : (e + 1) * beads].T
        px, py, pz = (pos[z, c].astype(F32) for c in range(3))
        norm = -0.25 * (px * px + py * py + pz * pz)
        none = jnp.zeros_like(px)
        parts = [px, py, pz, none, none] + [part.astype(F32) for part in split_three(norm)]
        for y in range(tiles_y):
            first = jnp.concatenate([part[y : y + 1] for part in parts], axis=0)
            own[z, y, beads:rows, :] = jnp.concatenate([first, second], axis=0).astype(BF16)
        at = pl.ds(pl.multiple_of((x * step + z) * rows, 16), rows)
        low, high = own[z, 0], own[z, tiles_y - 1]
        col_in[at, :] = jnp.where(high_y, low, high)
        col_out[at, :] = jnp.where(high_y, high, low)

    def put(row, z):
        for y in range(tiles_y):
            row[y * rows : (y + 1) * rows, :] = own[z, y]

    @pl.when(x == 0)
    def _():
        ends_out[0:rows, :] = jnp.where(high_y, own[0, tiles_y - 1], own[0, 0])

        @pl.when(high_x)
        def _():
            put(row_in, 0)

        @pl.when(~high_x)
        def _():
            put(row_out, 0)

    @pl.when(x == tiles_x - 1)
    def _():
        ends_out[rows : 2 * rows, :] = jnp.where(high_y, own[step - 1, tiles_y - 1], own[step - 1, 0])

        @pl.when(high_x)
        def _():
            put(row_out, step - 1)

        @pl.when(~high_x)
        def _():
            put(row_in, step - 1)

    @pl.when(x == 0)
    def _():
        body = jnp.concatenate(
            [pose[0, r] for r in range(3, 7)] + [motion[0, r] for r in range(6)]
            + [inverse[0, 0, r : r + 1, :] for r in range(4)] + [jnp.zeros((2, beads), F32)], axis=0)
        body = jnp.concatenate(split_three(body), axis=0)
        for message in (col_in, ends_out, row_in, row_out):
            message[message.shape[0] - BODY :, :] = body


def project(features, pos, weight_v, pose, motion, inverse):
    tx, ty, f, beads = features.shape
    rows = beads + EXTRA
    whole = lambda s: pl.BlockSpec(s, lambda i: (0,) * len(s))
    sds = lambda *s: jax.ShapeDtypeStruct(s, BF16)
    col, line, end = (tx * rows + BODY, beads), (ty * rows + BODY, beads), (2 * rows + BODY, beads)
    return pl.pallas_call(
        project_kernel,
        grid=(tx // STEP,),
        out_shape=[sds(tx, ty, rows, beads), sds(*col), sds(*end), sds(tx * rows, beads), sds(*line), sds(*line)],
        in_specs=[
            pl.BlockSpec((STEP, ty, f, beads), lambda i: (i, 0, 0, 0)),
            pl.BlockSpec((STEP, 3, ty, beads), lambda i: (i, 0, 0, 0)),
            whole(weight_v.shape), whole(pose.shape), whole(motion.shape), whole(inverse.shape),
        ],
        out_specs=[
            pl.BlockSpec((STEP, ty, rows, beads), lambda i: (i, 0, 0, 0)),
            whole(col), whole(end), whole((tx * rows, beads)), whole(line), whole(line),
        ],
        compiler_params=pltpu.CompilerParams(vmem_limit_bytes=LIMIT),
    )(features, pos, weight_v, pose, motion, inverse)


def pairs_kernel(strips, halo, shape, *refs):
    tiles = [(i, j) for rows, cols in strips for i in rows for j in cols]
    n = len(tiles)
    tx, ty, beads, width_h, chans, nb, slots = shape
    refs = list(refs)
    take = lambda k: [refs.pop(0) for _ in range(k)]
    ids, partner, codes, rate, features, weight_u, lever, slot, owner, own = take(10)
    around = take(7) if halo else []
    sums = take(3 if halo else 1)
    table, where_to, tsem = take(3)
    shift_of, norm_of, terms = take(3)
    sets = [take(7), take(7)]
    vp, vsem, total, parts = take(4) if halo else (own, None, sums[0], None)
    wide = ty + 2
    here = lambda i, j: (i + 1) * wide + j + 1 if halo else i * ty + j
    side = chans * width_h

    if halo:
        rows = beads + EXTRA
        high_x, high_y = outward("gx"), outward("gy")
        x_in, x_out = jnp.where(high_x, 0, tx + 1), jnp.where(high_x, tx + 1, 0)
        y_in, y_out = jnp.where(high_y, 0, ty + 1), jnp.where(high_y, ty + 1, 0)
        line = lambda i: vp.at[pl.ds(i * wide + 1, ty)]
        cols, lines, ends = around[0:2], around[2:4], around[4:6]
        pairs_of = []
        for src, end, x in zip(lines, ends, (x_in, x_out)):
            for y in range(ty):
                pairs_of.append((src.at[pl.ds(y * rows, rows)], vp.at[x * wide + 1 + y]))
            pairs_of.append((end.at[pl.ds(0, rows)], vp.at[x * wide + y_in]))
            pairs_of.append((end.at[pl.ds(rows, rows)], vp.at[x * wide + y_out]))
        for i in range(tx):
            for col, y in zip(cols, (y_in, y_out)):
                pairs_of.append((col.at[pl.ds(i * rows, rows)], vp.at[(i + 1) * wide + y]))
            pairs_of.append((own.at[i * ty : (i + 1) * ty], line(i + 1)))
        early = 2 * (ty + 2) + 6
        copies = [pltpu.make_async_copy(src, dst, vsem.at[q]) for q, (src, dst) in enumerate(pairs_of)]
        for copy in copies:
            copy.start()
    total[...] = around[6][...] if halo else jnp.zeros_like(total)

    def where_is(t):
        return lax.div(ids[t], jnp.int32(ty)), lax.rem(ids[t], jnp.int32(ty))

    both = codes.shape
    code = codes[...]
    a = lax.shift_right_logical(code * 11, 5)
    pitch = wide if halo else ty
    first = lax.broadcasted_iota(jnp.int32, both, 1) * pitch + lax.broadcasted_iota(jnp.int32, both, 2)
    table[:, :, 0:ty] = first + (a - 1) * pitch + code - 3 * a - 1 + (wide + 1 if halo else 0)
    tables = pltpu.make_async_copy(table, where_to, tsem)
    tables.start()

    row8 = rows_iota(8, beads)
    row16 = rows_iota(EXTRA, beads)
    for c in range(9):
        a, b = c // 3 - 1, c % 3 - 1
        shift_of[c] = jnp.where(row16 == 3, 1.0 * a, jnp.where(row16 == 4, 1.0 * b, 0.0)).astype(BF16)
        for q, val in enumerate((-0.5 * a, -0.5 * b, -0.25 * (a * a + b * b))):
            norm_of[c, q] = jnp.full((8, beads), val, F32)

    def make_u(s, ub):
        (i, j), (k, l) = where_is(2 * s), where_is(2 * s + 1)
        both = jnp.concatenate([features[i, j], features[k, l]], axis=1)
        u = jnp.dot(weight_u[...], both, preferred_element_type=F32).astype(BF16)
        for e in range(2):
            for k in range(chans):
                ub[e, :, k * beads : (k + 1) * beads] = u[
                    k * width_h : (k + 1) * width_h, e * beads : (e + 1) * beads]

    def moved_block(i, j, m):
        return vp[where_to[m, i, j], beads : beads + EXTRA, :] + shift_of[partner[m, i, j]]

    def products(t, ub, e, buf, g):
        cols = slice(2 * g * beads, 2 * (g + 1) * beads)
        i, j = where_is(t)
        lhs = jnp.concatenate([vp[where_to[m, i, j], 0:beads, :] for m in range(nb)], axis=0)
        buf[:, cols] = jnp.dot(lhs, ub[e, :, cols], preferred_element_type=F32)

    def scores(t, ub, e, buf, zbuf):
        i, j = where_is(t)
        up = vp[here(i, j), beads : beads + EXTRA, :].astype(F32)[0:8]
        px, py = (jnp.broadcast_to(0.5 * up[c : c + 1], (8, beads)) for c in (0, 1))
        high = jnp.where(row8 < 3, 0.5 * up, jnp.where(row8 == 3, px, jnp.where(row8 == 4, py, 1.0)))
        low = jnp.where(row8 < 3, pltpu.roll(up, 3, 0), 0.0)
        mine = jnp.concatenate([high, low], axis=0).astype(BF16)
        none = jnp.zeros_like(mine)
        mine = jnp.concatenate([jnp.concatenate([mine, none], axis=1), jnp.concatenate([none, mine], axis=1)], axis=0)
        feats = []
        for m in range(nb):
            code = partner[m, i, j]
            block = moved_block(i, j, m).astype(F32)
            up = block[0:8]
            qx, qy = (jnp.broadcast_to(up[c : c + 1], (8, beads)) for c in (0, 1))
            norm = jnp.broadcast_to(up[5:6] + up[6:7] + up[7:8], (8, beads)) + norm_of[code, 2]
            norm = norm + qx * norm_of[code, 0] + qy * norm_of[code, 1]
            n1 = norm.astype(BF16).astype(F32)
            rest = norm - n1
            n2 = rest.astype(BF16).astype(F32)
            high = jnp.where(row8 < 5, up, jnp.where(row8 == 5, n1, jnp.where(row8 == 6, n2, rest - n2)))
            feats.append(jnp.concatenate([high, block[8:16]], axis=0).astype(BF16))
        left = jnp.concatenate([jnp.concatenate(feats[h::2], axis=1) for h in range(2)], axis=0)
        zbuf[...] = lax.dot_general(left, mine, (((0,), (0,)), ((), ())), preferred_element_type=F32)

    def couples(buf, zbuf, cbuf, which):
        step = 16
        for m in which:
            for r in range(0, beads, step):
                z = zbuf[m // 2 * beads + r : m // 2 * beads + r + step, (m % 2) * beads : (m % 2 + 1) * beads]
                env = jnp.maximum(1.0 + z, 0.0)
                total = None
                for k in range(chans):
                    part = jnp.exp2(z * (rate[k] * (CUT_SQUARE / math.log(2.0)))) * buf[
                        m * beads + r : m * beads + r + step, k * beads : (k + 1) * beads]
                    total = part if total is None else total + part
                cbuf[m * beads + r : m * beads + r + step, :] = ((env * env) * total).astype(BF16)

    def gather(t, cbuf):
        i, j = where_is(t)
        lhs = jnp.concatenate([moved_block(i, j, m) for m in range(nb)], axis=1)
        out = jnp.dot(lhs, cbuf[...], preferred_element_type=F32) * (1.0 / width_h)
        mine = vp[here(i, j), beads : beads + EXTRA, :].astype(F32)
        w = out[8:9]
        fx = mine[0:1] * w - out[0:1] - out[3:4]
        fy = mine[1:2] * w - out[1:2] - out[4:5]
        fz = mine[2:3] * w - out[2:3]
        lx, ly, lz = (lever[i, c, pl.ds(j, 1), :] for c in range(3))
        value = jnp.concatenate(
            [fx, fy, fz, ly * fz - lz * fy, lz * fx - lx * fz, lx * fy - ly * fx,
             jnp.zeros((2, beads), F32)], axis=0)
        term = jnp.concatenate(split_two(value), axis=0)
        terms[t] = term

    def add_up(s):
        left, right = [], []
        for t in (2 * s, 2 * s + 1):
            i, j = where_is(t)
            key = owner[i, pl.ds(j, 1), :] * slots + slot[i, pl.ds(j, 1), :]
            left.append(terms[t])
            right.append(one_hot(key, slots, 4 * slots))
        got = lax.dot_general(jnp.concatenate(left, axis=1), jnp.concatenate(right, axis=1),
                              (((1,), (1,)), ((), ())), preferred_element_type=F32)
        return got[0:8] + got[8:16]

    last = n // 2 - 1

    def fill(s, into):
        ub, sa, sb, za, zb, _, _ = into
        scores(2 * s, ub, 0, sa, za)
        scores(2 * s + 1, ub, 1, sb, zb)
        for g in range(chans // 2):
            products(2 * s, ub, 0, sa, g)
            products(2 * s + 1, ub, 1, sb, g)

    def half(s, now, later):
        _, sa, sb, za, zb, ca, cb = now
        before = jnp.maximum(s - 1, 0)
        nxt = jnp.minimum(s + 1, last)
        scores(2 * nxt + 0, later[0], 0, later[1], later[3])
        products(2 * nxt + 0, later[0], 0, later[1], 0)
        couples(sa, za, ca, range(0, 3))
        products(2 * nxt + 0, later[0], 0, later[1], 1)
        couples(sa, za, ca, range(3, 6))
        scores(2 * nxt + 1, later[0], 1, later[2], later[4])
        products(2 * nxt + 1, later[0], 1, later[2], 0)
        couples(sb, zb, cb, range(0, 3))
        products(2 * nxt + 1, later[0], 1, later[2], 1)
        couples(sb, zb, cb, range(3, 6))
        make_u(jnp.minimum(s + 2, last), now[0])
        gather(2 * before, later[5])
        gather(2 * before + 1, later[6])
        total[...] = total[...] + jnp.where(s == 0, 0.0, add_up(before))

    make_u(0, sets[0][0])
    make_u(min(1, last), sets[1][0])
    if halo:
        for copy in copies[:early]:
            copy.wait()
    tables.wait()
    fill(0, sets[0])
    if halo:
        for copy in copies[early:]:
            copy.wait()

    def body(g, carry):
        half(2 * g, sets[0], sets[1])
        half(2 * g + 1, sets[1], sets[0])
        return carry

    lax.fori_loop(0, n // 4, body, 0)
    gather(n - 2, sets[1][5])
    gather(n - 1, sets[1][6])
    total[...] = total[...] + add_up(last)
    if halo:
        turn = lambda d, high: 1 + jnp.where(high, d, -d)
        parts[1, 1] = total[...]
        for a, b in DIRS:
            keep = [t for t, (i, j) in enumerate(tiles)
                    if (a == 0 or i == (0 if a < 0 else tx - 1)) and (b == 0 or j == (0 if b < 0 else ty - 1))]
            left, right = [], []
            for t in keep:
                i, j = tiles[t]
                key = owner[i, j : j + 1, :] * slots + slot[i, j : j + 1, :]
                left.append(terms[t])
                right.append(one_hot(key, slots, (3 * a + b + 4) * slots))
            got = lax.dot_general(jnp.concatenate(left, axis=1), jnp.concatenate(right, axis=1),
                                  (((1,), (1,)), ((), ())), preferred_element_type=F32)
            parts[turn(b, high_y), turn(a, high_x)] = got[0:8] + got[8:16]
        for q in range(3):
            sums[q][...] = parts[q]


def pairs(strips, halo, args, own, around):
    tiles = [(i, j) for rows, cols in strips for i in rows for j in cols]
    partner, rate, features, weight_u, lever, slot, owner, slots = args
    tx, ty, f, beads = features.shape
    nb = partner.shape[0]
    chans = rate.shape[0]
    width_h = weight_u.shape[0] // chans
    rows = beads + EXTRA
    n = len(tiles)
    out = jax.ShapeDtypeStruct((3, 8, slots) if halo else (8, slots), F32)
    scratch = [
        pltpu.VMEM((nb, tx, beads), jnp.int32),
        pltpu.SMEM((nb, tx, beads), jnp.int32),
        pltpu.SemaphoreType.DMA,
        pltpu.VMEM((9, EXTRA, beads), BF16),
        pltpu.VMEM((9, 3, 8, beads), F32),
        pltpu.VMEM((n, 16, beads), BF16),
    ]
    scratch += 2 * [
        pltpu.VMEM((2, width_h, chans * beads), BF16),
        pltpu.VMEM((nb * beads, chans * beads), F32),
        pltpu.VMEM((nb * beads, chans * beads), F32),
        pltpu.VMEM((nb // 2 * beads, 2 * beads), F32),
        pltpu.VMEM((nb // 2 * beads, 2 * beads), F32),
        pltpu.VMEM((nb * beads, beads), BF16),
        pltpu.VMEM((nb * beads, beads), BF16),
    ]
    if halo:
        scratch += [pltpu.VMEM(((tx + 2) * (ty + 2), rows, beads), BF16), pltpu.SemaphoreType.DMA((3 * tx + 2 * ty + 4,)),
                    pltpu.VMEM((8, slots), F32), pltpu.VMEM((3, 3, 8, slots), F32)]
    ids = jnp.asarray([i * ty + j for i, j in tiles], jnp.int32)
    shape = (tx, ty, beads, width_h, chans, nb, slots)
    return pl.pallas_call(
        lambda *refs: pairs_kernel(strips, halo, shape, *refs),
        out_shape=[out] * (3 if halo else 1),
        in_specs=[SMEM, SMEM, VMEM, SMEM, VMEM, VMEM, VMEM, VMEM, VMEM, HBM if halo else VMEM]
        + ([HBM] * 6 + [VMEM] if halo else []),
        out_specs=[VMEM] * (3 if halo else 1),
        scratch_shapes=scratch,
        compiler_params=pltpu.CompilerParams(vmem_limit_bytes=MEDIUM),
        cost_estimate=pl.CostEstimate(flops=n * 150_000_000, bytes_accessed=n * 100_000, transcendentals=0),
    )(ids, partner, partner, rate, features, weight_u, lever, slot, owner, own.reshape((tx * ty, rows, beads)), *(around if halo else []))


def rotation_rows(q):
    w, a, b, c = q
    return [
        [1 - 2 * (b * b + c * c), 2 * (a * b - w * c), 2 * (a * c + w * b)],
        [2 * (a * b + w * c), 1 - 2 * (a * a + c * c), 2 * (b * c - w * a)],
        [2 * (a * c - w * b), 2 * (b * c + w * a), 1 - 2 * (a * a + b * b)],
    ]


def integrate(q, motion, inverse, f):
    vel = [motion[r] + STEP_DT * inverse[0] * f[r] for r in range(3)]
    ang = [motion[3 + r] + STEP_DT * f[3 + r] for r in range(3)]
    old = rotation_rows(q)
    frame = [sum(old[r][c] * ang[r] for r in range(3)) * inverse[1 + c] for c in range(3)]
    om = [sum(old[r][c] * frame[c] for c in range(3)) for r in range(3)]
    w, x, y, z = q
    rate = [
        -(om[0] * x + om[1] * y + om[2] * z),
        w * om[0] + om[1] * z - om[2] * y,
        w * om[1] + om[2] * x - om[0] * z,
        w * om[2] + om[0] * y - om[1] * x,
    ]
    step = [q[r] + 0.5 * STEP_DT * rate[r] for r in range(4)]
    size = jnp.sqrt(sum(s * s for s in step))
    new = [s / size for s in step]
    turned = rotation_rows(new)
    rel = [sum(turned[r][k] * old[c][k] for k in range(3)) for r in range(3) for c in range(3)]
    return new, vel, ang, [STEP_DT * v for v in vel] + rel


def finish_kernel(count, *refs):
    sums, refs = refs[:count], refs[count:]
    finish_body(sums, *refs)


def finish_body(sums, pose, motion, inverse, col_a, col_b, line_a, line_b, end_a, end_b, pos, lever, slot, owner,
                moved, state, table):
    tx, ty = pos.shape[0], pos.shape[2]
    slots = owner.shape[2]
    high_x, high_y = outward("gx"), outward("gy")
    turn = lambda d, high: 1 + jnp.where(high, d, -d)
    bodies = {}
    for (a, b), ref in {(1, 0): col_a, (1, 2): col_b, (0, 1): line_a, (2, 1): line_b, (0, 2): end_a, (2, 2): end_b}.items():
        bodies[a, b] = (ref, ref.shape[0] - BODY)
    for a, ref in ((0, end_a), (2, end_b)):
        bodies[a, 0] = (ref, ref.shape[0] - 2 * BODY)
    if len(sums) == 1:
        totals = lambda b, a: sums[0][a, b]
    else:
        cols, other, got = sums
        totals = lambda b, a: (other[1, b] + cols[0, b] + got[2, b], cols[1, b] + other[0, b] + got[0, b],
                               got[1, b] + cols[2, b])[a]
    for a in range(3):
        for b in range(3):
            f = totals(b, a)
            f = [f[r : r + 1] for r in range(6)]
            if (a, b) == (1, 1):
                q = [pose[0, 3 + r] for r in range(4)]
                mot = [motion[0, r] for r in range(6)]
                inv = [inverse[0, 0, r : r + 1, :] for r in range(4)]
            else:
                ref, at = bodies[a, b]
                third = BODY // 3
                body = sum(ref[at + k * third : at + (k + 1) * third, :].astype(F32) for k in range(3))
                body = [body[r : r + 1] for r in range(14)]
                q, mot, inv = body[0:4], body[4:10], body[10:14]
            new, vel, ang, packed = integrate(q, mot, inv, f)
            if (a, b) == (1, 1):
                centre = [pose[0, r] + STEP_DT * vel[r] for r in range(3)]
                for r, val in enumerate(centre + new + vel + ang):
                    state[0, r] = val
            packed = jnp.concatenate(packed + [jnp.zeros((4, slots), F32)], axis=0)
            table[a, b] = jnp.concatenate(split_two(packed), axis=0)

    def place(i, j, a, b):
        key = owner[i, pl.ds(j, 1), :] * slots + slot[i, pl.ds(j, 1), :]
        rows = table[1, 1] if a == 0 and b == 0 else table[turn(a, high_x), turn(b, high_y)]
        got = jnp.dot(rows, one_hot(key, slots, (3 * a + b + 4) * slots), preferred_element_type=F32)
        got = got[0:16] + got[16:32]
        lev = [lever[i, c, pl.ds(j, 1), :] for c in range(3)]
        return [got[r : r + 1] + sum(got[3 + 3 * r + c : 4 + 3 * r + c] * lev[c] for c in range(3)) for r in range(3)]

    def line(i, carry):
        for j in range(ty):
            for r, val in enumerate(place(i, j, 0, 0)):
                moved[i, r, j : j + 1, :] = pos[i, r, j : j + 1, :].astype(F32) + val - lever[i, r, j : j + 1, :]
        return carry

    lax.fori_loop(0, tx, line, 0, unroll=UNROLL)
    for a, b in DIRS:
        for i in range(tx) if a == 0 else [0 if a < 0 else tx - 1]:
            for j in range(ty) if b == 0 else [0 if b < 0 else ty - 1]:
                for r, val in enumerate(place(i, j, a, b)):
                    moved[i, r, j : j + 1, :] = moved[i, r, j : j + 1, :] + val


def finish(sums, pose, motion, inverse, cols, lines, ends, pos, lever, slot, owner):
    slots = pose.shape[3]
    return pl.pallas_call(
        lambda *refs: finish_kernel(len(sums), *refs),
        out_shape=[jax.ShapeDtypeStruct(lever.shape, F32), jax.ShapeDtypeStruct((1, 13, 1, slots), F32)],
        in_specs=[VMEM] * (13 + len(sums)),
        out_specs=[VMEM] * 2,
        scratch_shapes=[pltpu.VMEM((3, 3, 32, slots), BF16)],
        compiler_params=pltpu.CompilerParams(vmem_limit_bytes=SMALL),
    )(*sums, pose, motion, inverse, *cols, *lines, *ends, pos, lever, slot, owner)


def corner_kernel(col_a, col_b, end_in, end_out):
    rows = (end_in.shape[0] - 2 * BODY) // 2
    last = col_a.shape[0] - BODY - rows
    high = outward("gx")
    for q, (col, last) in enumerate(((col_a, last), (col_b, rows))):
        first, final = col[0:rows, :], col[last : last + rows, :]
        end_in[q * rows : (q + 1) * rows, :] = jnp.where(high, first, final)
        end_out[q * rows : (q + 1) * rows, :] = jnp.where(high, final, first)
    for q, col in enumerate((col_a, col_b)):
        body = col[col.shape[0] - BODY :, :]
        at = 2 * rows + q * BODY
        end_in[at : at + BODY, :] = body
        end_out[at : at + BODY, :] = body


def corners(col_a, col_b, rows):
    out = jax.ShapeDtypeStruct((2 * (rows + BODY), col_a.shape[1]), BF16)
    return pl.pallas_call(
        corner_kernel,
        out_shape=[out] * 2,
        in_specs=[VMEM] * 2,
        out_specs=[VMEM] * 2,
        compiler_params=pltpu.CompilerParams(vmem_limit_bytes=SMALL),
        cost_estimate=pl.CostEstimate(flops=8_000_000_000, bytes_accessed=20_000_000, transcendentals=0),
    )(col_a, col_b)


def swap(value, axis, start):
    n = lax.axis_size(axis)
    route = []
    for c in range(start, n + start, 2):
        route += [(c % n, (c + 1) % n), ((c + 1) % n, c % n)]
    return lax.ppermute(value, axis, route)


def inside(value, axis):
    return swap(value, axis, 0)


def outside(value, axis):
    return swap(value, axis, 1)


def local(positions, features, lever, partner, body_slot, owner_dir, body_pose, body_motion,
          body_inverse, weight_u, weight_v, radial_rate):
    tx, ty = positions.shape[0], positions.shape[1]
    slots = body_pose.shape[3]
    rows = positions.shape[3] + EXTRA
    pos, lever = (jnp.transpose(v, (0, 2, 1, 3)) for v in (positions, lever))
    pose, motion = (jnp.transpose(v, (0, 2, 1, 3)) for v in (body_pose, body_motion))
    codes = jnp.transpose(partner, (2, 0, 1))
    own, col_in, ends_out, col_out, row_in, row_out = project(features, pos, weight_v, pose, motion, body_inverse)
    line_a, line_b = inside(row_in, "gx"), outside(row_out, "gx")
    col_a, ends_b = inside(col_in, "gy"), outside(ends_out, "gy")
    col_b = outside(col_out, "gy")
    end_in, end_out = corners(col_a, ends_b, rows)
    end_a, end_b = inside(end_in, "gx"), outside(end_out, "gx")
    args = (codes, radial_rate, features, weight_u, lever, body_slot, owner_dir, slots)
    inner = [((i,), range(1, ty - 1)) for i in range(1, tx - 1)]
    rim = [((0,), range(ty)), ((tx - 1,), range(ty)), (range(1, tx - 1), (0,)), (range(1, tx - 1), (ty - 1,))]
    (first,) = pairs(inner, False, args, own, None)
    parts = pairs(rim, True, args, own, [col_a, col_b, line_a, line_b, end_a, end_b, first])
    mine = parts[1] + inside(parts[0], "gy")
    got = outside(jnp.stack([parts[2], mine]), "gy")
    mine = mine + got[0]
    cols = jnp.stack([inside(mine, "gy"), mine, got[1] + parts[2]], axis=1)
    if lax.axis_size("gx") == 4:
        other = inside(cols, "gx")
        got = outside(jnp.stack([cols[2], cols[1] + other[0], other[2]]), "gx")
        sums = [cols, other, got]
    else:
        mine = cols[1] + inside(cols[0], "gx")
        got = outside(jnp.stack([cols[2], mine]), "gx")
        mine = mine + got[0]
        sums = [jnp.stack([inside(mine, "gx"), mine, got[1] + cols[2]])]
    moved, state = finish(sums, pose, motion, body_inverse, (col_a, ends_b), (line_a, line_b), (end_a, end_b),
                          pos, lever, body_slot, owner_dir)
    return (jnp.transpose(moved, (0, 2, 1, 3)), jnp.transpose(state, (0, 2, 1, 3)))


def solution(mesh):
    placed = (
        P("gx", "gy", None, None),
        P("gx", "gy", None, None),
        P("gx", "gy", None, None),
        P("gx", "gy", None),
        P("gx", "gy", None),
        P("gx", "gy", None),
        P("gx", "gy", None, None),
        P("gx", "gy", None, None),
        P("gx", "gy", None, None),
        P(),
        P(),
        P(),
    )
    return jax.shard_map(
        local,
        mesh=mesh,
        in_specs=placed,
        out_specs=(P("gx", "gy", None, None), P("gx", "gy", None, None)),
        check_vma=False,
    )
```
